32 devices in a mesh: seq: 4 (over z), tp: 8 (over y, x, core).
Axes of the slice: x: 2, y: 2, z: 4, core: 2. Of those that a mesh axis runs over, the one named last changes fastest.
Arguments:
- inputs: bfloat16 [4096, 4096], P('seq'), may hold values from -6 to 6
- cotangent: bfloat16 [4096, 4096], P('seq'), may hold values from -6 to 6
- w_in: bfloat16 [4096, 5120], P(None, 'tp'), may hold values from -0.125 to 0.125
- conv_w: float32 [3, 5120], P(None, 'tp'), may hold values from -3.5 to 3.5
- norm_gain: float32 [4096], P('tp'), may hold values from 0.25 to 1.75
- w_out: bfloat16 [4096, 4096], P('tp'), may hold values from -0.125 to 0.125
- keep_flags: int32 [32], P('tp'), may hold values 0 or 1
Outputs:
- layer_out: bfloat16 [4096, 4096], P('seq', 'tp')
- input_grad: bfloat16 [4096, 4096], P('seq', 'tp')
The draws below stay inside these ranges and needn't reach their ends.
All inputs are finite; a program needn't handle non-finite values. No bound on the sum of `keep_flags` on one device may be relied on, other than what follows from the above.
Results may differ from the reference program's by a relative error of at most 0.0071.
Values may be sent and summed in bfloat16 or wider, within the bound.
No kernel may reach another device: no remote copies, remote signals or barrier semaphores. Data moves between devices by JAX's collectives and lax.ppermute only.
A program may use at most 192 MiB of HBM per device.

```python
from functools import partial
import jax
import jax.numpy as jnp
import numpy as np
from jax import lax

D = 4096
H = 32
FEAT = 16
DV = 128
EXP = 153
TOK_DEV = 1024
TOKENS = 4096
N_SEQ = 4


def set_ends(drawn, rng, smallest, high):
    index_at = [jax.random.randint(jax.random.fold_in(rng, axis), (), 0, length) for axis, length in enumerate(drawn.shape)]
    main_axis = drawn.shape.index(max(drawn.shape))
    next_to = index_at[:main_axis] + [(index_at[main_axis] + 1) % drawn.shape[main_axis]] + index_at[main_axis + 1:]
    return drawn.at[tuple(index_at)].set(smallest).at[tuple(next_to)].set(high)


def with_spikes(drawn, own_key, source, target, parts, factor):
    owner, partner = [(jnp.arange(drawn.shape[axis_at]) // (drawn.shape[axis_at] // parts)).reshape([-1 if axis == axis_at else 1 for axis in range(drawn.ndim)]) for axis_at in (source, target)]
    chosen = jax.random.permutation(own_key, parts)[partner]
    strong = (owner == chosen) | (owner == (partner + parts // 2) % parts)
    return jnp.where(strong, factor * drawn, drawn)


def block_levels(rng, dims, split, least, top_value):
    def one(axis_at, parts):
        draws = jax.random.uniform(jax.random.fold_in(jax.random.fold_in(rng, 6), axis_at), (parts,), jnp.float32, least / len(split), top_value / len(split))
        return jnp.repeat(jnp.exp(draws), dims[axis_at] // parts).reshape((-1,) + (1,) * (len(dims) - axis_at - 1))

    factor_of = one(*split[0])
    for cut in split[1:]:
        factor_of = factor_of * one(*cut)
    return factor_of


def normal_values(key, dims, width, bound, shards=(), kind=jnp.bfloat16):
    values = jax.random.normal(key, dims, jnp.float32) * width
    if len(shards) > 0:
        values = block_levels(key, dims, shards, -0.22, 0.18) * values
    return jnp.clip(values, min=-bound, max=bound).astype(kind)


def heavy_noise(own_key, shape, spread, bound, shards, heavy, kind=jnp.bfloat16):
    array = spread * jax.random.normal(own_key, shape, jnp.float32)
    if shards:
        array = array * block_levels(own_key, shape, shards, -0.22, 0.18)
    return jnp.clip(with_spikes(array, jax.random.fold_in(own_key, 3), *heavy), -bound, bound).astype(kind)


def setup_inputs(seed: int = 0) -> dict:
    key_of = jax.random.split(jax.random.key(seed), 8)
    return {
        "inputs": normal_values(key_of[0], (TOKENS, D), 1.0, 6.0, ((0, 4),)),
        "cotangent": normal_values(key_of[1], (TOKENS, D), 1.0, 6.0, ((0, 4),)),
        "w_in": heavy_noise(key_of[2], (D, H * (2 * FEAT + DV)), D ** -0.5, 0.125, ((1, 8),), (1, 0, 8, 2.0)),
        "conv_w": normal_values(key_of[3], (3, H * (2 * FEAT + DV)), 3 ** -0.5, 3.5, ((1, 8),), jnp.float32),
        "norm_gain": jnp.clip(1.0 + 0.15 * jax.random.normal(key_of[4], (H * DV,), jnp.float32), 0.25, 1.75),
        "w_out": heavy_noise(key_of[5], (H * DV, D), (H * DV) ** -0.5, 0.125, ((0, 8),), (0, 1, 8, 2.0)),
        "keep_flags": set_ends((jax.random.randint(key_of[6], (H,), 0, 4) < 3).astype(jnp.int32), jax.random.fold_in(key_of[6], 1), 0, 1),
    }


epsilon = 1e-06
highest = lax.Precision.HIGHEST

def pair_table(feature_dim):
    selector = np.zeros((feature_dim * feature_dim, feature_dim * (feature_dim + 1) // 2), np.float32)
    column = 0
    for row_index in range(feature_dim):
        for col_index in range(row_index, feature_dim):
            selector[row_index * feature_dim + col_index, column] = 0.7071067811865476 if row_index == col_index else 1.0
            column = column + 1
    return selector

def taylor_features(scaled, selector):
    outer_prod = scaled[..., :, None] * scaled[..., None, :]
    flattened = outer_prod.reshape(scaled.shape[:-1] + (scaled.shape[-1] * scaled.shape[-1],))
    pair_terms = jnp.einsum('thp,pm->thm', flattened, selector, precision=highest)
    constant = jnp.ones(scaled.shape[:-1] + (1,), scaled.dtype)
    return jnp.concatenate([constant, scaled, pair_terms], -1)

def causal_mask(row_total):
    return jnp.arange(row_total)[:, None] >= jnp.arange(row_total)[None, :]

def conv_forward(extended, conv_w):
    widened = extended.astype(jnp.float32)
    mixed = conv_w[0] * widened[2:] + conv_w[1] * widened[1:-1] + conv_w[2] * widened[:-2]
    return mixed.astype(jnp.bfloat16)

def conv_backward(extended_grad, conv_w):
    mixed = conv_w[0] * extended_grad[:-2] + conv_w[1] * extended_grad[1:-1] + conv_w[2] * extended_grad[2:]
    return mixed.astype(jnp.bfloat16)

def split_heads(convolved, head_count):
    widened = convolved.astype(jnp.float32).reshape(convolved.shape[0], head_count, 2 * FEAT + DV)
    return (widened[:, :, :FEAT], widened[:, :, FEAT:2 * FEAT], widened[:, :, 2 * FEAT:])

def block_forward(queries, key_part, values, selector):
    quarter_root = FEAT ** (-0.25)
    logits = jnp.einsum('thf,shf->hts', queries, key_part, precision=highest) * (quarter_root * quarter_root)
    causal = causal_mask(queries.shape[0])
    weights = jnp.where(causal[None], 1.0 + logits + 0.5 * logits * logits, 0.0)
    query_features = taylor_features(queries * quarter_root, selector)
    key_features = taylor_features(key_part * quarter_root, selector)
    local_state = jnp.einsum('the,thv->hev', key_features, values, precision=highest)
    local_mix = jnp.einsum('hts,shv->thv', weights, values, precision=highest)
    return (logits, weights, query_features, key_features, local_state, local_mix)

def head_norm(numerator, head_gains, keep_scale):
    radius = jnp.sqrt(lax.optimization_barrier(jnp.mean(numerator * numerator, -1, keepdims=True)) + epsilon)
    normed = numerator / radius
    output = (normed * head_gains[None] * keep_scale[None, :, None]).astype(jnp.bfloat16)
    return (radius, normed, output)

def norm_backward(grad_heads, normed, radius, head_gains, keep_scale):
    scaled_grad = grad_heads * head_gains[None] * keep_scale[None, :, None]
    return (scaled_grad - normed * lax.optimization_barrier(jnp.mean(scaled_grad * normed, -1, keepdims=True))) / radius

def block_backward(queries, key_part, values, logits, weights, query_features, key_features, prefix_state, suffix_state, d_numer, selector):
    quarter_root = FEAT ** (-0.25)
    d_values = jnp.einsum('hts,thv->shv', weights, d_numer, precision=highest)
    d_values = d_values + jnp.einsum('she,hev->shv', key_features, suffix_state, precision=highest)
    d_weights = jnp.einsum('thv,shv->hts', d_numer, values, precision=highest)
    causal = causal_mask(queries.shape[0])
    d_logits = jnp.where(causal[None], d_weights * (1.0 + logits), 0.0) * (quarter_root * quarter_root)
    d_queries = jnp.einsum('hts,shf->thf', d_logits, key_part, precision=highest)
    d_keys = jnp.einsum('hts,thf->shf', d_logits, queries, precision=highest)
    d_query_features = jnp.einsum('thv,hev->the', d_numer, prefix_state, precision=highest)
    d_key_features = jnp.einsum('shv,hev->she', values, suffix_state, precision=highest)
    pull_query = jax.vjp(partial(taylor_features, selector=selector), queries * quarter_root)[1]
    pull_key = jax.vjp(partial(taylor_features, selector=selector), key_part * quarter_root)[1]
    d_queries = d_queries + pull_query(d_query_features)[0] * quarter_root
    d_keys = d_keys + pull_key(d_key_features)[0] * quarter_root
    merged = jnp.concatenate([d_queries, d_keys, d_values], -1)
    return merged.reshape(merged.shape[0], -1)

def reference(inputs, cotangent, w_in, conv_w, norm_gain, w_out, keep_flags):
    selector = jnp.asarray(pair_table(FEAT)).astype(jnp.float32)
    width_all = H * (2 * FEAT + DV)
    projected = jnp.dot(inputs, w_in, preferred_element_type=jnp.float32).astype(jnp.bfloat16)
    extended = jnp.concatenate([jnp.zeros((2, width_all), jnp.bfloat16), projected], 0)
    convolved = conv_forward(extended, conv_w)
    blocked = convolved.reshape(N_SEQ, TOK_DEV, width_all)
    head_gains = norm_gain.reshape(H, DV)
    keep_scale = keep_flags.astype(jnp.float32)

    def forward_step(carried_state, block_rows):
        queries, key_part, values = split_heads(block_rows, H)
        logits, weights, query_features, key_features, local_state, local_mix = block_forward(queries, key_part, values, selector)
        numerator = local_mix + jnp.einsum('the,hev->thv', query_features, carried_state, precision=highest)
        radius, normed, output = head_norm(numerator, head_gains, keep_scale)
        return (carried_state + local_state, (carried_state, radius, normed, output))
    initial = jnp.zeros((H, EXP, DV), jnp.float32)
    final_state, saved_values = lax.scan(forward_step, initial, blocked)
    prefixes, all_radius, normals, outputs = saved_values
    flat_output = outputs.reshape(TOKENS, H * DV)
    layer_out = (inputs.astype(jnp.float32) + jnp.dot(flat_output, w_out, preferred_element_type=jnp.float32)).astype(jnp.bfloat16)
    grad_heads = jnp.dot(cotangent, w_out.T, preferred_element_type=jnp.float32).reshape(N_SEQ, TOK_DEV, H, DV)
    d_numers = norm_backward(grad_heads, normals, all_radius, head_gains, keep_scale)

    def backward_step(suffix_state, packed):
        block_rows, prefix_state, d_numer = packed
        queries, key_part, values = split_heads(block_rows, H)
        logits, weights, query_features, key_features, local_state, local_mix = block_forward(queries, key_part, values, selector)
        d_block = block_backward(queries, key_part, values, logits, weights, query_features, key_features, prefix_state, suffix_state, d_numer, selector)
        grad_term = jnp.einsum('the,thv->hev', query_features, d_numer, precision=highest)
        return (suffix_state + grad_term, d_block)
    suffix_final, d_blocks = lax.scan(backward_step, initial, (blocked, prefixes, d_numers), reverse=True)
    d_convolved = d_blocks.reshape(TOKENS, width_all)
    extended_grad = jnp.concatenate([d_convolved, jnp.zeros((2, width_all), jnp.float32)], 0)
    d_projected = conv_backward(extended_grad, conv_w)
    input_grad = (cotangent.astype(jnp.float32) + jnp.dot(d_projected, w_in.T, preferred_element_type=jnp.float32)).astype(jnp.bfloat16)
    return (layer_out, input_grad)
```

```python
import functools

import jax
import jax.numpy as jnp
import numpy as np
from jax import lax
from jax.experimental import pallas as pl
from jax.experimental.pallas import tpu as pltpu
from jax.sharding import PartitionSpec as P

FEAT = 16
DV = 128
HW = 2 * FEAT + DV
EP = 256
ES = 160
CH = 256
EPS = 1e-06
BF = jnp.bfloat16
F32 = jnp.float32
VMEM = 40 * 1024 * 1024


def mm(a, b):
    return lax.dot_general(a, b, (((1,), (0,)), ((), ())), preferred_element_type=F32)


def mm_nt(a, b):
    return lax.dot_general(a, b, (((1,), (1,)), ((), ())), preferred_element_type=F32)


def mm_tn(a, b):
    return lax.dot_general(a, b, (((0,), (0,)), ((), ())), preferred_element_type=F32)


def selectors(heads):
    sel = np.zeros((heads, 128, 4 * EP + 256), np.float32)
    bias = np.zeros((8, EP), np.float32)
    bias[1, :FEAT] = 1.0
    bias[0, FEAT] = bias[1, FEAT] = 1.0
    for h in range(heads):
        q0 = (HW * h) % 128
        k0 = q0 + FEAT
        for i in range(FEAT):
            sel[h, q0 + i, i] = 0.5
            sel[h, k0 + i, 2 * EP + i] = 0.5
            sel[h, k0 + i, 4 * EP + q0 + i] = 0.25
            sel[h, q0 + i, 4 * EP + 128 + k0 + i] = 0.25
        col = FEAT + 1
        for i in range(FEAT):
            for j in range(i, FEAT):
                sel[h, q0 + i, col] = 0.25 if i == j else 0.5
                sel[h, q0 + j, EP + col] = 0.5
                sel[h, k0 + i, 2 * EP + col] = 0.5
                sel[h, k0 + j, 3 * EP + col] = 0.5
                col += 1
    return jnp.asarray(sel, BF), jnp.asarray(bias, F32)


def window(h):
    t = (HW * h) // 128
    return slice(128 * t, 128 * t + 128)


def value_place(h):
    start = HW * h + 2 * FEAT
    return start // 128, start % 128


def lane_iota():
    return lax.broadcasted_iota(jnp.int32, (CH, 128), 1)


def take_values(conv, h):
    tile, off = value_place(h)
    first = conv[:, 128 * tile : 128 * tile + 128]
    if off == 0:
        return first
    second = conv[:, 128 * tile + 128 : min(128 * tile + 256, conv.shape[1])]
    if second.shape[1] < 128:
        second = jnp.concatenate([second, jnp.zeros((CH, 128 - second.shape[1]), second.dtype)], 1)
    a = pltpu.roll(first, 128 - off, 1)
    b = pltpu.roll(second, 128 - off, 1)
    return jnp.where(lane_iota() < 128 - off, a, b)


def causal():
    r = lax.broadcasted_iota(jnp.int32, (CH, CH), 0)
    c = lax.broadcasted_iota(jnp.int32, (CH, CH), 1)
    return r >= c


def params():
    return pltpu.CompilerParams(dimension_semantics=("arbitrary",), vmem_limit_bytes=VMEM)


def whole(shape):
    return pl.BlockSpec(shape, lambda c: (0,) * len(shape))


def project_kernel(heads, x_ref, halo_ref, w_ref, cw_ref, sel_ref, bias_ref,
                   cv_ref, v_ref, pq_ref, pk_ref, loc_ref, state_ref, ext, run):
    c = pl.program_id(0)

    @pl.when(c == 0)
    def _():
        before = mm(halo_ref[...], w_ref[...]).astype(BF).astype(F32)
        ext[0:8, :] = before[8:16]
        run[...] = jnp.zeros_like(run)

    ext[8:, :] = mm(x_ref[...], w_ref[...]).astype(BF).astype(F32)
    conv = (cw_ref[0:1] * ext[8 : 8 + CH, :] + cw_ref[1:2] * ext[7 : 7 + CH, :]
            + cw_ref[2:3] * ext[6 : 6 + CH, :])
    ext[0:8, :] = ext[CH : CH + 8, :]
    conv_b = conv.astype(BF)
    cv_ref[...] = conv_b
    conv = conv_b.astype(F32)
    b0 = bias_ref[0:1]
    b1 = bias_ref[1:2]
    for h in range(heads):
        u = mm(conv_b[:, window(h)], sel_ref[h, :, : 4 * EP])
        pq_ref[h] = ((u[:, :EP] + b0) * (u[:, EP : 2 * EP] + b1)).astype(BF)
        pk = ((u[:, 2 * EP : 3 * EP] + b0) * (u[:, 3 * EP :] + b1)).astype(BF)
        pk_ref[h] = pk
        v = take_values(conv, h).astype(BF)
        v_ref[:, DV * h : DV * h + DV] = v
        loc_ref[0, h] = run[h].astype(BF)
        run[h] = run[h] + mm_tn(v, pk)

    @pl.when(c == pl.num_programs(0) - 1)
    def _():
        for h in range(heads):
            state_ref[h] = run[h].T[:ES].astype(BF)


def project(x, halo, w_in, conv_w, sel, bias, heads):
    rows, d = x.shape
    width = w_in.shape[1]
    n = rows // CH
    return pl.pallas_call(
        functools.partial(project_kernel, heads),
        grid=(n,),
        in_specs=[
            pl.BlockSpec((CH, d), lambda c: (c, 0)),
            whole((16, d)),
            whole((d, width)),
            whole((3, width)),
            whole(sel.shape),
            whole(bias.shape),
        ],
        out_specs=[
            pl.BlockSpec((CH, width), lambda c: (c, 0)),
            pl.BlockSpec((CH, heads * DV), lambda c: (c, 0)),
            pl.BlockSpec((heads, CH, EP), lambda c: (0, c, 0)),
            pl.BlockSpec((heads, CH, EP), lambda c: (0, c, 0)),
            pl.BlockSpec((1, heads, DV, EP), lambda c: (c, 0, 0, 0)),
            whole((heads, ES, DV)),
        ],
        out_shape=[
            jax.ShapeDtypeStruct((rows, width), BF),
            jax.ShapeDtypeStruct((rows, heads * DV), BF),
            jax.ShapeDtypeStruct((heads, rows, EP), BF),
            jax.ShapeDtypeStruct((heads, rows, EP), BF),
            jax.ShapeDtypeStruct((n, heads, DV, EP), BF),
            jax.ShapeDtypeStruct((heads, ES, DV), BF),
        ],
        scratch_shapes=[pltpu.VMEM((CH + 8, width), F32), pltpu.VMEM((heads, DV, EP), F32)],
        compiler_params=params(),
        cost_estimate=pl.CostEstimate(flops=2 * rows * d * width, bytes_accessed=20 << 20, transcendentals=0),
        name="project",
    )(x, halo, w_in, conv_w, sel, bias)


def local_kernel(heads, ct_ref, wo_ref, gain_ref, v_ref, pq_ref, pk_ref, loc_ref, g_ref, num_ref):
    g_ref[...] = mm_nt(ct_ref[...], wo_ref[...]) * gain_ref[...]
    mask = causal()
    for h in range(heads):
        pq = pq_ref[h]
        logits = mm_nt(pq[:, :FEAT], pk_ref[h, :, :FEAT])
        weights = jnp.where(mask, 1.0 + logits + 0.5 * logits * logits, 0.0).astype(BF)
        at = slice(DV * h, DV * h + DV)
        num_ref[:, at] = mm(weights, v_ref[:, at]) + mm_nt(pq, loc_ref[0, h])


def local_part(ct, w_out, gain, v, pq, pk, loc, heads):
    rows, d = ct.shape
    n = rows // CH
    wide = heads * DV
    row = pl.BlockSpec((CH, wide), lambda c: (c, 0))
    feat = pl.BlockSpec((heads, CH, EP), lambda c: (0, c, 0))
    return pl.pallas_call(
        functools.partial(local_kernel, heads),
        grid=(n,),
        in_specs=[
            pl.BlockSpec((CH, d), lambda c: (c, 0)),
            whole((wide, d)),
            whole((1, wide)),
            row,
            feat,
            feat,
            pl.BlockSpec((1, heads, DV, EP), lambda c: (c, 0, 0, 0)),
        ],
        out_specs=[row, row],
        out_shape=[jax.ShapeDtypeStruct((rows, wide), F32)] * 2,
        compiler_params=params(),
        cost_estimate=pl.CostEstimate(flops=2 * rows * d * wide, bytes_accessed=20 << 20, transcendentals=0),
        name="local_part",
    )(ct, w_out, gain, v, pq, pk, loc)


def norm_kernel(heads, g_ref, num_ref, gain_ref, pq_ref, pre_ref, ho_ref, dn_ref, loc_ref, state_ref, run):
    c = pl.program_id(0)

    @pl.when(c == 0)
    def _():
        run[...] = jnp.zeros_like(run)

    for h in range(heads):
        at = slice(DV * h, DV * h + DV)
        pq = pq_ref[h]
        num = num_ref[:, at] + mm(pq[:, :ES], pre_ref[h])
        inv = lax.rsqrt(jnp.mean(num * num, 1, keepdims=True) + EPS)
        normed = num * inv
        ho_ref[:, at] = (normed * gain_ref[:, at]).astype(BF)
        g = g_ref[:, at]
        dn = ((g - normed * jnp.mean(g * normed, 1, keepdims=True)) * inv).astype(BF)
        dn_ref[:, at] = dn
        loc_ref[0, h] = run[h].astype(BF)
        run[h] = run[h] + mm_tn(dn, pq)

    @pl.when(c == pl.num_programs(0) - 1)
    def _():
        for h in range(heads):
            state_ref[h] = run[h].T[:ES].astype(BF)


def norm_part(g, num, gain, pq, pre, heads):
    rows, wide = g.shape
    n = rows // CH
    row = pl.BlockSpec((CH, wide), lambda c: (n - 1 - c, 0))
    return pl.pallas_call(
        functools.partial(norm_kernel, heads),
        grid=(n,),
        in_specs=[
            row,
            row,
            whole((1, wide)),
            pl.BlockSpec((heads, CH, EP), lambda c: (0, n - 1 - c, 0)),
            whole((heads, ES, DV)),
        ],
        out_specs=[
            row,
            row,
            pl.BlockSpec((1, heads, DV, EP), lambda c: (n - 1 - c, 0, 0, 0)),
            whole((heads, ES, DV)),
        ],
        out_shape=[
            jax.ShapeDtypeStruct((rows, wide), BF),
            jax.ShapeDtypeStruct((rows, wide), BF),
            jax.ShapeDtypeStruct((n, heads, DV, EP), BF),
            jax.ShapeDtypeStruct((heads, ES, DV), BF),
        ],
        scratch_shapes=[pltpu.VMEM((heads, DV, EP), F32)],
        compiler_params=params(),
        cost_estimate=pl.CostEstimate(flops=1 << 30, bytes_accessed=8 << 20, transcendentals=0),
        name="norm_part",
    )(g, num, gain, pq, pre)


def inner_kernel(heads, cv_ref, v_ref, pq_ref, pk_ref, dn_ref, loc_ref, pre_ref, sel_ref, bias_ref,
                 dqk_ref, dv_ref, pre_t):
    @pl.when(pl.program_id(0) == 0)
    def _():
        pre_t[...] = jnp.zeros_like(pre_t)
        for h in range(heads):
            pre_t[h, :, :ES] = pre_ref[h].astype(F32).T

    mask = causal()
    b0 = bias_ref[0:1]
    b1 = bias_ref[1:2]
    for h in range(heads):
        at = slice(DV * h, DV * h + DV)
        dn = dn_ref[:, at]
        logits = mm_nt(pq_ref[h, :, :FEAT], pk_ref[h, :, :FEAT])
        weights = jnp.where(mask, 1.0 + logits + 0.5 * logits * logits, 0.0).astype(BF)
        dv_ref[:, at] = mm_tn(weights, dn)
        dl = jnp.where(mask, mm_nt(dn, v_ref[:, at]) * (1.0 + logits), 0.0).astype(BF)
        state = (loc_ref[0, h].astype(F32) + pre_t[h]).astype(BF)
        dphi = mm(dn, state)
        cw = cv_ref[:, window(h)]
        u = mm(cw, sel_ref[h, :, : 2 * EP])
        da = (dphi * (u[:, EP:] + b1)).astype(BF)
        db = (dphi * (u[:, :EP] + b0)).astype(BF)
        moved = mm(cw, sel_ref[h, :, 4 * EP :]).astype(BF)
        dqk_ref[h] = (
            mm_nt(da, sel_ref[h, :, :EP])
            + mm_nt(db, sel_ref[h, :, EP : 2 * EP])
            + mm(dl, moved[:, :128])
            + mm_tn(dl, moved[:, 128:])
        )


def inner_part(cv, v, pq, pk, dn, loc, pre, sel, bias, heads):
    rows, width = cv.shape
    n = rows // CH
    wide = heads * DV
    row = pl.BlockSpec((CH, wide), lambda c: (c, 0))
    feat = pl.BlockSpec((heads, CH, EP), lambda c: (0, c, 0))
    return pl.pallas_call(
        functools.partial(inner_kernel, heads),
        grid=(n,),
        in_specs=[
            pl.BlockSpec((CH, width), lambda c: (c, 0)),
            row,
            feat,
            feat,
            row,
            pl.BlockSpec((1, heads, DV, EP), lambda c: (c, 0, 0, 0)),
            whole((heads, ES, DV)),
            whole(sel.shape),
            whole(bias.shape),
        ],
        out_specs=[pl.BlockSpec((heads, CH, 128), lambda c: (0, c, 0)), row],
        out_shape=[
            jax.ShapeDtypeStruct((heads, rows, 128), F32),
            jax.ShapeDtypeStruct((rows, wide), F32),
        ],
        scratch_shapes=[pltpu.VMEM((heads, DV, EP), F32)],
        compiler_params=params(),
        cost_estimate=pl.CostEstimate(flops=12 << 30, bytes_accessed=14 << 20, transcendentals=0),
        name="inner_part",
    )(cv, v, pq, pk, dn, loc, pre, sel, bias)


def outer_kernel(heads, cv_ref, v_ref, pk_ref, dqk_ref, dv_ref, loc_ref, suf_ref, sel_ref, bias_ref, cw_ref,
                 dp_ref, first_ref, last_ref, ext, suf_t):
    c = pl.program_id(0)
    width = cv_ref.shape[1]

    @pl.when(c == 0)
    def _():
        suf_t[...] = jnp.zeros_like(suf_t)
        for h in range(heads):
            suf_t[h, :, :ES] = suf_ref[h].astype(F32).T
        ext[CH:, :] = jnp.zeros((8, width), F32)

    b0 = bias_ref[0:1]
    b1 = bias_ref[1:2]
    lane = lane_iota()
    tiles = [None] * (-(-width // 128))

    def put(t, piece):
        tiles[t] = piece if tiles[t] is None else tiles[t] + piece

    for h in range(heads):
        at = slice(DV * h, DV * h + DV)
        state = (loc_ref[0, h].astype(F32) + suf_t[h]).astype(BF)
        dphi = mm(v_ref[:, at], state)
        u = mm(cv_ref[:, window(h)], sel_ref[h, :, 2 * EP : 4 * EP])
        da = (dphi * (u[:, EP:] + b1)).astype(BF)
        db = (dphi * (u[:, :EP] + b0)).astype(BF)
        dqk = (
            dqk_ref[h]
            + mm_nt(da, sel_ref[h, :, 2 * EP : 3 * EP])
            + mm_nt(db, sel_ref[h, :, 3 * EP : 4 * EP])
        )
        put((HW * h) // 128, dqk)
        dv = dv_ref[:, at] + mm_nt(pk_ref[h], state)
        tile, off = value_place(h)
        if off == 0:
            put(tile, dv)
        else:
            moved = pltpu.roll(dv, off, 1)
            put(tile, jnp.where(lane >= off, moved, 0.0))
            put(tile + 1, jnp.where(lane < off, moved, 0.0))
    for t, tile in enumerate(tiles):
        end = min(128 * t + 128, width)
        ext[:CH, 128 * t : end] = tile[:, : end - 128 * t]
    dp = (cw_ref[0:1] * ext[:CH, :] + cw_ref[1:2] * ext[1 : CH + 1, :]
          + cw_ref[2:3] * ext[2 : CH + 2, :])
    dp_ref[...] = dp.astype(BF)

    @pl.when(c == 0)
    def _():
        last_ref[...] = dp[CH - 16 :]

    ext[CH:, :] = ext[0:8, :]
    first_ref[...] = ext[0:8, :]


def outer_part(cv, v, pk, dqk, dv, loc, suf, sel, bias, conv_w, heads):
    rows, width = cv.shape
    n = rows // CH
    wide = heads * DV
    row = pl.BlockSpec((CH, wide), lambda c: (n - 1 - c, 0))
    full_row = pl.BlockSpec((CH, width), lambda c: (n - 1 - c, 0))
    return pl.pallas_call(
        functools.partial(outer_kernel, heads),
        grid=(n,),
        in_specs=[
            full_row,
            row,
            pl.BlockSpec((heads, CH, EP), lambda c: (0, n - 1 - c, 0)),
            pl.BlockSpec((heads, CH, 128), lambda c: (0, n - 1 - c, 0)),
            row,
            pl.BlockSpec((1, heads, DV, EP), lambda c: (n - 1 - c, 0, 0, 0)),
            whole((heads, ES, DV)),
            whole(sel.shape),
            whole(bias.shape),
            whole((3, width)),
        ],
        out_specs=[full_row, whole((8, width)), whole((16, width))],
        out_shape=[
            jax.ShapeDtypeStruct((rows, width), BF),
            jax.ShapeDtypeStruct((8, width), F32),
            jax.ShapeDtypeStruct((16, width), F32),
        ],
        scratch_shapes=[pltpu.VMEM((CH + 8, width), F32), pltpu.VMEM((heads, DV, EP), F32)],
        compiler_params=params(),
        cost_estimate=pl.CostEstimate(flops=6 << 30, bytes_accessed=12 << 20, transcendentals=0),
        name="outer_part",
    )(cv, v, pk, dqk, dv, loc, suf, sel, bias, conv_w)


def shifted(array, by):
    count = lax.axis_size("seq")
    pairs = [(i, i + by) for i in range(count) if 0 <= i + by < count]
    return lax.ppermute(array, "seq", pairs)


def summed_before(part, sign):
    count = lax.axis_size("seq")
    total = None
    for step in range(1, count):
        got = shifted(part, sign * step).astype(F32)
        total = got if total is None else total + got
    return total.astype(BF)


def per_device(inputs, cotangent, w_in, conv_w, norm_gain, w_out, keep_flags):
    heads = keep_flags.shape[0]
    rows = inputs.shape[0]
    sel, bias = selectors(heads)
    slice_width = inputs.shape[1] // lax.axis_size("tp")
    column = lax.axis_index("tp") * slice_width
    gain = (norm_gain.reshape(heads, DV) * keep_flags.astype(F32)[:, None]).reshape(1, heads * DV)
    halo = shifted(inputs[-16:], 1)
    cv, v, pq, pk, loc, state = project(inputs, halo, w_in, conv_w, sel, bias, heads)
    pre = summed_before(state, 1)
    g, num = local_part(cotangent, w_out, gain, v, pq, pk, loc, heads)
    ho, dn, gloc, gstate = norm_part(g, num, gain, pq, pre, heads)
    suf = summed_before(gstate, -1)
    out_term = jnp.dot(ho, w_out, preferred_element_type=F32).astype(BF)
    dqk, dv = inner_part(cv, v, pq, pk, dn, loc, pre, sel, bias, heads)
    dp, first, last = outer_part(cv, v, pk, dqk, dv, gloc, suf, sel, bias, conv_w, heads)
    after = shifted(first, -1)
    tail = last[14:] + jnp.stack(
        [conv_w[2] * after[0], conv_w[1] * after[0] + conv_w[2] * after[1]]
    )
    dp = lax.dynamic_update_slice(dp, tail.astype(BF), (rows - 2, 0))
    grad = lax.dot_general(dp, w_in, (((1,), (1,)), ((), ())), preferred_element_type=F32).astype(BF)
    out_sum = lax.psum_scatter(out_term, "tp", scatter_dimension=1, tiled=True)
    grad_sum = lax.psum_scatter(grad, "tp", scatter_dimension=1, tiled=True)
    x_own = lax.dynamic_slice_in_dim(inputs, column, slice_width, 1).astype(F32)
    c_own = lax.dynamic_slice_in_dim(cotangent, column, slice_width, 1).astype(F32)
    return (x_own + out_sum).astype(BF), (c_own + grad_sum).astype(BF)


def solution(mesh):
    placed = (
        P("seq", None),
        P("seq", None),
        P(None, "tp"),
        P(None, "tp"),
        P("tp"),
        P("tp", None),
        P("tp"),
    )
    return jax.shard_map(
        per_device,
        mesh=mesh,
        in_specs=placed,
        out_specs=(P("seq", "tp"), P("seq", "tp")),
        check_vma=False,
    )
```

```python
import functools

import jax
import jax.numpy as jnp
import numpy as np
from jax import lax
from jax.experimental import pallas as pl
from jax.experimental.pallas import tpu as pltpu
from jax.sharding import PartitionSpec as P

FEAT = 16
DV = 128
HW = 2 * FEAT + DV
EP = 256
ES = 160
CH = 256
EPS = 1e-06
BF = jnp.bfloat16
F32 = jnp.float32
VMEM = 16 * 1024 * 1024


def mm(a, b):
    return lax.dot_general(a, b, (((1,), (0,)), ((), ())), preferred_element_type=F32)


def mm_nt(a, b):
    return lax.dot_general(a, b, (((1,), (1,)), ((), ())), preferred_element_type=F32)


def mm_tn(a, b):
    return lax.dot_general(a, b, (((0,), (0,)), ((), ())), preferred_element_type=F32)


def selectors(heads):
    sel = np.zeros((heads, 128, 4 * EP + 256), np.float32)
    bias = np.zeros((8, EP), np.float32)
    bias[1, :FEAT] = 1.0
    bias[0, FEAT] = bias[1, FEAT] = 1.0
    for h in range(heads):
        q0 = (HW * h) % 128
        k0 = q0 + FEAT
        for i in range(FEAT):
            sel[h, q0 + i, i] = 0.5
            sel[h, k0 + i, 2 * EP + i] = 0.5
            sel[h, k0 + i, 4 * EP + q0 + i] = 0.25
            sel[h, q0 + i, 4 * EP + 128 + k0 + i] = 0.25
        col = FEAT + 1
        for i in range(FEAT):
            for j in range(i, FEAT):
                sel[h, q0 + i, col] = 0.25 if i == j else 0.5
                sel[h, q0 + j, EP + col] = 0.5
                sel[h, k0 + i, 2 * EP + col] = 0.5
                sel[h, k0 + j, 3 * EP + col] = 0.5
                col += 1
    return jnp.asarray(sel, BF), jnp.asarray(bias, F32)


def window(h):
    t = (HW * h) // 128
    return slice(128 * t, 128 * t + 128)


def value_place(h):
    start = HW * h + 2 * FEAT
    return start // 128, start % 128


def lane_iota():
    return lax.broadcasted_iota(jnp.int32, (CH, 128), 1)


def take_values(conv, h):
    tile, off = value_place(h)
    first = conv[:, 128 * tile : 128 * tile + 128]
    if off == 0:
        return first
    second = conv[:, 128 * tile + 128 : min(128 * tile + 256, conv.shape[1])]
    if second.shape[1] < 128:
        second = jnp.concatenate([second, jnp.zeros((CH, 128 - second.shape[1]), second.dtype)], 1)
    a = pltpu.roll(first, 128 - off, 1)
    b = pltpu.roll(second, 128 - off, 1)
    return jnp.where(lane_iota() < 128 - off, a, b)


def causal():
    r = lax.broadcasted_iota(jnp.int32, (CH, CH), 0)
    c = lax.broadcasted_iota(jnp.int32, (CH, CH), 1)
    return r >= c


def params():
    return pltpu.CompilerParams(dimension_semantics=("arbitrary",), vmem_limit_bytes=VMEM)


def whole(shape):
    return pl.BlockSpec(shape, lambda c, *_: (0,) * len(shape))


KEPT = pl.BlockSpec(memory_space=pltpu.VMEM)


def kept(shape, dtype):
    return pltpu.VMEM(shape, dtype)


def keep(array):
    return pltpu.with_memory_space_constraint(array, pltpu.VMEM)


def stay(array):
    return pltpu.with_memory_space_constraint(array, pltpu.HBM)


def cost(flops):
    return pl.CostEstimate(flops=int(flops), bytes_accessed=1 << 20, transcendentals=0)


LIGHT = cost(1000)


def rows_at(c):
    return pl.ds(pl.multiple_of(c * CH, CH), CH)


def project_kernel(heads, x_ref, halo_ref, w_ref, cw_ref, sel_ref, bias_ref,
                   cv_ref, v_ref, pq_ref, pk_ref, loc_ref, state_ref, ext, run):
    c = pl.program_id(0)
    at = rows_at(c)

    @pl.when(c == 0)
    def _():
        before = mm(halo_ref[...], w_ref[...]).astype(BF).astype(F32)
        ext[0:8, :] = before[8:16]
        run[...] = jnp.zeros_like(run)

    ext[8:, :] = mm(x_ref[...], w_ref[...]).astype(BF).astype(F32)
    conv = (cw_ref[0:1] * ext[8 : 8 + CH, :] + cw_ref[1:2] * ext[7 : 7 + CH, :]
            + cw_ref[2:3] * ext[6 : 6 + CH, :])
    ext[0:8, :] = ext[CH : CH + 8, :]
    conv_b = conv.astype(BF)
    cv_ref[at, :] = conv_b
    conv = conv_b.astype(F32)
    b0 = bias_ref[0:1]
    b1 = bias_ref[1:2]
    for h in range(heads):
        u = mm(conv_b[:, window(h)], sel_ref[h, :, : 4 * EP])
        pq_ref[h, at, :] = ((u[:, :EP] + b0) * (u[:, EP : 2 * EP] + b1)).astype(BF)
        pk = ((u[:, 2 * EP : 3 * EP] + b0) * (u[:, 3 * EP :] + b1)).astype(BF)
        pk_ref[h, at, :] = pk
        v = take_values(conv, h).astype(BF)
        v_ref[at, DV * h : DV * h + DV] = v
        loc_ref[c, h] = run[h].astype(BF)
        run[h] = run[h] + mm_tn(v, pk)

    @pl.when(c == pl.num_programs(0) - 1)
    def _():
        for h in range(heads):
            state_ref[h] = run[h].T[:ES].astype(BF)


def project(x, halo, w_in, conv_w, sel, bias, heads):
    rows, d = x.shape
    width = w_in.shape[1]
    n = rows // CH
    return pl.pallas_call(
        functools.partial(project_kernel, heads),
        grid=(n,),
        in_specs=[
            pl.BlockSpec((CH, d), lambda c: (c, 0)),
            whole((16, d)),
            KEPT,
            whole((3, width)),
            KEPT,
            whole(bias.shape),
        ],
        out_specs=[KEPT] * 5 + [whole((heads, ES, DV))],
        out_shape=[
            kept((rows, width), BF),
            kept((rows, heads * DV), BF),
            kept((heads, rows, EP), BF),
            kept((heads, rows, EP), BF),
            kept((n, heads, DV, EP), BF),
            jax.ShapeDtypeStruct((heads, ES, DV), BF),
        ],
        scratch_shapes=[pltpu.VMEM((CH + 8, width), F32), pltpu.VMEM((heads, DV, EP), F32)],
        compiler_params=params(),
        cost_estimate=cost(100 << 30),
        name="project",
    )(stay(x), halo, keep(w_in), conv_w, keep(sel), bias)


def local_kernel(heads, ct_ref, wo_ref, gain_ref, v_ref, pq_ref, pk_ref, loc_ref, cv_ref, sel_ref, g_ref, num_ref):
    c = pl.program_id(0)
    at = rows_at(c)
    g_ref[at, :] = mm_nt(ct_ref[...], wo_ref[...]) * gain_ref[...]
    mask = causal()
    for h in range(heads):
        pq = pq_ref[h, at, :]
        logits = mm_nt(pq[:, :FEAT], pk_ref[h, at, :FEAT])
        weights = jnp.where(mask, 1.0 + logits + 0.5 * logits * logits, 0.0).astype(BF)
        lanes = slice(DV * h, DV * h + DV)
        num_ref[at, lanes] = mm(weights, v_ref[at, lanes]) + mm_nt(pq, loc_ref[c, h])


def local_part(ct, w_out, gain, v, pq, pk, loc, cv, sel, heads):
    rows, d = ct.shape
    n = rows // CH
    wide = heads * DV
    return pl.pallas_call(
        functools.partial(local_kernel, heads),
        grid=(n,),
        in_specs=[pl.BlockSpec((CH, d), lambda c: (c, 0)), KEPT, whole((1, wide))] + [KEPT] * 6,
        out_specs=[KEPT, KEPT],
        out_shape=[kept((rows, wide), F32)] * 2,
        compiler_params=params(),
        cost_estimate=LIGHT,
        name="local_part",
    )(stay(ct), keep(w_out), gain, *map(keep, (v, pq, pk, loc, cv, sel)))


def norm_kernel(heads, parts, g_ref, num_ref, gain_ref, pq_ref, *refs):
    got = refs[:parts]
    ho_ref, dn_ref, loc_ref, pre_ref, state_ref, run = refs[parts + 5 :]
    step = pl.program_id(0)
    c = pl.num_programs(0) - 1 - step
    at = rows_at(c)

    @pl.when(step == 0)
    def _():
        run[...] = jnp.zeros_like(run)
        total = got[0][...].astype(F32)
        for one in got[1:]:
            total = total + one[...].astype(F32)
        pre_ref[...] = total.astype(BF)

    for h in range(heads):
        lanes = slice(DV * h, DV * h + DV)
        pq = pq_ref[h, at, :]
        num = num_ref[at, lanes] + mm(pq[:, :ES], pre_ref[h])
        inv = lax.rsqrt(jnp.mean(num * num, 1, keepdims=True) + EPS)
        normed = num * inv
        ho_ref[at, lanes] = (normed * gain_ref[:, lanes]).astype(BF)
        g = g_ref[at, lanes]
        dn = ((g - normed * jnp.mean(g * normed, 1, keepdims=True)) * inv).astype(BF)
        dn_ref[at, lanes] = dn
        loc_ref[c, h] = run[h].astype(BF)
        run[h] = run[h] + mm_tn(dn, pq)

    @pl.when(step == pl.num_programs(0) - 1)
    def _():
        for h in range(heads):
            state_ref[h] = run[h].T[:ES].astype(BF)


def norm_part(g, num, gain, pq, got, later, heads):
    rows, wide = g.shape
    n = rows // CH
    return pl.pallas_call(
        functools.partial(norm_kernel, heads, len(got)),
        grid=(n,),
        in_specs=[KEPT, KEPT, whole((1, wide)), KEPT] + [whole((heads, ES, DV))] * len(got) + [KEPT] * 5,
        out_specs=[KEPT] * 4 + [whole((heads, ES, DV))],
        out_shape=[
            kept((rows, wide), BF),
            kept((rows, wide), BF),
            kept((n, heads, DV, EP), BF),
            kept((heads, ES, DV), BF),
            jax.ShapeDtypeStruct((heads, ES, DV), BF),
        ],
        scratch_shapes=[pltpu.VMEM((heads, DV, EP), F32)],
        compiler_params=params(),
        cost_estimate=LIGHT,
        name="norm_part",
    )(keep(g), keep(num), gain, keep(pq), *got, *map(keep, later))


def inner_kernel(heads, cv_ref, v_ref, pq_ref, pk_ref, dn_ref, loc_ref, pre_ref, sel_ref, gloc_ref, bias_ref,
                 dqk_ref, dv_ref, pre_t):
    c = pl.program_id(0)
    at = rows_at(c)

    @pl.when(c == 0)
    def _():
        pre_t[...] = jnp.zeros_like(pre_t)
        for h in range(heads):
            pre_t[h, :, :ES] = pre_ref[h].astype(F32).T

    mask = causal()
    b0 = bias_ref[0:1]
    b1 = bias_ref[1:2]
    dqk = None
    for h in range(heads):
        lanes = slice(DV * h, DV * h + DV)
        dn = dn_ref[at, lanes]
        logits = mm_nt(pq_ref[h, at, :FEAT], pk_ref[h, at, :FEAT])
        weights = jnp.where(mask, 1.0 + logits + 0.5 * logits * logits, 0.0).astype(BF)
        dv_ref[at, lanes] = mm_tn(weights, dn)
        dl = jnp.where(mask, mm_nt(dn, v_ref[at, lanes]) * (1.0 + logits), 0.0).astype(BF)
        state = (loc_ref[c, h].astype(F32) + pre_t[h]).astype(BF)
        dphi = mm(dn, state)
        cw = cv_ref[at, window(h)]
        u = mm(cw, sel_ref[h, :, : 2 * EP])
        da = (dphi * (u[:, EP:] + b1)).astype(BF)
        db = (dphi * (u[:, :EP] + b0)).astype(BF)
        moved = mm(cw, sel_ref[h, :, 4 * EP :]).astype(BF)
        part = (
            mm_nt(da, sel_ref[h, :, :EP])
            + mm_nt(db, sel_ref[h, :, EP : 2 * EP])
            + mm(dl, moved[:, :128])
            + mm_tn(dl, moved[:, 128:])
        )
        dqk = part if dqk is None else dqk + part
    dqk_ref[at, :] = dqk


def inner_part(cv, v, pq, pk, dn, loc, pre, sel, gloc, bias, heads):
    rows = cv.shape[0]
    n = rows // CH
    return pl.pallas_call(
        functools.partial(inner_kernel, heads),
        grid=(n,),
        in_specs=[KEPT] * 9 + [whole(bias.shape)],
        out_specs=[KEPT, KEPT],
        out_shape=[kept((rows, 128), F32), kept((rows, heads * DV), F32)],
        scratch_shapes=[pltpu.VMEM((heads, DV, EP), F32)],
        compiler_params=params(),
        cost_estimate=LIGHT,
        name="inner_part",
    )(*map(keep, (cv, v, pq, pk, dn, loc, pre, sel, gloc)), bias)


def outer_kernel(heads, parts, cv_ref, v_ref, pk_ref, dqk_ref, dv_ref, loc_ref, sel_ref, bias_ref, cw_ref, *refs):
    got = refs[:parts]
    dp_ref, first_ref, last_ref, ext, suf_t = refs[parts:]
    step = pl.program_id(0)
    c = pl.num_programs(0) - 1 - step
    at = rows_at(c)
    width = cv_ref.shape[1]

    @pl.when(step == 0)
    def _():
        suf_t[...] = jnp.zeros_like(suf_t)
        for h in range(heads):
            total = got[0][h].astype(F32)
            for one in got[1:]:
                total = total + one[h].astype(F32)
            suf_t[h, :, :ES] = total.T
        ext[CH:, :] = jnp.zeros((8, width), F32)

    b0 = bias_ref[0:1]
    b1 = bias_ref[1:2]
    lane = lane_iota()
    tiles = [None] * (-(-width // 128))

    def put(t, piece):
        tiles[t] = piece if tiles[t] is None else tiles[t] + piece

    dqk = dqk_ref[at, :]
    for h in range(heads):
        lanes = slice(DV * h, DV * h + DV)
        state = (loc_ref[c, h].astype(F32) + suf_t[h]).astype(BF)
        dphi = mm(v_ref[at, lanes], state)
        u = mm(cv_ref[at, window(h)], sel_ref[h, :, 2 * EP : 4 * EP])
        da = (dphi * (u[:, EP:] + b1)).astype(BF)
        db = (dphi * (u[:, :EP] + b0)).astype(BF)
        own = (
            dqk
            + mm_nt(da, sel_ref[h, :, 2 * EP : 3 * EP])
            + mm_nt(db, sel_ref[h, :, 3 * EP : 4 * EP])
        )
        q0 = (HW * h) % 128
        put((HW * h) // 128, jnp.where((lane >= q0) & (lane < q0 + 2 * FEAT), own, 0.0))
        dv = dv_ref[at, lanes] + mm_nt(pk_ref[h, at, :], state)
        tile, off = value_place(h)
        if off == 0:
            put(tile, dv)
        else:
            moved = pltpu.roll(dv, off, 1)
            put(tile, jnp.where(lane >= off, moved, 0.0))
            put(tile + 1, jnp.where(lane < off, moved, 0.0))
    for t, tile in enumerate(tiles):
        end = min(128 * t + 128, width)
        ext[:CH, 128 * t : end] = tile[:, : end - 128 * t]
    dp = (cw_ref[0:1] * ext[:CH, :] + cw_ref[1:2] * ext[1 : CH + 1, :]
          + cw_ref[2:3] * ext[2 : CH + 2, :])
    dp_ref[at, :] = dp.astype(BF)

    @pl.when(step == 0)
    def _():
        last_ref[...] = dp[CH - 16 :]

    ext[CH:, :] = ext[0:8, :]
    first_ref[...] = ext[0:8, :]


def outer_part(cv, v, pk, dqk, dv, loc, got, sel, bias, conv_w, heads):
    rows, width = cv.shape
    n = rows // CH
    return pl.pallas_call(
        functools.partial(outer_kernel, heads, len(got)),
        grid=(n,),
        in_specs=[KEPT] * 7
        + [whole(bias.shape), whole((3, width))]
        + [whole((heads, ES, DV))] * len(got),
        out_specs=[KEPT, whole((8, width)), KEPT],
        out_shape=[
            kept((rows, width), BF),
            jax.ShapeDtypeStruct((8, width), F32),
            kept((16, width), F32),
        ],
        scratch_shapes=[pltpu.VMEM((CH + 8, width), F32), pltpu.VMEM((heads, DV, EP), F32)],
        compiler_params=params(),
        cost_estimate=LIGHT,
        name="outer_part",
    )(*map(keep, (cv, v, pk, dqk, dv, loc, sel)), bias, conv_w, *got)


def columns_kernel(count, place_ref, w_ref, *refs):
    outs, sems = refs[: count - 1], refs[-1]
    wide = outs[0].shape[1]
    copies = []
    for m in range(1, count):
        start = pl.multiple_of(lax.bitwise_xor(place_ref[0], m) * wide, wide)
        copies.append(
            pltpu.make_async_copy(w_ref.at[:, pl.ds(start, wide)], outs[m - 1], sems.at[m - 1])
        )
    for copy in copies:
        copy.start()
    for copy in copies:
        copy.wait()


def columns(place, w_out, count):
    rows, d = w_out.shape
    anywhere = pl.BlockSpec(memory_space=pltpu.HBM)
    return pl.pallas_call(
        functools.partial(columns_kernel, count),
        grid_spec=pltpu.PrefetchScalarGridSpec(
            num_scalar_prefetch=1,
            grid=(1,),
            in_specs=[anywhere],
            out_specs=[anywhere] * (count - 1),
            scratch_shapes=[pltpu.SemaphoreType.DMA((count - 1,))],
        ),
        out_shape=[jax.ShapeDtypeStruct((rows, d // count), w_out.dtype)] * (count - 1),
        compiler_params=pltpu.CompilerParams(vmem_limit_bytes=VMEM),
        cost_estimate=LIGHT,
        name="columns",
    )(place, stay(w_out))


def shifted(array, by):
    count = lax.axis_size("seq")
    pairs = [(i, i + by) for i in range(count) if 0 <= i + by < count]
    return lax.ppermute(array, "seq", pairs)


def from_others(part, sign):
    return [shifted(part, sign * step) for step in range(1, lax.axis_size("seq"))]


def out_kernel(count, sw, place_ref, *refs):
    tops, lows, ws = refs[:count], refs[count : 2 * count], refs[2 * count : 3 * count]
    send_ref, keep_ref = refs[3 * count :]
    c = pl.program_id(0)
    half_chunks = pl.num_programs(0) // 2
    odd = place_ref[1] == 1

    def product(parts):
        total = None
        for part, w in zip(parts, ws):
            one = mm(part[...], w[...])
            total = one if total is None else total + one
        first, second = total[:, :sw], total[:, sw:]
        send_ref[...] = jnp.where(odd, first, second).astype(BF)
        keep_ref[...] = jnp.where(odd, second, first)

    @pl.when(c < half_chunks)
    def _():
        product(tops)

    @pl.when(c >= half_chunks)
    def _():
        product(lows)


def out_part(place, tops, lows, ws):
    count = len(ws)
    rows = 2 * CH * (lows[0][1] // CH)
    wide = tops[0][0].shape[1]
    sw = ws[1].shape[1] // 2
    part = rows // (2 * CH)
    row = pl.BlockSpec((CH, sw), lambda c, place: (c, 0))
    operands, specs = [], []
    for array, start in tops:
        operands.append(array)
        specs.append(
            pl.BlockSpec((CH, wide), lambda c, place, s=start // CH: (s + jnp.minimum(c, part - 1), 0))
        )
    for array, start in lows:
        operands.append(array)
        specs.append(
            pl.BlockSpec((CH, wide), lambda c, place, s=start // CH: (s + jnp.maximum(c - part, 0), 0))
        )
    return pl.pallas_call(
        functools.partial(out_kernel, count, sw),
        grid_spec=pltpu.PrefetchScalarGridSpec(
            num_scalar_prefetch=1,
            grid=(rows // CH,),
            in_specs=specs
            + [pl.BlockSpec((wide, 2 * sw), lambda c, place: (0, place[0]))]
            + [pl.BlockSpec((wide, 2 * sw), lambda c, place: (0, 0))] * (count - 1),
            out_specs=[row, row],
        ),
        out_shape=[jax.ShapeDtypeStruct((rows, sw), BF), jax.ShapeDtypeStruct((rows, sw), F32)],
        compiler_params=params(),
        cost_estimate=LIGHT,
        name="out_part",
    )(place, *operands, *map(stay, ws))


def grad_top_kernel(place_ref, dp_ref, w_ref, out_ref):
    half, sw = out_ref.shape[1:]
    block = 2 * lax.bitwise_xor(place_ref[0], pl.program_id(0)) + 1 - place_ref[1]
    w = w_ref[pl.ds(pl.multiple_of(block * sw, sw), sw), :]
    out_ref[0] = mm_nt(dp_ref[:half, :], w).astype(BF)


def grad_low_kernel(place_ref, dp_ref, w_ref, last_ref, after_ref, cw_ref, x_ref, y_ref,
                    out_ref, low_ref, x_top_ref, y_low_ref):
    half, sw = out_ref.shape[1:]
    r = pl.program_id(0)

    @pl.when(r == 0)
    def _():
        low_ref[...] = dp_ref[half:, :]
        row = lax.broadcasted_iota(jnp.int32, last_ref.shape, 0)
        a0, a1 = after_ref[0:1], after_ref[1:2]
        one = cw_ref[2:3] * a0
        two = cw_ref[1:2] * a0 + cw_ref[2:3] * a1
        tail = last_ref[...] + jnp.where(row == 14, one, 0.0) + jnp.where(row == 15, two, 0.0)
        low_ref[half - 16 :, :] = tail.astype(BF)
        x_top_ref[...] = x_ref[:half, :]
        y_low_ref[...] = y_ref[half:, :]

    block = 2 * lax.bitwise_xor(place_ref[0], r) + 1 - place_ref[1]
    w = w_ref[pl.ds(pl.multiple_of(block * sw, sw), sw), :]
    out_ref[0] = mm_nt(low_ref[...], w).astype(BF)


def grad_send(place, dp, w_in, count, halo=None):
    rows, width = dp.shape
    half = rows // 2
    sw = w_in.shape[0] // (2 * count)
    out_spec = pl.BlockSpec((1, half, sw), lambda r, place: (r, 0, 0))
    out_shape = jax.ShapeDtypeStruct((count, half, sw), BF)
    args = [keep(dp), keep(w_in)]
    in_specs = [KEPT, KEPT]
    if halo is not None:
        last, after, conv_w, x_got, y_got = halo
        args += [keep(last), after, conv_w, keep(x_got), keep(y_got)]
        in_specs += [KEPT, whole((8, width)), whole((3, width)), KEPT, KEPT]
        out_spec = [out_spec, KEPT, KEPT, KEPT]
        out_shape = [out_shape, kept((half, width), BF)] + [kept((half, x_got.shape[1]), BF)] * 2
    return pl.pallas_call(
        grad_top_kernel if halo is None else grad_low_kernel,
        grid_spec=pltpu.PrefetchScalarGridSpec(
            num_scalar_prefetch=1, grid=(count,), in_specs=in_specs, out_specs=out_spec
        ),
        out_shape=out_shape,
        compiler_params=params(),
        cost_estimate=LIGHT,
        name="grad_top" if halo is None else "grad_low",
    )(place, *args)


def grad_keep_kernel(count, low_first, place_ref, dp_ref, w_ref, got_ref, send_ref, keep_ref):
    r = pl.program_id(0)
    half, sw = got_ref.shape[1:]
    block = 2 * lax.bitwise_xor(place_ref[0], r) + place_ref[1]
    w = w_ref[pl.ds(pl.multiple_of(block * sw, sw), sw), :]
    total = (mm_nt(dp_ref[:half, :], w) + got_ref[0].astype(F32)).astype(BF)
    leaves = (r % 2 == 1) if low_first else (r >= count // 2)

    @pl.when(leaves)
    def _():
        send_ref[0] = total

    @pl.when(jnp.logical_not(leaves))
    def _():
        keep_ref[0] = total


def grad_keep(place, dp, w_in, got, low_first):
    width = dp.shape[1]
    count, half, sw = got.shape
    part = count // 2
    blk = (1, half, sw)
    if low_first:
        specs = [pl.BlockSpec(blk, lambda r, place: (r // 2, 0, 0))] * 2
    else:
        specs = [
            pl.BlockSpec(blk, lambda r, place: (jnp.maximum(r - part, 0), 0, 0)),
            pl.BlockSpec(blk, lambda r, place: (jnp.minimum(r, part - 1), 0, 0)),
        ]
    return pl.pallas_call(
        functools.partial(grad_keep_kernel, count, low_first),
        grid_spec=pltpu.PrefetchScalarGridSpec(
            num_scalar_prefetch=1,
            grid=(count,),
            in_specs=[KEPT, KEPT, pl.BlockSpec(blk, lambda r, place: (r, 0, 0))],
            out_specs=specs,
        ),
        out_shape=[jax.ShapeDtypeStruct((part, half, sw), BF)] * 2,
        compiler_params=params(),
        cost_estimate=LIGHT,
        name="grad_keep",
    )(place, keep(dp), keep(w_in), got)


def swapped(array, distance):
    count = lax.axis_size("tp")
    return lax.ppermute(array, "tp", [(i, i ^ distance) for i in range(count)])


def summed(a, b):
    return a.astype(F32) + b.astype(F32)


def reduce_both(a_send, a_keep, b_send, b_keep, a_own, b_own, meanwhile):
    pairs = lax.axis_size("tp") // 2
    a_step, b_step = 1, pairs // 2
    while True:
        a_got = swapped(a_send, 2 * a_step)
        b_got = swapped(b_send, 2 * b_step)
        left = a_keep.shape[0]
        a_keep, b_keep = meanwhile(a_keep, b_keep)
        if left == 1:
            return a_keep[0], a_got[0], b_keep[0], b_got[0]
        a_send = summed(a_keep[1::2], a_got[1::2]).astype(BF)
        b_send = summed(b_keep[left // 2 :], b_got[left // 2 :]).astype(BF)
        a_keep = summed(a_keep[0::2], a_got[0::2])
        b_keep = summed(b_keep[: left // 2], b_got[: left // 2])
        if left == 2:
            a_keep = a_keep + a_own
            b_keep = b_keep + b_own
        a_step, b_step = a_step * 2, b_step // 2


def finish_kernel(half, ak_ref, ag_ref, bk_ref, bg_ref, out_ref):
    out_ref[:half, :] = (ak_ref[...] + ag_ref[...].astype(F32)).astype(BF)
    out_ref[half:, :] = (bk_ref[...] + bg_ref[...].astype(F32)).astype(BF)


def finish(a_keep, a_got, b_keep, b_got):
    half, sw = a_keep.shape
    return pl.pallas_call(
        functools.partial(finish_kernel, half),
        out_shape=jax.ShapeDtypeStruct((2 * half, sw), BF),
        compiler_params=pltpu.CompilerParams(vmem_limit_bytes=VMEM),
        cost_estimate=LIGHT,
        name="finish",
    )(a_keep, a_got, b_keep, b_got)


def per_device(inputs, cotangent, w_in, conv_w, norm_gain, w_out, keep_flags):
    heads = keep_flags.shape[0]
    sel, bias = selectors(heads)
    tp = lax.axis_size("tp")
    pairs = tp // 2
    me = lax.axis_index("tp")
    pair = me // 2
    place = jnp.stack([pair, me % 2]).astype(jnp.int32)
    slice_width = inputs.shape[1] // tp
    column = me * slice_width
    gain = (norm_gain.reshape(heads, DV) * keep_flags.astype(F32)[:, None]).reshape(1, heads * DV)
    halo = shifted(inputs[-16:], 1)

    half = inputs.shape[0] // 2
    far = list(columns(place, w_out, pairs))
    near = [swapped(far.pop(0), 2 * m) for m in (1, 2)]
    halo, place, gain = lax.optimization_barrier((halo, place, gain))
    cv, v, pq, pk, loc, state = project(inputs, halo, w_in, conv_w, sel, bias, heads)
    state, near, far = lax.optimization_barrier((state, near, far))
    far = [swapped(columns, 2 * m) for m, columns in enumerate(far, 3)]
    before = from_others(state, 1)
    g, num = local_part(cotangent, w_out, gain, v, pq, pk, loc, cv, sel, heads)
    ho, dn, gloc, pre, gstate = norm_part(g, num, gain, pq, before, (cv, v, pk, loc, sel), heads)
    step = pairs // 2
    got = {r: swapped(ho, 2 * r) for r in range(1, pairs) if r != 1 + step}
    later = from_others(gstate, -1)
    bias_, far = lax.optimization_barrier((bias, far))
    dqk, dv = inner_part(cv, v, pq, pk, dn, loc, pre, sel, gloc, bias_, heads)
    dp, first, last = outer_part(cv, v, pk, dqk, dv, gloc, later, sel, bias, conv_w, heads)
    after = shifted(first, -1)
    got_top = swapped(grad_send(place, dp, w_in, pairs), 1)
    sent_low, dp_low, x_top, y_low = grad_send(
        place, dp, w_in, pairs, (last, after, conv_w, got[1], got[step])
    )
    got_low = swapped(sent_low, 1)
    tops = [(ho, 0)] + [(got.get(r), 0) for r in range(1, pairs)]
    lows = [(ho, half)] + [(got.get(r), half) for r in range(1, pairs)]
    x_top, y_low = swapped(x_top, 2 * step), swapped(y_low, 2)
    w_cols = [w_out] + near + far
    a_send, a_keep = grad_keep(place, dp, w_in, got_top, True)
    b_send, b_keep = grad_keep(place, dp_low, w_in, got_low, False)
    b_send, x_top, y_low = lax.optimization_barrier((b_send, x_top, y_low))
    tops[1 + step], lows[1 + step] = (x_top, 0), (y_low, 0)

    x_own = lax.dynamic_slice_in_dim(inputs, column, slice_width, 1).astype(F32)
    c_own = lax.dynamic_slice_in_dim(cotangent, column, slice_width, 1).astype(F32)
    stage = []

    def meanwhile(a, b):
        if not stage:
            out_send, out_keep = out_part(place, tops, lows, w_cols)
            stage.append(x_own + out_keep)
            stage.append(out_send)
            a, b, stage[1] = lax.optimization_barrier((a, b, stage[1]))
            stage.append(swapped(stage[1], 1))
        elif len(stage) == 3:
            stage.append((stage[0] + stage[2].astype(F32)).astype(BF))
            a, b, stage[3] = lax.optimization_barrier((a, b, stage[3]))
        return a, b

    halves = reduce_both(a_send, a_keep, b_send, b_keep, c_own[None, :half], c_own[None, half:], meanwhile)
    return stage[3], finish(*halves)


def solution(mesh):
    placed = (
        P("seq", None),
        P("seq", None),
        P(None, "tp"),
        P(None, "tp"),
        P("tp"),
        P("tp", None),
        P("tp"),
    )
    return jax.shard_map(
        per_device,
        mesh=mesh,
        in_specs=placed,
        out_specs=(P("seq", "tp"), P("seq", "tp")),
        check_vma=False,
    )
```

```python
import functools

import jax
import jax.numpy as jnp
import numpy as np
from jax import lax
from jax.experimental import pallas as pl
from jax.experimental.pallas import tpu as pltpu
from jax.sharding import PartitionSpec as P

FEAT = 16
DV = 128
HW = 2 * FEAT + DV
EP = 256
ES = 160
CH = 256
EPS = 1e-06
BF = jnp.bfloat16
F32 = jnp.float32
VMEM = 16 * 1024 * 1024


def mm(a, b):
    return lax.dot_general(a, b, (((1,), (0,)), ((), ())), preferred_element_type=F32)


def mm_nt(a, b):
    return lax.dot_general(a, b, (((1,), (1,)), ((), ())), preferred_element_type=F32)


def mm_tn(a, b):
    return lax.dot_general(a, b, (((0,), (0,)), ((), ())), preferred_element_type=F32)


def selectors(heads):
    sel = np.zeros((heads, 128, 4 * EP), np.float32)
    bias = np.zeros((8, EP), np.float32)
    bias[1, :FEAT] = 1.0
    bias[0, FEAT] = bias[1, FEAT] = 1.0
    for h in range(heads):
        q0 = (HW * h) % 128
        k0 = q0 + FEAT
        for i in range(FEAT):
            sel[h, q0 + i, i] = 0.5
            sel[h, k0 + i, 2 * EP + i] = 0.5
        col = FEAT + 1
        for i in range(FEAT):
            for j in range(i, FEAT):
                sel[h, q0 + i, col] = 0.25 if i == j else 0.5
                sel[h, q0 + j, EP + col] = 0.5
                sel[h, k0 + i, 2 * EP + col] = 0.5
                sel[h, k0 + j, 3 * EP + col] = 0.5
                col += 1
    return jnp.asarray(sel, BF), jnp.asarray(bias, F32)


def window(h):
    t = (HW * h) // 128
    return slice(128 * t, 128 * t + 128)


def value_place(h):
    start = HW * h + 2 * FEAT
    return start // 128, start % 128


def lane_iota():
    return lax.broadcasted_iota(jnp.int32, (CH, 128), 1)


def take_values(conv, h):
    tile, off = value_place(h)
    first = conv[:, 128 * tile : 128 * tile + 128]
    if off == 0:
        return first
    second = conv[:, 128 * tile + 128 : min(128 * tile + 256, conv.shape[1])]
    if second.shape[1] < 128:
        second = jnp.concatenate([second, jnp.zeros((CH, 128 - second.shape[1]), second.dtype)], 1)
    a = pltpu.roll(first, 128 - off, 1)
    b = pltpu.roll(second, 128 - off, 1)
    return jnp.where(lane_iota() < 128 - off, a, b)


def causal():
    r = lax.broadcasted_iota(jnp.int32, (CH, CH), 0)
    c = lax.broadcasted_iota(jnp.int32, (CH, CH), 1)
    return r >= c


def params():
    return pltpu.CompilerParams(dimension_semantics=("arbitrary",), vmem_limit_bytes=VMEM)


def whole(shape):
    return pl.BlockSpec(shape, lambda c, *_: (0,) * len(shape))


KEPT = pl.BlockSpec(memory_space=pltpu.VMEM)


def kept(shape, dtype):
    return pltpu.VMEM(shape, dtype)


def keep(array):
    return pltpu.with_memory_space_constraint(array, pltpu.VMEM)


def stay(array):
    return pltpu.with_memory_space_constraint(array, pltpu.HBM)


def cost(flops):
    return pl.CostEstimate(flops=int(flops), bytes_accessed=1 << 20, transcendentals=0)


LIGHT = cost(1000)


def rows_at(c):
    return pl.ds(pl.multiple_of(c * CH, CH), CH)


def biased(u, bias):
    return jnp.concatenate([u[:, :128] + bias[:, :128], u[:, 128:]], 1)


def project_kernel(heads, x_ref, halo_ref, w_ref, cw_ref, sel_ref, bias_ref,
                   v_ref, pq_ref, pk_ref, fq_ref, fk_ref, loc_ref, state_ref, ext, run):
    c = pl.program_id(0)
    at = rows_at(c)

    @pl.when(c == 0)
    def _():
        before = mm(halo_ref[...], w_ref[...]).astype(BF).astype(F32)
        ext[0:8, :] = before[8:16]
        run[...] = jnp.zeros_like(run)

    ext[8:, :] = mm(x_ref[...], w_ref[...]).astype(BF).astype(F32)
    conv = (cw_ref[0:1] * ext[8 : 8 + CH, :] + cw_ref[1:2] * ext[7 : 7 + CH, :]
            + cw_ref[2:3] * ext[6 : 6 + CH, :])
    ext[0:8, :] = ext[CH : CH + 8, :]
    conv_b = conv.astype(BF)
    conv = conv_b.astype(F32)
    b0 = bias_ref[0:1]
    b1 = bias_ref[1:2]
    for h in range(heads):
        u = mm(conv_b[:, window(h)], sel_ref[h])
        first, second = biased(u[:, :EP], b0), biased(u[:, EP : 2 * EP], b1)
        pq_ref[h, at, :] = (first * second).astype(BF)
        fq_ref[h, at, :EP] = first.astype(BF)
        fq_ref[h, at, EP:] = second.astype(BF)
        first, second = biased(u[:, 2 * EP : 3 * EP], b0), biased(u[:, 3 * EP :], b1)
        pk = (first * second).astype(BF)
        pk_ref[h, at, :] = pk
        fk_ref[h, at, :EP] = first.astype(BF)
        fk_ref[h, at, EP:] = second.astype(BF)
        v = take_values(conv, h).astype(BF)
        v_ref[at, DV * h : DV * h + DV] = v
        loc_ref[c, h] = run[h].astype(BF)
        run[h] = run[h] + mm_tn(v, pk)

    @pl.when(c == pl.num_programs(0) - 1)
    def _():
        for h in range(heads):
            state_ref[h] = run[h].T[:ES].astype(BF)


def project(x, halo, w_in, conv_w, sel, bias, heads):
    rows, d = x.shape
    width = w_in.shape[1]
    n = rows // CH
    return pl.pallas_call(
        functools.partial(project_kernel, heads),
        grid=(n,),
        in_specs=[
            pl.BlockSpec((CH, d), lambda c: (c, 0)),
            whole((16, d)),
            KEPT,
            whole((3, width)),
            KEPT,
            whole(bias.shape),
        ],
        out_specs=[KEPT] * 6 + [whole((heads, ES, DV))],
        out_shape=[
            kept((rows, heads * DV), BF),
            kept((heads, rows, EP), BF),
            kept((heads, rows, EP), BF),
            kept((heads, rows, 2 * EP), BF),
            kept((heads, rows, 2 * EP), BF),
            kept((n, heads, DV, EP), BF),
            jax.ShapeDtypeStruct((heads, ES, DV), BF),
        ],
        scratch_shapes=[pltpu.VMEM((CH + 8, width), F32), pltpu.VMEM((heads, DV, EP), F32)],
        compiler_params=params(),
        cost_estimate=cost(100 << 30),
        name="project",
    )(stay(x), halo, keep(w_in), conv_w, keep(sel), bias)


def local_kernel(heads, ct_ref, wo_ref, gain_ref, v_ref, pq_ref, pk_ref, loc_ref, fq_ref, fk_ref, sel_ref,
                 g_ref, num_ref, wt_ref, slope_ref):
    c = pl.program_id(0)
    at = rows_at(c)
    g_ref[at, :] = mm_nt(ct_ref[...], wo_ref[...]) * gain_ref[...]
    mask = causal()
    for h in range(heads):
        pq = pq_ref[h, at, :]
        logits = mm_nt(pq[:, :FEAT], pk_ref[h, at, :FEAT])
        slope = 1.0 + logits
        weights = jnp.where(mask, 0.5 + 0.5 * slope * slope, 0.0).astype(BF)
        wt_ref[h, at, :] = weights
        slope_ref[h, at, :] = jnp.where(mask, slope, 0.0).astype(BF)
        lanes = slice(DV * h, DV * h + DV)
        num_ref[at, lanes] = mm(weights, v_ref[at, lanes]) + mm_nt(pq, loc_ref[c, h])


def local_part(ct, w_out, gain, v, pq, pk, loc, fq, fk, sel, heads):
    rows, d = ct.shape
    n = rows // CH
    wide = heads * DV
    return pl.pallas_call(
        functools.partial(local_kernel, heads),
        grid=(n,),
        in_specs=[pl.BlockSpec((CH, d), lambda c: (c, 0)), KEPT, whole((1, wide))] + [KEPT] * 7,
        out_specs=[KEPT] * 4,
        out_shape=[kept((rows, wide), F32)] * 2 + [kept((heads, rows, CH), BF)] * 2,
        compiler_params=params(),
        cost_estimate=LIGHT,
        name="local_part",
    )(stay(ct), keep(w_out), gain, *map(keep, (v, pq, pk, loc, fq, fk, sel)))


def norm_kernel(heads, parts, passed, g_ref, num_ref, gain_ref, pq_ref, ones_ref, *refs):
    got = refs[:parts]
    ho_ref, dn_ref, loc_ref, pre_ref, state_ref, run = refs[parts + passed :]
    step = pl.program_id(0)
    c = pl.num_programs(0) - 1 - step
    at = rows_at(c)

    @pl.when(step == 0)
    def _():
        run[...] = jnp.zeros_like(run)
        total = got[0][...].astype(F32)
        for one in got[1:]:
            total = total + one[...].astype(F32)
        pre_ref[...] = total.astype(BF)

    for h in range(0, heads, 2):
        lanes = slice(DV * h, DV * h + 2 * DV)
        pqs = [pq_ref[h, at, :], pq_ref[h + 1, at, :]]
        num = num_ref[at, lanes] + jnp.concatenate(
            [mm(pqs[0][:, :ES], pre_ref[h]), mm(pqs[1][:, :ES], pre_ref[h + 1])], 1
        )
        inv = lax.rsqrt(mm((num * num).astype(BF), ones_ref[...]) + EPS)
        normed = num * inv
        ho_ref[at, lanes] = (normed * gain_ref[:, lanes]).astype(BF)
        g = g_ref[at, lanes]
        dn = ((g - normed * mm((g * normed).astype(BF), ones_ref[...])) * inv).astype(BF)
        dn_ref[at, lanes] = dn
        for i in range(2):
            loc_ref[c, h + i] = run[h + i].astype(BF)
            run[h + i] = run[h + i] + mm_tn(dn[:, DV * i : DV * i + DV], pqs[i])

    @pl.when(step == pl.num_programs(0) - 1)
    def _():
        for h in range(heads):
            state_ref[h] = run[h].T[:ES].astype(BF)


def norm_part(g, num, gain, pq, got, later, heads):
    ones = jnp.asarray(np.kron(np.eye(2), np.full((DV, DV), 1.0 / DV)), BF)
    rows, wide = g.shape
    n = rows // CH
    return pl.pallas_call(
        functools.partial(norm_kernel, heads, len(got), len(later)),
        grid=(n,),
        in_specs=[KEPT, KEPT, whole((1, wide)), KEPT, whole((2 * DV, 2 * DV))]
        + [whole((heads, ES, DV))] * len(got)
        + [KEPT] * len(later),
        out_specs=[KEPT] * 4 + [whole((heads, ES, DV))],
        out_shape=[
            kept((rows, wide), BF),
            kept((rows, wide), BF),
            kept((n, heads, DV, EP), BF),
            kept((heads, ES, DV), BF),
            jax.ShapeDtypeStruct((heads, ES, DV), BF),
        ],
        scratch_shapes=[pltpu.VMEM((heads, DV, EP), F32)],
        compiler_params=params(),
        cost_estimate=cost(16 << 30),
        name="norm_part",
    )(keep(g), keep(num), gain, keep(pq), ones, *got, *map(keep, later))


def inner_kernel(heads, v_ref, pq_ref, pk_ref, fq_ref, wt_ref, slope_ref, dn_ref, loc_ref, pre_ref, sel_ref,
                 fk_ref, gloc_ref, dqk_ref, dv_ref, xk_ref, pre_t):
    c = pl.program_id(0)
    at = rows_at(c)

    @pl.when(c == 0)
    def _():
        pre_t[...] = jnp.zeros_like(pre_t)
        for h in range(heads):
            pre_t[h, :, :ES] = pre_ref[h].astype(F32).T

    linear = lane_iota() < FEAT
    dqk = None
    for h in range(heads):
        lanes = slice(DV * h, DV * h + DV)
        dn = dn_ref[at, lanes]
        dv_ref[at, lanes] = mm_tn(wt_ref[h, at, :], dn)
        dl = (mm_nt(dn, v_ref[at, lanes]) * slope_ref[h, at, :].astype(F32)).astype(BF)
        xk_ref[h, at, :] = mm_tn(dl, pq_ref[h, at, :128])
        state = (loc_ref[c, h].astype(F32) + pre_t[h]).astype(BF)
        dphi = mm(dn, state)
        dphi = jnp.concatenate(
            [dphi[:, :128] + jnp.where(linear, mm(dl, pk_ref[h, at, :128]), 0.0), dphi[:, 128:]], 1
        )
        da = (dphi * fq_ref[h, at, EP:].astype(F32)).astype(BF)
        db = (dphi * fq_ref[h, at, :EP].astype(F32)).astype(BF)
        part = mm_nt(da, sel_ref[h, :, :EP]) + mm_nt(db, sel_ref[h, :, EP : 2 * EP])
        dqk = part if dqk is None else dqk + part
    dqk_ref[at, :] = dqk


def inner_part(v, pq, pk, fq, wt, slope, dn, loc, pre, sel, fk, gloc, heads):
    rows = v.shape[0]
    n = rows // CH
    return pl.pallas_call(
        functools.partial(inner_kernel, heads),
        grid=(n,),
        in_specs=[KEPT] * 12,
        out_specs=[KEPT] * 3,
        out_shape=[
            kept((rows, 128), F32),
            kept((rows, heads * DV), F32),
            kept((heads, rows, 128), F32),
        ],
        scratch_shapes=[pltpu.VMEM((heads, DV, EP), F32)],
        compiler_params=params(),
        cost_estimate=LIGHT,
        name="inner_part",
    )(*map(keep, (v, pq, pk, fq, wt, slope, dn, loc, pre, sel, fk, gloc)))


def outer_kernel(heads, parts, v_ref, pk_ref, fk_ref, dqk_ref, dv_ref, xk_ref, loc_ref, sel_ref, cw_ref, *refs):
    got = refs[:parts]
    top_ref, dp_ref, first_ref, last_ref, ext, suf_t = refs[parts:]
    half_chunks = pl.num_programs(0) // 2
    step = pl.program_id(0)
    c = pl.num_programs(0) - 1 - step
    at = rows_at(c)
    width = cw_ref.shape[1]

    @pl.when(step == 0)
    def _():
        suf_t[...] = jnp.zeros_like(suf_t)
        for h in range(heads):
            total = got[0][h].astype(F32)
            for one in got[1:]:
                total = total + one[h].astype(F32)
            suf_t[h, :, :ES] = total.T
        ext[CH:, :] = jnp.zeros((8, width), F32)

    lane = lane_iota()
    tiles = [None] * (-(-width // 128))

    def put(t, piece):
        tiles[t] = piece if tiles[t] is None else tiles[t] + piece

    dqk = dqk_ref[at, :]
    for h in range(heads):
        lanes = slice(DV * h, DV * h + DV)
        state = (loc_ref[c, h].astype(F32) + suf_t[h]).astype(BF)
        dphi = mm(v_ref[at, lanes], state)
        dphi = jnp.concatenate(
            [dphi[:, :128] + jnp.where(lane < FEAT, xk_ref[h, at, :], 0.0), dphi[:, 128:]], 1
        )
        da = (dphi * fk_ref[h, at, EP:].astype(F32)).astype(BF)
        db = (dphi * fk_ref[h, at, :EP].astype(F32)).astype(BF)
        own = (
            dqk
            + mm_nt(da, sel_ref[h, :, 2 * EP : 3 * EP])
            + mm_nt(db, sel_ref[h, :, 3 * EP : 4 * EP])
        )
        q0 = (HW * h) % 128
        put((HW * h) // 128, jnp.where((lane >= q0) & (lane < q0 + 2 * FEAT), own, 0.0))
        dv = dv_ref[at, lanes] + mm_nt(pk_ref[h, at, :], state)
        tile, off = value_place(h)
        if off == 0:
            put(tile, dv)
        else:
            moved = pltpu.roll(dv, off, 1)
            put(tile, jnp.where(lane >= off, moved, 0.0))
            put(tile + 1, jnp.where(lane < off, moved, 0.0))
    for t, tile in enumerate(tiles):
        end = min(128 * t + 128, width)
        ext[:CH, 128 * t : end] = tile[:, : end - 128 * t]
    dp = (cw_ref[0:1] * ext[:CH, :] + cw_ref[1:2] * ext[1 : CH + 1, :]
          + cw_ref[2:3] * ext[2 : CH + 2, :])
    dp_ref[at, :] = dp.astype(BF)

    @pl.when(c < half_chunks)
    def _():
        top_ref[at, :] = dp.astype(BF)

    @pl.when(step == 0)
    def _():
        last_ref[...] = dp[CH - 16 :]

    ext[CH:, :] = ext[0:8, :]
    first_ref[...] = ext[0:8, :]


def outer_part(v, pk, fk, dqk, dv, xk, loc, got, sel, conv_w, heads):
    rows, width = v.shape[0], conv_w.shape[1]
    n = rows // CH
    return pl.pallas_call(
        functools.partial(outer_kernel, heads, len(got)),
        grid=(n,),
        in_specs=[KEPT] * 8 + [whole((3, width))] + [whole((heads, ES, DV))] * len(got),
        out_specs=[KEPT, KEPT, whole((8, width)), KEPT],
        out_shape=[
            kept((rows // 2, width), BF),
            kept((rows, width), BF),
            jax.ShapeDtypeStruct((8, width), F32),
            kept((16, width), F32),
        ],
        scratch_shapes=[pltpu.VMEM((CH + 8, width), F32), pltpu.VMEM((heads, DV, EP), F32)],
        compiler_params=params(),
        cost_estimate=cost(16 << 30),
        name="outer_part",
    )(*map(keep, (v, pk, fk, dqk, dv, xk, loc, sel)), conv_w, *got)


def columns_kernel(which, place_ref, w_ref, *refs):
    outs, sems = refs[-1 - len(which) : -1], refs[-1]
    wide = outs[0].shape[1]
    copies = []
    for i, m in enumerate(which):
        start = pl.multiple_of(lax.bitwise_xor(place_ref[0], m) * wide, wide)
        copies.append(pltpu.make_async_copy(w_ref.at[:, pl.ds(start, wide)], outs[i], sems.at[i]))
    if len(refs) > len(which) + 1:
        x_ref, wi_ref, tail_ref, wi_out_ref = refs[:4]
        rows = tail_ref.shape[0]
        copies.append(
            pltpu.make_async_copy(x_ref.at[pl.ds(x_ref.shape[0] - rows, rows), :], tail_ref, sems.at[len(which)])
        )
        count, sw = wi_out_ref.shape[:2]
        for r in range(count):
            block = 2 * lax.bitwise_xor(place_ref[0], r) + 1 - place_ref[1]
            copies.append(
                pltpu.make_async_copy(
                    wi_ref.at[pl.ds(pl.multiple_of(block * sw, sw), sw), :],
                    wi_out_ref.at[r],
                    sems.at[len(which) + 1 + r],
                )
            )
    for copy in copies:
        copy.start()
    for copy in copies:
        copy.wait()


def columns(place, w_out, which, count, x=None, w_in=None):
    rows, d = w_out.shape
    anywhere = pl.BlockSpec(memory_space=pltpu.HBM)
    out_shape = [jax.ShapeDtypeStruct((rows, d // count), w_out.dtype)] * len(which)
    args = [stay(w_out)]
    if x is not None:
        args += [stay(x), stay(w_in)]
        out_shape = [
            jax.ShapeDtypeStruct((16, x.shape[1]), x.dtype),
            jax.ShapeDtypeStruct((count, w_in.shape[0] // (2 * count), w_in.shape[1]), w_in.dtype),
        ] + out_shape
    return pl.pallas_call(
        functools.partial(columns_kernel, which),
        grid_spec=pltpu.PrefetchScalarGridSpec(
            num_scalar_prefetch=1,
            grid=(1,),
            in_specs=[anywhere] * len(args),
            out_specs=[anywhere] * len(out_shape),
            scratch_shapes=[pltpu.SemaphoreType.DMA((len(which) + 1 + count,))],
        ),
        out_shape=out_shape,
        compiler_params=pltpu.CompilerParams(vmem_limit_bytes=VMEM),
        cost_estimate=LIGHT,
        name="columns",
    )(place, *args)


def shifted(array, by):
    count = lax.axis_size("seq")
    pairs = [(i, i + by) for i in range(count) if 0 <= i + by < count]
    return lax.ppermute(array, "seq", pairs)


def from_others(part, sign):
    return [shifted(part, sign * step) for step in range(1, lax.axis_size("seq"))]


def out_kernel(count, sw, place_ref, *refs):
    tops, lows, ws = refs[:count], refs[count : 2 * count], refs[2 * count : 3 * count]
    send_ref, keep_ref = refs[3 * count :]
    c = pl.program_id(0)
    half_chunks = pl.num_programs(0) // 2
    odd = place_ref[1] == 1

    def product(parts):
        total = None
        for part, w in zip(parts, ws):
            one = mm(part[...], w[...])
            total = one if total is None else total + one
        first, second = total[:, :sw], total[:, sw:]
        send_ref[...] = jnp.where(odd, first, second).astype(BF)
        keep_ref[...] = jnp.where(odd, second, first)

    @pl.when(c < half_chunks)
    def _():
        product(tops)

    @pl.when(c >= half_chunks)
    def _():
        product(lows)


def out_part(place, tops, lows, ws):
    count = len(ws)
    rows = 2 * CH * (lows[0][1] // CH)
    wide = tops[0][0].shape[1]
    sw = ws[1].shape[1] // 2
    part = rows // (2 * CH)
    row = pl.BlockSpec((CH, sw), lambda c, place: (c, 0))
    operands, specs = [], []
    for array, start in tops:
        operands.append(array)
        specs.append(
            pl.BlockSpec((CH, wide), lambda c, place, s=start // CH: (s + jnp.minimum(c, part - 1), 0))
        )
    for array, start in lows:
        operands.append(array)
        specs.append(
            pl.BlockSpec((CH, wide), lambda c, place, s=start // CH: (s + jnp.maximum(c - part, 0), 0))
        )
    return pl.pallas_call(
        functools.partial(out_kernel, count, sw),
        grid_spec=pltpu.PrefetchScalarGridSpec(
            num_scalar_prefetch=1,
            grid=(rows // CH,),
            in_specs=specs
            + [pl.BlockSpec((wide, 2 * sw), lambda c, place: (0, place[0]))]
            + [pl.BlockSpec((wide, 2 * sw), lambda c, place: (0, 0))] * (count - 1),
            out_specs=[row, row],
        ),
        out_shape=[jax.ShapeDtypeStruct((rows, sw), BF), jax.ShapeDtypeStruct((rows, sw), F32)],
        compiler_params=params(),
        cost_estimate=cost(16 << 30),
        name="out_part",
    )(place, *operands, *map(stay, ws))


def complete_kernel(dp_ref, last_ref, after_ref, cw_ref, low_ref):
    half = low_ref.shape[0]
    low_ref[...] = dp_ref[half:, :]
    row = lax.broadcasted_iota(jnp.int32, last_ref.shape, 0)
    a0, a1 = after_ref[0:1], after_ref[1:2]
    one = cw_ref[2:3] * a0
    two = cw_ref[1:2] * a0 + cw_ref[2:3] * a1
    tail = last_ref[...] + jnp.where(row == 14, one, 0.0) + jnp.where(row == 15, two, 0.0)
    low_ref[half - 16 :, :] = tail.astype(BF)


def complete(dp, last, after, conv_w):
    rows, width = dp.shape
    return pl.pallas_call(
        complete_kernel,
        in_specs=[KEPT] * 4,
        out_specs=KEPT,
        out_shape=kept((rows // 2, width), BF),
        compiler_params=pltpu.CompilerParams(vmem_limit_bytes=VMEM),
        cost_estimate=LIGHT,
        name="complete",
    )(keep(dp), keep(last), after, conv_w)


def grad_kernel(count, low_first, place_ref, dp_ref, other_ref, w_ref, w_other_ref, send_ref, keep_ref, both):
    r = pl.program_id(0)
    half, sw = send_ref.shape[1:]
    width = w_ref.shape[1]

    @pl.when(r == 0)
    def _():
        both[:, :width] = dp_ref[...]
        both[:, width:] = other_ref[...]

    block = 2 * lax.bitwise_xor(place_ref[0], r) + place_ref[1]
    w = w_ref[pl.ds(pl.multiple_of(block * sw, sw), sw), :]
    total = mm_nt(both[...], jnp.concatenate([w, w_other_ref[r]], 1)).astype(BF)
    part = count // 2
    leaves = (r % 2 == 1) if low_first else (r >= part)

    @pl.when(leaves)
    def _():
        send_ref[r // 2 if low_first else r - part] = total

    @pl.when(jnp.logical_not(leaves))
    def _():
        keep_ref[r // 2 if low_first else r] = total


def grad_part(place, dp, other, w_in, w_other, low_first):
    half, width = dp.shape
    count, sw = w_other.shape[:2]
    return pl.pallas_call(
        functools.partial(grad_kernel, count, low_first),
        grid_spec=pltpu.PrefetchScalarGridSpec(
            num_scalar_prefetch=1,
            grid=(count,),
            in_specs=[KEPT] * 4,
            out_specs=[KEPT] * 2,
            scratch_shapes=[pltpu.VMEM((half, 2 * width), BF)],
        ),
        out_shape=[kept((count // 2, half, sw), BF)] * 2,
        compiler_params=params(),
        cost_estimate=LIGHT,
        name="grad_part",
    )(place, *map(keep, (dp, other, w_in, w_other)))


def halves_kernel(x_ref, y_ref, x_top_ref, y_low_ref):
    half = x_top_ref.shape[0]
    x_top_ref[...] = x_ref[:half, :]
    y_low_ref[...] = y_ref[half:, :]


def halves(x_got, y_got):
    rows, wide = x_got.shape
    return pl.pallas_call(
        halves_kernel,
        in_specs=[KEPT] * 2,
        out_specs=[KEPT] * 2,
        out_shape=[kept((rows // 2, wide), BF)] * 2,
        compiler_params=pltpu.CompilerParams(vmem_limit_bytes=VMEM),
        cost_estimate=LIGHT,
        name="halves",
    )(keep(x_got), keep(y_got))


def swapped(array, distance):
    count = lax.axis_size("tp")
    return lax.ppermute(array, "tp", [(i, i ^ distance) for i in range(count)])


def summed(a, b):
    return a.astype(F32) + b.astype(F32)


def passing_kernel(first, stride, keep_ref, got_ref, out_ref):
    for i in range(out_ref.shape[0]):
        out_ref[i] = summed(keep_ref[first + stride * i], got_ref[first + stride * i]).astype(BF)


def passing(kept_sum, got, first, stride):
    left, half, sw = got.shape
    return pl.pallas_call(
        functools.partial(passing_kernel, first, stride),
        in_specs=[KEPT] * 2,
        out_specs=KEPT,
        out_shape=kept((left // 2, half, sw), BF),
        compiler_params=pltpu.CompilerParams(vmem_limit_bytes=VMEM),
        cost_estimate=LIGHT,
        name="passing",
    )(keep(kept_sum), keep(got))


def reduce_both(a_send, a_keep, b_send, b_keep, a_own, b_own, meanwhile):
    pairs = lax.axis_size("tp") // 2
    a_step, b_step = 1, pairs // 2
    while True:
        a_got = swapped(a_send, 2 * a_step)
        b_got = swapped(b_send, 2 * b_step)
        left = a_keep.shape[0]
        a_keep, b_keep = meanwhile(a_keep, b_keep)
        if left == 1:
            return a_keep[0], a_got[0], b_keep[0], b_got[0]
        a_send = passing(a_keep, a_got, 1, 2)
        b_send = passing(b_keep, b_got, left // 2, 1)
        a_keep = summed(a_keep[0::2], a_got[0::2])
        b_keep = summed(b_keep[: left // 2], b_got[: left // 2])
        if left == 2:
            a_keep = a_keep + a_own
            b_keep = b_keep + b_own
        a_step, b_step = a_step * 2, b_step // 2


def finish_kernel(half, ak_ref, ag_ref, bk_ref, bg_ref, out_ref):
    out_ref[:half, :] = (ak_ref[...] + ag_ref[...].astype(F32)).astype(BF)
    out_ref[half:, :] = (bk_ref[...] + bg_ref[...].astype(F32)).astype(BF)


def finish(a_keep, a_got, b_keep, b_got):
    half, sw = a_keep.shape
    return pl.pallas_call(
        functools.partial(finish_kernel, half),
        out_shape=jax.ShapeDtypeStruct((2 * half, sw), BF),
        compiler_params=pltpu.CompilerParams(vmem_limit_bytes=VMEM),
        cost_estimate=LIGHT,
        name="finish",
    )(a_keep, a_got, b_keep, b_got)


def per_device(inputs, cotangent, w_in, conv_w, norm_gain, w_out, keep_flags):
    heads = keep_flags.shape[0]
    sel, bias = selectors(heads)
    tp = lax.axis_size("tp")
    pairs = tp // 2
    me = lax.axis_index("tp")
    pair = me // 2
    place = jnp.stack([pair, me % 2]).astype(jnp.int32)
    slice_width = inputs.shape[1] // tp
    column = me * slice_width
    gain = (norm_gain.reshape(heads, DV) * keep_flags.astype(F32)[:, None]).reshape(1, heads * DV)

    half = inputs.shape[0] // 2
    tail, w_other, *near = columns(place, w_out, (1, 2), pairs, inputs, w_in)
    w_other = swapped(w_other, 1)
    halo = shifted(tail, 1)
    near = [swapped(one, 2 * m) for m, one in enumerate(near, 1)]
    far = columns(place, w_out, range(3, pairs), pairs)
    halo, place, gain, far = lax.optimization_barrier((halo, place, gain, far))
    v, pq, pk, fq, fk, loc, state = project(inputs, halo, w_in, conv_w, sel, bias, heads)
    state, w_other = lax.optimization_barrier((state, w_other))
    before = from_others(state, 1)
    v, near, far = lax.optimization_barrier((v, near, far))
    far = [swapped(one, 2 * m) for m, one in enumerate(far, 3)]
    g, num, wt, slope = local_part(cotangent, w_out, gain, v, pq, pk, loc, fq, fk, sel, heads)
    ho, dn, gloc, pre, gstate = norm_part(
        g, num, gain, pq, before, (v, pk, fq, fk, wt, slope, loc, sel), heads
    )
    step = pairs // 2
    got = {r: swapped(ho, 2 * r) for r in range(1, pairs) if r != 1 + step}
    later = from_others(gstate, -1)
    pre, far = lax.optimization_barrier((pre, far))
    dqk, dv, xk = inner_part(v, pq, pk, fq, wt, slope, dn, loc, pre, sel, fk, gloc, heads)
    dp_top, dp, first, last = outer_part(v, pk, fk, dqk, dv, xk, gloc, later, sel, conv_w, heads)
    other_top = swapped(dp_top, 1)
    dp_low = complete(dp, last, shifted(first, -1), conv_w)
    other_low = swapped(dp_low, 1)
    x_top, y_low = halves(got[1], got[step])
    x_top, y_low = swapped(x_top, 2 * step), swapped(y_low, 2)
    a_send, a_keep = grad_part(place, dp_top, other_top, w_in, w_other, True)
    b_send, b_keep = grad_part(place, dp_low, other_low, w_in, w_other, False)
    tops = [(ho, 0)] + [(got.get(r, x_top), 0) for r in range(1, pairs)]
    lows = [(ho, half)] + [(got[r], half) if r in got else (y_low, 0) for r in range(1, pairs)]
    w_cols = [w_out] + near + far
    x_own = lax.dynamic_slice_in_dim(inputs, column, slice_width, 1).astype(F32)
    c_own = lax.dynamic_slice_in_dim(cotangent, column, slice_width, 1).astype(F32)
    stage = []

    def meanwhile(a, b):
        if not stage:
            out_send, out_keep = out_part(place, tops, lows, w_cols)
            stage.append(x_own + out_keep)
            stage.append(out_send)
            a, b, stage[1] = lax.optimization_barrier((a, b, stage[1]))
            stage.append(swapped(stage[1], 1))
        elif len(stage) == 3:
            stage.append((stage[0] + stage[2].astype(F32)).astype(BF))
            a, b, stage[3] = lax.optimization_barrier((a, b, stage[3]))
        return a, b

    sums = reduce_both(a_send, a_keep, b_send, b_keep, c_own[None, :half], c_own[None, half:], meanwhile)
    return stage[3], finish(*sums)


def solution(mesh):
    placed = (
        P("seq", None),
        P("seq", None),
        P(None, "tp"),
        P(None, "tp"),
        P("tp"),
        P("tp", None),
        P("tp"),
    )
    return jax.shard_map(
        per_device,
        mesh=mesh,
        in_specs=placed,
        out_specs=(P("seq", "tp"), P("seq", "tp")),
        check_vma=False,
    )
```

```python
import functools

import jax
import jax.numpy as jnp
import numpy as np
from jax import lax
from jax.experimental import pallas as pl
from jax.experimental.pallas import tpu as pltpu
from jax.sharding import PartitionSpec as P

FEAT = 16
DV = 128
HW = 2 * FEAT + DV
EP = 256
ES = 160
CH = 256
EPS = 1e-06
BF = jnp.bfloat16
F32 = jnp.float32
MIB = 1024 * 1024


def mm(a, b):
    return lax.dot_general(a, b, (((1,), (0,)), ((), ())), preferred_element_type=F32)


def mm_nt(a, b):
    return lax.dot_general(a, b, (((1,), (1,)), ((), ())), preferred_element_type=F32)


def mm_tn(a, b):
    return lax.dot_general(a, b, (((0,), (0,)), ((), ())), preferred_element_type=F32)


def selectors(heads):
    sel = np.zeros((heads, 128, 4 * EP), np.float32)
    bias = np.zeros((8, EP), np.float32)
    bias[1, :FEAT] = 1.0
    bias[0, FEAT] = bias[1, FEAT] = 1.0
    for h in range(heads):
        q0 = (HW * h) % 128
        k0 = q0 + FEAT
        for i in range(FEAT):
            sel[h, q0 + i, i] = 0.5
            sel[h, k0 + i, 2 * EP + i] = 0.5
        col = FEAT + 1
        for i in range(FEAT):
            for j in range(i, FEAT):
                sel[h, q0 + i, col] = 0.25 if i == j else 0.5
                sel[h, q0 + j, EP + col] = 0.5
                sel[h, k0 + i, 2 * EP + col] = 0.5
                sel[h, k0 + j, 3 * EP + col] = 0.5
                col += 1
    return jnp.asarray(sel, BF), jnp.asarray(bias, F32)


def window(h):
    t = (HW * h) // 128
    return slice(128 * t, 128 * t + 128)


def value_place(h):
    start = HW * h + 2 * FEAT
    return start // 128, start % 128


def lane_iota():
    return lax.broadcasted_iota(jnp.int32, (CH, 128), 1)


def take_values(conv, h):
    tile, off = value_place(h)
    first = conv[:, 128 * tile : 128 * tile + 128]
    if off == 0:
        return first
    second = conv[:, 128 * tile + 128 : min(128 * tile + 256, conv.shape[1])]
    if second.shape[1] < 128:
        second = jnp.concatenate([second, jnp.zeros((CH, 128 - second.shape[1]), second.dtype)], 1)
    a = pltpu.roll(first, 128 - off, 1)
    b = pltpu.roll(second, 128 - off, 1)
    return jnp.where(lane_iota() < 128 - off, a, b)


def causal():
    r = lax.broadcasted_iota(jnp.int32, (CH, CH), 0)
    c = lax.broadcasted_iota(jnp.int32, (CH, CH), 1)
    return r >= c


def params(mib):
    return pltpu.CompilerParams(dimension_semantics=("arbitrary",), vmem_limit_bytes=mib * MIB)


def whole(shape):
    return pl.BlockSpec(shape, lambda c, *_: (0,) * len(shape))


KEPT = pl.BlockSpec(memory_space=pltpu.VMEM)


def kept(shape, dtype):
    return pltpu.VMEM(shape, dtype)


def keep(array):
    return pltpu.with_memory_space_constraint(array, pltpu.VMEM)


def stay(array):
    return pltpu.with_memory_space_constraint(array, pltpu.HBM)


def cost(flops):
    return pl.CostEstimate(flops=int(flops), bytes_accessed=1 << 20, transcendentals=0)


LIGHT = cost(1000)


def rows_at(c):
    return pl.ds(pl.multiple_of(c * CH, CH), CH)


def biased(u, bias):
    return jnp.concatenate([u[:, :128] + bias[:, :128], u[:, 128:]], 1)


def project_kernel(heads, x_ref, halo_ref, w_ref, cw_ref, sel_ref, bias_ref,
                   v_ref, pq_ref, pk_ref, fq_ref, fk_ref, loc_ref, state_ref, ext, run):
    c = pl.program_id(0)
    at = rows_at(c)

    @pl.when(c == 0)
    def _():
        before = mm(halo_ref[...], w_ref[...]).astype(BF).astype(F32)
        ext[0:8, :] = before[8:16]
        run[...] = jnp.zeros_like(run)

    ext[8:, :] = mm(x_ref[...], w_ref[...]).astype(BF).astype(F32)
    conv = (cw_ref[0:1] * ext[8 : 8 + CH, :] + cw_ref[1:2] * ext[7 : 7 + CH, :]
            + cw_ref[2:3] * ext[6 : 6 + CH, :])
    ext[0:8, :] = ext[CH : CH + 8, :]
    conv_b = conv.astype(BF)
    conv = conv_b.astype(F32)
    b0 = bias_ref[0:1]
    b1 = bias_ref[1:2]
    for h in range(heads):
        u = mm(conv_b[:, window(h)], sel_ref[h])
        first, second = biased(u[:, :EP], b0), biased(u[:, EP : 2 * EP], b1)
        pq_ref[h, at, :] = (first * second).astype(BF)
        fq_ref[h, at, :EP] = first.astype(BF)
        fq_ref[h, at, EP:] = second.astype(BF)
        first, second = biased(u[:, 2 * EP : 3 * EP], b0), biased(u[:, 3 * EP :], b1)
        pk = (first * second).astype(BF)
        pk_ref[h, at, :] = pk
        fk_ref[h, at, :EP] = first.astype(BF)
        fk_ref[h, at, EP:] = second.astype(BF)
        v = take_values(conv, h).astype(BF)
        v_ref[at, DV * h : DV * h + DV] = v
        loc_ref[c, h] = run[h].astype(BF)
        run[h] = run[h] + mm_tn(v, pk)

    @pl.when(c == pl.num_programs(0) - 1)
    def _():
        for h in range(heads):
            state_ref[h] = run[h].T[:ES].astype(BF)


def project(x, halo, w_in, conv_w, sel, bias, heads):
    rows, d = x.shape
    width = w_in.shape[1]
    n = rows // CH
    return pl.pallas_call(
        functools.partial(project_kernel, heads),
        grid=(n,),
        in_specs=[
            pl.BlockSpec((CH, d), lambda c: (c, 0)),
            whole((16, d)),
            KEPT,
            whole((3, width)),
            KEPT,
            whole(bias.shape),
        ],
        out_specs=[KEPT] * 6 + [whole((heads, ES, DV))],
        out_shape=[
            kept((rows, heads * DV), BF),
            kept((heads, rows, EP), BF),
            kept((heads, rows, EP), BF),
            kept((heads, rows, 2 * EP), BF),
            kept((heads, rows, 2 * EP), BF),
            kept((n, heads, DV, EP), BF),
            jax.ShapeDtypeStruct((heads, ES, DV), BF),
        ],
        scratch_shapes=[pltpu.VMEM((CH + 8, width), F32), pltpu.VMEM((heads, DV, EP), F32)],
        compiler_params=params(12),
        cost_estimate=cost(100 << 30),
        name="project",
    )(stay(x), halo, keep(w_in), conv_w, keep(sel), bias)


def local_kernel(heads, ct_ref, wo_ref, gain_ref, v_ref, pq_ref, pk_ref, loc_ref, fq_ref, fk_ref, sel_ref,
                 g_ref, num_ref, wt_ref, slope_ref):
    c = pl.program_id(0)
    at = rows_at(c)
    g_ref[at, :] = mm_nt(ct_ref[...], wo_ref[...]) * gain_ref[...]
    mask = causal()
    for h in range(heads):
        pq = pq_ref[h, at, :]
        logits = mm_nt(pq[:, :FEAT], pk_ref[h, at, :FEAT])
        slope = 1.0 + logits
        weights = jnp.where(mask, 0.5 + 0.5 * slope * slope, 0.0).astype(BF)
        wt_ref[h, at, :] = weights
        slope_ref[h, at, :] = jnp.where(mask, slope, 0.0).astype(BF)
        lanes = slice(DV * h, DV * h + DV)
        num_ref[at, lanes] = mm(weights, v_ref[at, lanes]) + mm_nt(pq, loc_ref[c, h])


def local_part(ct, w_out, gain, v, pq, pk, loc, fq, fk, sel, heads):
    rows, d = ct.shape
    n = rows // CH
    wide = heads * DV
    return pl.pallas_call(
        functools.partial(local_kernel, heads),
        grid=(n,),
        in_specs=[pl.BlockSpec((CH, d), lambda c: (c, 0)), KEPT, whole((1, wide))] + [KEPT] * 7,
        out_specs=[KEPT] * 4,
        out_shape=[kept((rows, wide), F32)] * 2 + [kept((heads, rows, CH), BF)] * 2,
        compiler_params=params(12),
        cost_estimate=LIGHT,
        name="local_part",
    )(stay(ct), keep(w_out), gain, *map(keep, (v, pq, pk, loc, fq, fk, sel)))


def norm_kernel(heads, parts, passed, g_ref, num_ref, gain_ref, pq_ref, ones_ref, *refs):
    got = refs[:parts]
    ho_ref, dn_ref, loc_ref, pre_ref, state_ref, run = refs[parts + passed :]
    step = pl.program_id(0)
    c = pl.num_programs(0) - 1 - step
    at = rows_at(c)

    @pl.when(step == 0)
    def _():
        run[...] = jnp.zeros_like(run)
        total = got[0][...].astype(F32)
        for one in got[1:]:
            total = total + one[...].astype(F32)
        pre_ref[...] = total.astype(BF)

    for h in range(0, heads, 2):
        lanes = slice(DV * h, DV * h + 2 * DV)
        pqs = [pq_ref[h, at, :], pq_ref[h + 1, at, :]]
        num = num_ref[at, lanes] + jnp.concatenate(
            [mm(pqs[0][:, :ES], pre_ref[h]), mm(pqs[1][:, :ES], pre_ref[h + 1])], 1
        )
        inv = lax.rsqrt(mm((num * num).astype(BF), ones_ref[...]) + EPS)
        normed = num * inv
        ho_ref[at, lanes] = (normed * gain_ref[:, lanes]).astype(BF)
        g = g_ref[at, lanes]
        dn = ((g - normed * mm((g * normed).astype(BF), ones_ref[...])) * inv).astype(BF)
        dn_ref[at, lanes] = dn
        for i in range(2):
            loc_ref[c, h + i] = run[h + i].astype(BF)
            run[h + i] = run[h + i] + mm_tn(dn[:, DV * i : DV * i + DV], pqs[i])

    @pl.when(step == pl.num_programs(0) - 1)
    def _():
        for h in range(heads):
            state_ref[h] = run[h].T[:ES].astype(BF)


def norm_part(g, num, gain, pq, got, later, heads):
    ones = jnp.asarray(np.kron(np.eye(2), np.full((DV, DV), 1.0 / DV)), BF)
    rows, wide = g.shape
    n = rows // CH
    return pl.pallas_call(
        functools.partial(norm_kernel, heads, len(got), len(later)),
        grid=(n,),
        in_specs=[KEPT, KEPT, whole((1, wide)), KEPT, whole((2 * DV, 2 * DV))]
        + [whole((heads, ES, DV))] * len(got)
        + [KEPT] * len(later),
        out_specs=[KEPT] * 4 + [whole((heads, ES, DV))],
        out_shape=[
            kept((rows, wide), BF),
            kept((rows, wide), BF),
            kept((n, heads, DV, EP), BF),
            kept((heads, ES, DV), BF),
            jax.ShapeDtypeStruct((heads, ES, DV), BF),
        ],
        scratch_shapes=[pltpu.VMEM((heads, DV, EP), F32)],
        compiler_params=params(8),
        cost_estimate=cost(16 << 30),
        name="norm_part",
    )(keep(g), keep(num), gain, keep(pq), ones, *got, *map(keep, later))


def inner_kernel(heads, v_ref, pq_ref, pk_ref, fq_ref, wt_ref, slope_ref, dn_ref, loc_ref, pre_ref, sel_ref,
                 fk_ref, gloc_ref, dqk_ref, dv_ref, xk_ref, pre_t):
    c = pl.program_id(0)
    at = rows_at(c)

    @pl.when(c == 0)
    def _():
        pre_t[...] = jnp.zeros_like(pre_t)
        for h in range(heads):
            pre_t[h, :, :ES] = pre_ref[h].astype(F32).T

    linear = lane_iota() < FEAT
    dqk = None
    for h in range(heads):
        lanes = slice(DV * h, DV * h + DV)
        dn = dn_ref[at, lanes]
        dv_ref[at, lanes] = mm_tn(wt_ref[h, at, :], dn)
        dl = (mm_nt(dn, v_ref[at, lanes]) * slope_ref[h, at, :].astype(F32)).astype(BF)
        xk_ref[h, at, :] = mm_tn(dl, pq_ref[h, at, :128])
        state = (loc_ref[c, h].astype(F32) + pre_t[h]).astype(BF)
        dphi = mm(dn, state)
        dphi = jnp.concatenate(
            [dphi[:, :128] + jnp.where(linear, mm(dl, pk_ref[h, at, :128]), 0.0), dphi[:, 128:]], 1
        )
        da = (dphi * fq_ref[h, at, EP:].astype(F32)).astype(BF)
        db = (dphi * fq_ref[h, at, :EP].astype(F32)).astype(BF)
        part = mm_nt(da, sel_ref[h, :, :EP]) + mm_nt(db, sel_ref[h, :, EP : 2 * EP])
        dqk = part if dqk is None else dqk + part
    dqk_ref[at, :] = dqk


def inner_part(v, pq, pk, fq, wt, slope, dn, loc, pre, sel, fk, gloc, heads):
    rows = v.shape[0]
    n = rows // CH
    return pl.pallas_call(
        functools.partial(inner_kernel, heads),
        grid=(n,),
        in_specs=[KEPT] * 12,
        out_specs=[KEPT] * 3,
        out_shape=[
            kept((rows, 128), F32),
            kept((rows, heads * DV), F32),
            kept((heads, rows, 128), F32),
        ],
        scratch_shapes=[pltpu.VMEM((heads, DV, EP), F32)],
        compiler_params=params(8),
        cost_estimate=LIGHT,
        name="inner_part",
    )(*map(keep, (v, pq, pk, fq, wt, slope, dn, loc, pre, sel, fk, gloc)))


def outer_kernel(heads, parts, v_ref, pk_ref, fk_ref, dqk_ref, dv_ref, xk_ref, loc_ref, sel_ref, cw_ref, *refs):
    got = refs[:parts]
    top_ref, dp_ref, first_ref, last_ref, ext, suf_t = refs[parts:]
    half_chunks = pl.num_programs(0) // 2
    step = pl.program_id(0)
    c = pl.num_programs(0) - 1 - step
    at = rows_at(c)
    width = cw_ref.shape[1]

    @pl.when(step == 0)
    def _():
        suf_t[...] = jnp.zeros_like(suf_t)
        for h in range(heads):
            total = got[0][h].astype(F32)
            for one in got[1:]:
                total = total + one[h].astype(F32)
            suf_t[h, :, :ES] = total.T
        ext[CH:, :] = jnp.zeros((8, width), F32)

    lane = lane_iota()
    tiles = [None] * (-(-width // 128))

    def put(t, piece):
        tiles[t] = piece if tiles[t] is None else tiles[t] + piece

    dqk = dqk_ref[at, :]
    for h in range(heads):
        lanes = slice(DV * h, DV * h + DV)
        state = (loc_ref[c, h].astype(F32) + suf_t[h]).astype(BF)
        dphi = mm(v_ref[at, lanes], state)
        dphi = jnp.concatenate(
            [dphi[:, :128] + jnp.where(lane < FEAT, xk_ref[h, at, :], 0.0), dphi[:, 128:]], 1
        )
        da = (dphi * fk_ref[h, at, EP:].astype(F32)).astype(BF)
        db = (dphi * fk_ref[h, at, :EP].astype(F32)).astype(BF)
        own = (
            dqk
            + mm_nt(da, sel_ref[h, :, 2 * EP : 3 * EP])
            + mm_nt(db, sel_ref[h, :, 3 * EP : 4 * EP])
        )
        q0 = (HW * h) % 128
        put((HW * h) // 128, jnp.where((lane >= q0) & (lane < q0 + 2 * FEAT), own, 0.0))
        dv = dv_ref[at, lanes] + mm_nt(pk_ref[h, at, :], state)
        tile, off = value_place(h)
        if off == 0:
            put(tile, dv)
        else:
            moved = pltpu.roll(dv, off, 1)
            put(tile, jnp.where(lane >= off, moved, 0.0))
            put(tile + 1, jnp.where(lane < off, moved, 0.0))
    for t, tile in enumerate(tiles):
        end = min(128 * t + 128, width)
        ext[:CH, 128 * t : end] = tile[:, : end - 128 * t]
    dp = (cw_ref[0:1] * ext[:CH, :] + cw_ref[1:2] * ext[1 : CH + 1, :]
          + cw_ref[2:3] * ext[2 : CH + 2, :])
    dp_ref[at, :] = dp.astype(BF)

    @pl.when(c < half_chunks)
    def _():
        top_ref[at, :] = dp.astype(BF)

    @pl.when(step == 0)
    def _():
        last_ref[...] = dp[CH - 16 :]

    ext[CH:, :] = ext[0:8, :]
    first_ref[...] = ext[0:8, :]


def outer_part(v, pk, fk, dqk, dv, xk, loc, got, sel, conv_w, heads):
    rows, width = v.shape[0], conv_w.shape[1]
    n = rows // CH
    return pl.pallas_call(
        functools.partial(outer_kernel, heads, len(got)),
        grid=(n,),
        in_specs=[KEPT] * 8 + [whole((3, width))] + [whole((heads, ES, DV))] * len(got),
        out_specs=[KEPT, KEPT, whole((8, width)), KEPT],
        out_shape=[
            kept((rows // 2, width), BF),
            kept((rows, width), BF),
            jax.ShapeDtypeStruct((8, width), F32),
            kept((16, width), F32),
        ],
        scratch_shapes=[pltpu.VMEM((CH + 8, width), F32), pltpu.VMEM((heads, DV, EP), F32)],
        compiler_params=params(8),
        cost_estimate=cost(16 << 30),
        name="outer_part",
    )(*map(keep, (v, pk, fk, dqk, dv, xk, loc, sel)), conv_w, *got)


def columns_kernel(which, place_ref, w_ref, *refs):
    outs, sems = refs[-1 - len(which) : -1], refs[-1]
    wide = outs[0].shape[1]
    copies = []
    for i, m in enumerate(which):
        start = pl.multiple_of(lax.bitwise_xor(place_ref[0], m) * wide, wide)
        copies.append(pltpu.make_async_copy(w_ref.at[:, pl.ds(start, wide)], outs[i], sems.at[i]))
    if len(refs) > len(which) + 1:
        x_ref, wi_ref, tail_ref, wi_out_ref = refs[:4]
        rows = tail_ref.shape[0]
        copies.append(
            pltpu.make_async_copy(x_ref.at[pl.ds(x_ref.shape[0] - rows, rows), :], tail_ref, sems.at[len(which)])
        )
        count, sw = wi_out_ref.shape[:2]
        for r in range(count):
            block = 2 * lax.bitwise_xor(place_ref[0], r) + 1 - place_ref[1]
            copies.append(
                pltpu.make_async_copy(
                    wi_ref.at[pl.ds(pl.multiple_of(block * sw, sw), sw), :],
                    wi_out_ref.at[r],
                    sems.at[len(which) + 1 + r],
                )
            )
    for copy in copies:
        copy.start()
    for copy in copies:
        copy.wait()


def columns(place, w_out, which, count, x=None, w_in=None):
    rows, d = w_out.shape
    anywhere = pl.BlockSpec(memory_space=pltpu.HBM)
    out_shape = [jax.ShapeDtypeStruct((rows, d // count), w_out.dtype)] * len(which)
    args = [stay(w_out)]
    if x is not None:
        args += [stay(x), stay(w_in)]
        out_shape = [
            jax.ShapeDtypeStruct((16, x.shape[1]), x.dtype),
            jax.ShapeDtypeStruct((count, w_in.shape[0] // (2 * count), w_in.shape[1]), w_in.dtype),
        ] + out_shape
    return pl.pallas_call(
        functools.partial(columns_kernel, which),
        grid_spec=pltpu.PrefetchScalarGridSpec(
            num_scalar_prefetch=1,
            grid=(1,),
            in_specs=[anywhere] * len(args),
            out_specs=[anywhere] * len(out_shape),
            scratch_shapes=[pltpu.SemaphoreType.DMA((len(which) + 1 + count,))],
        ),
        out_shape=out_shape,
        compiler_params=pltpu.CompilerParams(vmem_limit_bytes=4 * MIB),
        cost_estimate=LIGHT,
        name="columns",
    )(place, *args)


def shifted(array, by):
    count = lax.axis_size("seq")
    pairs = [(i, i + by) for i in range(count) if 0 <= i + by < count]
    return lax.ppermute(array, "seq", pairs)


def from_others(part, sign):
    return [shifted(part, sign * step) for step in range(1, lax.axis_size("seq"))]


def out_kernel(count, sw, place_ref, *refs):
    tops, lows, ws = refs[:count], refs[count : 2 * count], refs[2 * count : 3 * count]
    send_ref, keep_ref = refs[3 * count :]
    c = pl.program_id(0)
    half_chunks = pl.num_programs(0) // 2
    odd = place_ref[1] == 1

    def product(parts):
        total = None
        for part, w in zip(parts, ws):
            one = mm(part[...], w[...])
            total = one if total is None else total + one
        first, second = total[:, :sw], total[:, sw:]
        send_ref[...] = jnp.where(odd, first, second).astype(BF)
        keep_ref[...] = jnp.where(odd, second, first)

    @pl.when(c < half_chunks)
    def _():
        product(tops)

    @pl.when(c >= half_chunks)
    def _():
        product(lows)


def out_part(place, tops, lows, ws):
    count = len(ws)
    rows = 2 * CH * (lows[0][1] // CH)
    wide = tops[0][0].shape[1]
    sw = ws[1].shape[1] // 2
    part = rows // (2 * CH)
    row = pl.BlockSpec((CH, sw), lambda c, place: (c, 0))
    operands, specs = [], []
    for array, start in tops:
        operands.append(array)
        specs.append(
            pl.BlockSpec((CH, wide), lambda c, place, s=start // CH: (s + jnp.minimum(c, part - 1), 0))
        )
    for array, start in lows:
        operands.append(array)
        specs.append(
            pl.BlockSpec((CH, wide), lambda c, place, s=start // CH: (s + jnp.maximum(c - part, 0), 0))
        )
    return pl.pallas_call(
        functools.partial(out_kernel, count, sw),
        grid_spec=pltpu.PrefetchScalarGridSpec(
            num_scalar_prefetch=1,
            grid=(rows // CH,),
            in_specs=specs
            + [pl.BlockSpec((wide, 2 * sw), lambda c, place: (0, place[0]))]
            + [pl.BlockSpec((wide, 2 * sw), lambda c, place: (0, 0))] * (count - 1),
            out_specs=[row, row],
        ),
        out_shape=[jax.ShapeDtypeStruct((rows, sw), BF), jax.ShapeDtypeStruct((rows, sw), F32)],
        compiler_params=params(16),
        cost_estimate=cost(16 << 30),
        name="out_part",
    )(place, *operands, *map(stay, ws))


def complete_kernel(dp_ref, last_ref, after_ref, cw_ref, low_ref):
    half = low_ref.shape[0]
    low_ref[...] = dp_ref[half:, :]
    row = lax.broadcasted_iota(jnp.int32, last_ref.shape, 0)
    a0, a1 = after_ref[0:1], after_ref[1:2]
    one = cw_ref[2:3] * a0
    two = cw_ref[1:2] * a0 + cw_ref[2:3] * a1
    tail = last_ref[...] + jnp.where(row == 14, one, 0.0) + jnp.where(row == 15, two, 0.0)
    low_ref[half - 16 :, :] = tail.astype(BF)


def complete(dp, last, after, conv_w):
    rows, width = dp.shape
    return pl.pallas_call(
        complete_kernel,
        in_specs=[KEPT] * 4,
        out_specs=KEPT,
        out_shape=kept((rows // 2, width), BF),
        compiler_params=pltpu.CompilerParams(vmem_limit_bytes=4 * MIB),
        cost_estimate=LIGHT,
        name="complete",
    )(keep(dp), keep(last), after, conv_w)


def grad_kernel(count, low_first, place_ref, dp_ref, other_ref, w_ref, w_other_ref, send_ref, keep_ref, both):
    r = pl.program_id(0)
    half, sw = send_ref.shape[1:]
    width = w_ref.shape[1]

    @pl.when(r == 0)
    def _():
        both[:, :width] = dp_ref[...]
        both[:, width:] = other_ref[...]

    block = 2 * lax.bitwise_xor(place_ref[0], r) + place_ref[1]
    w = w_ref[pl.ds(pl.multiple_of(block * sw, sw), sw), :]
    total = mm_nt(both[...], jnp.concatenate([w, w_other_ref[r]], 1)).astype(BF)
    part = count // 2
    leaves = (r % 2 == 1) if low_first else (r >= part)

    @pl.when(leaves)
    def _():
        send_ref[r // 2 if low_first else r - part] = total

    @pl.when(jnp.logical_not(leaves))
    def _():
        keep_ref[r // 2 if low_first else r] = total


def grad_part(place, dp, other, w_in, w_other, low_first):
    half, width = dp.shape
    count, sw = w_other.shape[:2]
    return pl.pallas_call(
        functools.partial(grad_kernel, count, low_first),
        grid_spec=pltpu.PrefetchScalarGridSpec(
            num_scalar_prefetch=1,
            grid=(count,),
            in_specs=[KEPT] * 4,
            out_specs=[KEPT] * 2,
            scratch_shapes=[pltpu.VMEM((half, 2 * width), BF)],
        ),
        out_shape=[kept((count // 2, half, sw), BF)] * 2,
        compiler_params=params(8),
        cost_estimate=LIGHT,
        name="grad_part",
    )(place, *map(keep, (dp, other, w_in, w_other)))


def halves_kernel(x_ref, y_ref, x_top_ref, y_low_ref):
    half = x_top_ref.shape[0]
    x_top_ref[...] = x_ref[:half, :]
    y_low_ref[...] = y_ref[half:, :]


def halves(x_got, y_got):
    rows, wide = x_got.shape
    return pl.pallas_call(
        halves_kernel,
        in_specs=[KEPT] * 2,
        out_specs=[KEPT] * 2,
        out_shape=[kept((rows // 2, wide), BF)] * 2,
        compiler_params=pltpu.CompilerParams(vmem_limit_bytes=4 * MIB),
        cost_estimate=LIGHT,
        name="halves",
    )(keep(x_got), keep(y_got))


def swapped(array, distance):
    count = lax.axis_size("tp")
    return lax.ppermute(array, "tp", [(i, i ^ distance) for i in range(count)])


def summed(a, b):
    return a.astype(F32) + b.astype(F32)


def passing_kernel(first, stride, keep_ref, got_ref, out_ref):
    for i in range(out_ref.shape[0]):
        out_ref[i] = summed(keep_ref[first + stride * i], got_ref[first + stride * i]).astype(BF)


def passing(kept_sum, got, first, stride):
    left, half, sw = got.shape
    return pl.pallas_call(
        functools.partial(passing_kernel, first, stride),
        in_specs=[KEPT] * 2,
        out_specs=KEPT,
        out_shape=kept((left // 2, half, sw), BF),
        compiler_params=pltpu.CompilerParams(vmem_limit_bytes=4 * MIB),
        cost_estimate=LIGHT,
        name="passing",
    )(keep(kept_sum), keep(got))


def reduce_both(a_send, a_keep, b_send, b_keep, a_own, b_own, meanwhile):
    pairs = lax.axis_size("tp") // 2
    a_step, b_step = 1, pairs // 2
    while True:
        a_got = swapped(a_send, 2 * a_step)
        b_got = swapped(b_send, 2 * b_step)
        left = a_keep.shape[0]
        a_keep, b_keep = meanwhile(a_keep, b_keep)
        if left == 1:
            return a_keep[0], a_got[0], b_keep[0], b_got[0]
        a_send = passing(a_keep, a_got, 1, 2)
        b_send = passing(b_keep, b_got, left // 2, 1)
        a_keep = summed(a_keep[0::2], a_got[0::2])
        b_keep = summed(b_keep[: left // 2], b_got[: left // 2])
        if left == 2:
            a_keep = a_keep + a_own
            b_keep = b_keep + b_own
        a_step, b_step = a_step * 2, b_step // 2


def finish_kernel(half, ak_ref, ag_ref, bk_ref, bg_ref, out_ref):
    out_ref[:half, :] = (ak_ref[...] + ag_ref[...].astype(F32)).astype(BF)
    out_ref[half:, :] = (bk_ref[...] + bg_ref[...].astype(F32)).astype(BF)


def finish(a_keep, a_got, b_keep, b_got):
    half, sw = a_keep.shape
    return pl.pallas_call(
        functools.partial(finish_kernel, half),
        out_shape=jax.ShapeDtypeStruct((2 * half, sw), BF),
        compiler_params=pltpu.CompilerParams(vmem_limit_bytes=4 * MIB),
        cost_estimate=LIGHT,
        name="finish",
    )(a_keep, a_got, b_keep, b_got)


def per_device(inputs, cotangent, w_in, conv_w, norm_gain, w_out, keep_flags):
    heads = keep_flags.shape[0]
    sel, bias = selectors(heads)
    tp = lax.axis_size("tp")
    pairs = tp // 2
    me = lax.axis_index("tp")
    pair = me // 2
    place = jnp.stack([pair, me % 2]).astype(jnp.int32)
    slice_width = inputs.shape[1] // tp
    column = me * slice_width
    gain = (norm_gain.reshape(heads, DV) * keep_flags.astype(F32)[:, None]).reshape(1, heads * DV)

    half = inputs.shape[0] // 2
    tail, w_other, *near = columns(place, w_out, (1, 2), pairs, inputs, w_in)
    w_other = swapped(w_other, 1)
    halo = shifted(tail, 1)
    near = [swapped(one, 2 * m) for m, one in enumerate(near, 1)]
    far = columns(place, w_out, range(3, pairs), pairs)
    halo, place, gain, far = lax.optimization_barrier((halo, place, gain, far))
    v, pq, pk, fq, fk, loc, state = project(inputs, halo, w_in, conv_w, sel, bias, heads)
    state, w_other = lax.optimization_barrier((state, w_other))
    before = from_others(state, 1)
    v, near, far = lax.optimization_barrier((v, near, far))
    far = [swapped(one, 2 * m) for m, one in enumerate(far, 3)]
    g, num, wt, slope = local_part(cotangent, w_out, gain, v, pq, pk, loc, fq, fk, sel, heads)
    ho, dn, gloc, pre, gstate = norm_part(
        g, num, gain, pq, before, (v, pk, fq, fk, wt, slope, loc, sel), heads
    )
    step = pairs // 2
    got = {r: swapped(ho, 2 * r) for r in range(1, pairs) if r != 1 + step}
    later = from_others(gstate, -1)
    pre, far = lax.optimization_barrier((pre, far))
    dqk, dv, xk = inner_part(v, pq, pk, fq, wt, slope, dn, loc, pre, sel, fk, gloc, heads)
    dp_top, dp, first, last = outer_part(v, pk, fk, dqk, dv, xk, gloc, later, sel, conv_w, heads)
    other_top = swapped(dp_top, 1)
    dp_low = complete(dp, last, shifted(first, -1), conv_w)
    other_low = swapped(dp_low, 1)
    x_top, y_low = halves(got[1], got[step])
    x_top, y_low = swapped(x_top, 2 * step), swapped(y_low, 2)
    a_send, a_keep = grad_part(place, dp_top, other_top, w_in, w_other, True)
    b_send, b_keep = grad_part(place, dp_low, other_low, w_in, w_other, False)
    tops = [(ho, 0)] + [(got.get(r, x_top), 0) for r in range(1, pairs)]
    lows = [(ho, half)] + [(got[r], half) if r in got else (y_low, 0) for r in range(1, pairs)]
    w_cols = [w_out] + near + far
    x_own = lax.dynamic_slice_in_dim(inputs, column, slice_width, 1).astype(F32)
    c_own = lax.dynamic_slice_in_dim(cotangent, column, slice_width, 1).astype(F32)
    stage = []

    def meanwhile(a, b):
        if not stage:
            out_send, out_keep = out_part(place, tops, lows, w_cols)
            stage.append(x_own + out_keep)
            stage.append(out_send)
            a, b, stage[1] = lax.optimization_barrier((a, b, stage[1]))
            stage.append(swapped(stage[1], 1))
        elif len(stage) == 3:
            stage.append((stage[0] + stage[2].astype(F32)).astype(BF))
            a, b, stage[3] = lax.optimization_barrier((a, b, stage[3]))
        return a, b

    sums = reduce_both(a_send, a_keep, b_send, b_keep, c_own[None, :half], c_own[None, half:], meanwhile)
    return stage[3], finish(*sums)


def solution(mesh):
    placed = (
        P("seq", None),
        P("seq", None),
        P(None, "tp"),
        P(None, "tp"),
        P("tp"),
        P("tp", None),
        P("tp"),
    )
    return jax.shard_map(
        per_device,
        mesh=mesh,
        in_specs=placed,
        out_specs=(P("seq", "tp"), P("seq", "tp")),
        check_vma=False,
    )
```

```python
import functools

import jax
import jax.numpy as jnp
import numpy as np
from jax import lax
from jax.experimental import pallas as pl
from jax.experimental.pallas import tpu as pltpu
from jax.sharding import PartitionSpec as P

FEAT = 16
DV = 128
HW = 2 * FEAT + DV
EP = 256
ES = 160
CH = 256
EPS = 1e-06
BF = jnp.bfloat16
F32 = jnp.float32
MIB = 1024 * 1024


def mm(a, b):
    return lax.dot_general(a, b, (((1,), (0,)), ((), ())), preferred_element_type=F32)


def mm_nt(a, b):
    return lax.dot_general(a, b, (((1,), (1,)), ((), ())), preferred_element_type=F32)


def mm_tn(a, b):
    return lax.dot_general(a, b, (((0,), (0,)), ((), ())), preferred_element_type=F32)


def selectors(heads):
    sel = np.zeros((heads, 128, 4 * EP), np.float32)
    bias = np.zeros((8, EP), np.float32)
    bias[1, :FEAT] = 1.0
    bias[0, FEAT] = bias[1, FEAT] = 1.0
    for h in range(heads):
        q0 = (HW * h) % 128
        k0 = q0 + FEAT
        for i in range(FEAT):
            sel[h, q0 + i, i] = 0.5
            sel[h, k0 + i, 2 * EP + i] = 0.5
        col = FEAT + 1
        for i in range(FEAT):
            for j in range(i, FEAT):
                sel[h, q0 + i, col] = 0.25 if i == j else 0.5
                sel[h, q0 + j, EP + col] = 0.5
                sel[h, k0 + i, 2 * EP + col] = 0.5
                sel[h, k0 + j, 3 * EP + col] = 0.5
                col += 1
    return jnp.asarray(sel, BF), jnp.asarray(bias, F32)


def window(h):
    t = (HW * h) // 128
    return slice(128 * t, 128 * t + 128)


def value_place(h):
    start = HW * h + 2 * FEAT
    return start // 128, start % 128


def lane_iota():
    return lax.broadcasted_iota(jnp.int32, (CH, 128), 1)


def take_values(conv, h):
    tile, off = value_place(h)
    first = conv[:, 128 * tile : 128 * tile + 128]
    if off == 0:
        return first
    second = conv[:, 128 * tile + 128 : min(128 * tile + 256, conv.shape[1])]
    if second.shape[1] < 128:
        second = jnp.concatenate([second, jnp.zeros((CH, 128 - second.shape[1]), second.dtype)], 1)
    a = pltpu.roll(first, 128 - off, 1)
    b = pltpu.roll(second, 128 - off, 1)
    return jnp.where(lane_iota() < 128 - off, a, b)


def causal():
    r = lax.broadcasted_iota(jnp.int32, (CH, CH), 0)
    c = lax.broadcasted_iota(jnp.int32, (CH, CH), 1)
    return r >= c


def params(mib):
    return pltpu.CompilerParams(dimension_semantics=("arbitrary",), vmem_limit_bytes=mib * MIB)


def whole(shape):
    return pl.BlockSpec(shape, lambda c, *_: (0,) * len(shape))


KEPT = pl.BlockSpec(memory_space=pltpu.VMEM)


def kept(shape, dtype):
    return pltpu.VMEM(shape, dtype)


def keep(array):
    return pltpu.with_memory_space_constraint(array, pltpu.VMEM)


def stay(array):
    return pltpu.with_memory_space_constraint(array, pltpu.HBM)


def cost(flops):
    return pl.CostEstimate(flops=int(flops), bytes_accessed=1 << 20, transcendentals=0)


LIGHT = cost(1000)


def rows_at(c):
    return pl.ds(pl.multiple_of(c * CH, CH), CH)


def biased(u, bias):
    return jnp.concatenate([u[:, :128] + bias[:, :128], u[:, 128:]], 1)


def with_rows(hbm_ref, first_ref, buf, sems, use):
    c = pl.program_id(0)

    def fetch(k):
        slot = lax.rem(k, 2)
        return pltpu.make_async_copy(hbm_ref.at[rows_at(k), :], buf.at[slot], sems.at[slot])

    @pl.when(c == 0)
    def _():
        fetch(1).start()
        use(first_ref[...])

    @pl.when(c >= 1)
    def _():
        fetch(c).wait()

        @pl.when(c + 1 < pl.num_programs(0))
        def _():
            fetch(c + 1).start()

        use(buf[lax.rem(c, 2)])


def project_kernel(heads, x_ref, x_first_ref, ct_ref, halo_ref, w_ref, cw_ref, sel_ref, bias_ref,
                   v_ref, pq_ref, pk_ref, fq_ref, fk_ref, loc_ref, ct_first_ref, state_ref, ext, run, buf, sems):
    c = pl.program_id(0)
    at = rows_at(c)
    last = pl.num_programs(0) - 1
    ct_copy = pltpu.make_async_copy(ct_ref.at[pl.ds(0, CH), :], ct_first_ref, sems.at[2])

    @pl.when(c == 0)
    def _():
        before = mm(halo_ref[...], w_ref[...]).astype(BF).astype(F32)
        ext[0:8, :] = before[8:16]
        run[...] = jnp.zeros_like(run)

    @pl.when(c == last)
    def _():
        ct_copy.start()

    def product(rows):
        ext[8:, :] = mm(rows, w_ref[...]).astype(BF).astype(F32)

    with_rows(x_ref, x_first_ref, buf, sems, product)
    conv = (cw_ref[0:1] * ext[8 : 8 + CH, :] + cw_ref[1:2] * ext[7 : 7 + CH, :]
            + cw_ref[2:3] * ext[6 : 6 + CH, :])
    ext[0:8, :] = ext[CH : CH + 8, :]
    conv_b = conv.astype(BF)
    conv = conv_b.astype(F32)
    b0 = bias_ref[0:1]
    b1 = bias_ref[1:2]
    for h in range(heads):
        u = mm(conv_b[:, window(h)], sel_ref[h])
        first, second = biased(u[:, :EP], b0), biased(u[:, EP : 2 * EP], b1)
        pq_ref[h, at, :] = (first * second).astype(BF)
        fq_ref[h, at, :EP] = first.astype(BF)
        fq_ref[h, at, EP:] = second.astype(BF)
        first, second = biased(u[:, 2 * EP : 3 * EP], b0), biased(u[:, 3 * EP :], b1)
        pk = (first * second).astype(BF)
        pk_ref[h, at, :] = pk
        fk_ref[h, at, :EP] = first.astype(BF)
        fk_ref[h, at, EP:] = second.astype(BF)
        v = take_values(conv, h).astype(BF)
        v_ref[at, DV * h : DV * h + DV] = v
        loc_ref[c, h] = run[h].astype(BF)
        run[h] = run[h] + mm_tn(v, pk)

    @pl.when(c == last)
    def _():
        for h in range(heads):
            state_ref[h] = run[h].T[:ES].astype(BF)
        ct_copy.wait()


def project(x, x_first, ct, halo, w_in, conv_w, sel, bias, heads):
    rows, d = x.shape
    width = w_in.shape[1]
    n = rows // CH
    return pl.pallas_call(
        functools.partial(project_kernel, heads),
        grid=(n,),
        in_specs=[
            pl.BlockSpec(memory_space=pltpu.HBM),
            KEPT,
            pl.BlockSpec(memory_space=pltpu.HBM),
            whole((16, d)),
            KEPT,
            whole((3, width)),
            KEPT,
            whole(bias.shape),
        ],
        out_specs=[KEPT] * 7 + [whole((heads, ES, DV))],
        out_shape=[
            kept((rows, heads * DV), BF),
            kept((heads, rows, EP), BF),
            kept((heads, rows, EP), BF),
            kept((heads, rows, 2 * EP), BF),
            kept((heads, rows, 2 * EP), BF),
            kept((n, heads, DV, EP), BF),
            kept((CH, d), BF),
            jax.ShapeDtypeStruct((heads, ES, DV), BF),
        ],
        scratch_shapes=[
            pltpu.VMEM((CH + 8, width), F32),
            pltpu.VMEM((heads, DV, EP), F32),
            pltpu.VMEM((2, CH, d), BF),
            pltpu.SemaphoreType.DMA((3,)),
        ],
        compiler_params=params(9),
        cost_estimate=cost(100 << 30),
        name="project",
    )(stay(x), keep(x_first), stay(ct), halo, keep(w_in), conv_w, keep(sel), bias)


def local_kernel(heads, ct_ref, ct_first_ref, wo_ref, gain_ref, v_ref, pq_ref, pk_ref, loc_ref, fq_ref, fk_ref, sel_ref,
                 g_ref, num_ref, wt_ref, slope_ref, buf, sems):
    c = pl.program_id(0)
    at = rows_at(c)

    def product(rows):
        g_ref[at, :] = mm_nt(rows, wo_ref[...]) * gain_ref[...]

    with_rows(ct_ref, ct_first_ref, buf, sems, product)
    mask = causal()
    for h in range(heads):
        pq = pq_ref[h, at, :]
        logits = mm_nt(pq[:, :FEAT], pk_ref[h, at, :FEAT])
        slope = 1.0 + logits
        weights = jnp.where(mask, 0.5 + 0.5 * slope * slope, 0.0).astype(BF)
        wt_ref[h, at, :] = weights
        slope_ref[h, at, :] = jnp.where(mask, slope, 0.0).astype(BF)
        lanes = slice(DV * h, DV * h + DV)
        num_ref[at, lanes] = mm(weights, v_ref[at, lanes]) + mm_nt(pq, loc_ref[c, h])


def local_part(ct, ct_first, w_out, gain, v, pq, pk, loc, fq, fk, sel, heads):
    rows, d = ct.shape
    n = rows // CH
    wide = heads * DV
    return pl.pallas_call(
        functools.partial(local_kernel, heads),
        grid=(n,),
        in_specs=[pl.BlockSpec(memory_space=pltpu.HBM), KEPT, KEPT, whole((1, wide))] + [KEPT] * 7,
        out_specs=[KEPT] * 4,
        out_shape=[kept((rows, wide), F32)] * 2 + [kept((heads, rows, CH), BF)] * 2,
        scratch_shapes=[pltpu.VMEM((2, CH, d), BF), pltpu.SemaphoreType.DMA((2,))],
        compiler_params=params(8),
        cost_estimate=LIGHT,
        name="local_part",
    )(stay(ct), keep(ct_first), keep(w_out), gain, *map(keep, (v, pq, pk, loc, fq, fk, sel)))


def norm_kernel(heads, parts, passed, g_ref, num_ref, gain_ref, pq_ref, ones_ref, *refs):
    got = refs[:parts]
    ho_ref, dn_ref, loc_ref, pre_ref, state_ref, run = refs[parts + passed :]
    step = pl.program_id(0)
    c = pl.num_programs(0) - 1 - step
    at = rows_at(c)

    @pl.when(step == 0)
    def _():
        run[...] = jnp.zeros_like(run)
        total = got[0][...].astype(F32)
        for one in got[1:]:
            total = total + one[...].astype(F32)
        pre_ref[...] = total.astype(BF)

    for h in range(0, heads, 2):
        lanes = slice(DV * h, DV * h + 2 * DV)
        pqs = [pq_ref[h, at, :], pq_ref[h + 1, at, :]]
        num = num_ref[at, lanes] + jnp.concatenate(
            [mm(pqs[0][:, :ES], pre_ref[h]), mm(pqs[1][:, :ES], pre_ref[h + 1])], 1
        )
        inv = lax.rsqrt(mm((num * num).astype(BF), ones_ref[...]) + EPS)
        normed = num * inv
        ho_ref[at, lanes] = (normed * gain_ref[:, lanes]).astype(BF)
        g = g_ref[at, lanes]
        dn = ((g - normed * mm((g * normed).astype(BF), ones_ref[...])) * inv).astype(BF)
        dn_ref[at, lanes] = dn
        for i in range(2):
            loc_ref[c, h + i] = run[h + i].astype(BF)
            run[h + i] = run[h + i] + mm_tn(dn[:, DV * i : DV * i + DV], pqs[i])

    @pl.when(step == pl.num_programs(0) - 1)
    def _():
        for h in range(heads):
            state_ref[h] = run[h].T[:ES].astype(BF)


def norm_part(g, num, gain, pq, got, later, heads):
    ones = jnp.asarray(np.kron(np.eye(2), np.full((DV, DV), 1.0 / DV)), BF)
    rows, wide = g.shape
    n = rows // CH
    return pl.pallas_call(
        functools.partial(norm_kernel, heads, len(got), len(later)),
        grid=(n,),
        in_specs=[KEPT, KEPT, whole((1, wide)), KEPT, whole((2 * DV, 2 * DV))]
        + [whole((heads, ES, DV))] * len(got)
        + [KEPT] * len(later),
        out_specs=[KEPT] * 4 + [whole((heads, ES, DV))],
        out_shape=[
            kept((rows, wide), BF),
            kept((rows, wide), BF),
            kept((n, heads, DV, EP), BF),
            kept((heads, ES, DV), BF),
            jax.ShapeDtypeStruct((heads, ES, DV), BF),
        ],
        scratch_shapes=[pltpu.VMEM((heads, DV, EP), F32)],
        compiler_params=params(5),
        cost_estimate=cost(16 << 30),
        name="norm_part",
    )(keep(g), keep(num), gain, keep(pq), ones, *got, *map(keep, later))


def inner_kernel(heads, v_ref, pq_ref, pk_ref, fq_ref, wt_ref, slope_ref, dn_ref, loc_ref, pre_ref, sel_ref,
                 fk_ref, gloc_ref, dqk_ref, dv_ref, xk_ref, pre_t):
    c = pl.program_id(0)
    at = rows_at(c)

    @pl.when(c == 0)
    def _():
        pre_t[...] = jnp.zeros_like(pre_t)
        for h in range(heads):
            pre_t[h, :, :ES] = pre_ref[h].astype(F32).T

    linear = lane_iota() < FEAT
    dqk = None
    for h in range(heads):
        lanes = slice(DV * h, DV * h + DV)
        dn = dn_ref[at, lanes]
        dv_ref[at, lanes] = mm_tn(wt_ref[h, at, :], dn)
        dl = (mm_nt(dn, v_ref[at, lanes]) * slope_ref[h, at, :].astype(F32)).astype(BF)
        xk_ref[h, at, :] = mm_tn(dl, pq_ref[h, at, :128])
        state = (loc_ref[c, h].astype(F32) + pre_t[h]).astype(BF)
        dphi = mm(dn, state)
        dphi = jnp.concatenate(
            [dphi[:, :128] + jnp.where(linear, mm(dl, pk_ref[h, at, :128]), 0.0), dphi[:, 128:]], 1
        )
        da = (dphi * fq_ref[h, at, EP:].astype(F32)).astype(BF)
        db = (dphi * fq_ref[h, at, :EP].astype(F32)).astype(BF)
        part = mm_nt(da, sel_ref[h, :, :EP]) + mm_nt(db, sel_ref[h, :, EP : 2 * EP])
        dqk = part if dqk is None else dqk + part
    dqk_ref[at, :] = dqk


def inner_part(v, pq, pk, fq, wt, slope, dn, loc, pre, sel, fk, gloc, heads):
    rows = v.shape[0]
    n = rows // CH
    return pl.pallas_call(
        functools.partial(inner_kernel, heads),
        grid=(n,),
        in_specs=[KEPT] * 12,
        out_specs=[KEPT] * 3,
        out_shape=[
            kept((rows, 128), F32),
            kept((rows, heads * DV), F32),
            kept((heads, rows, 128), F32),
        ],
        scratch_shapes=[pltpu.VMEM((heads, DV, EP), F32)],
        compiler_params=params(5),
        cost_estimate=LIGHT,
        name="inner_part",
    )(*map(keep, (v, pq, pk, fq, wt, slope, dn, loc, pre, sel, fk, gloc)))


def outer_kernel(heads, parts, v_ref, pk_ref, fk_ref, dqk_ref, dv_ref, xk_ref, loc_ref, sel_ref, cw_ref, *refs):
    got = refs[:parts]
    top_ref, dp_ref, first_ref, last_ref, ext, suf_t = refs[parts:]
    half_chunks = pl.num_programs(0) // 2
    step = pl.program_id(0)
    c = pl.num_programs(0) - 1 - step
    at = rows_at(c)
    width = cw_ref.shape[1]

    @pl.when(step == 0)
    def _():
        suf_t[...] = jnp.zeros_like(suf_t)
        for h in range(heads):
            total = got[0][h].astype(F32)
            for one in got[1:]:
                total = total + one[h].astype(F32)
            suf_t[h, :, :ES] = total.T
        ext[CH:, :] = jnp.zeros((8, width), F32)

    lane = lane_iota()
    tiles = [None] * (-(-width // 128))

    def put(t, piece):
        tiles[t] = piece if tiles[t] is None else tiles[t] + piece

    dqk = dqk_ref[at, :]
    for h in range(heads):
        lanes = slice(DV * h, DV * h + DV)
        state = (loc_ref[c, h].astype(F32) + suf_t[h]).astype(BF)
        dphi = mm(v_ref[at, lanes], state)
        dphi = jnp.concatenate(
            [dphi[:, :128] + jnp.where(lane < FEAT, xk_ref[h, at, :], 0.0), dphi[:, 128:]], 1
        )
        da = (dphi * fk_ref[h, at, EP:].astype(F32)).astype(BF)
        db = (dphi * fk_ref[h, at, :EP].astype(F32)).astype(BF)
        own = (
            dqk
            + mm_nt(da, sel_ref[h, :, 2 * EP : 3 * EP])
            + mm_nt(db, sel_ref[h, :, 3 * EP : 4 * EP])
        )
        q0 = (HW * h) % 128
        put((HW * h) // 128, jnp.where((lane >= q0) & (lane < q0 + 2 * FEAT), own, 0.0))
        dv = dv_ref[at, lanes] + mm_nt(pk_ref[h, at, :], state)
        tile, off = value_place(h)
        if off == 0:
            put(tile, dv)
        else:
            moved = pltpu.roll(dv, off, 1)
            put(tile, jnp.where(lane >= off, moved, 0.0))
            put(tile + 1, jnp.where(lane < off, moved, 0.0))
    for t, tile in enumerate(tiles):
        end = min(128 * t + 128, width)
        ext[:CH, 128 * t : end] = tile[:, : end - 128 * t]
    dp = (cw_ref[0:1] * ext[:CH, :] + cw_ref[1:2] * ext[1 : CH + 1, :]
          + cw_ref[2:3] * ext[2 : CH + 2, :])
    dp_ref[at, :] = dp.astype(BF)

    @pl.when(c < half_chunks)
    def _():
        top_ref[at, :] = dp.astype(BF)

    @pl.when(step == 0)
    def _():
        last_ref[...] = dp[CH - 16 :]

    ext[CH:, :] = ext[0:8, :]
    first_ref[...] = ext[0:8, :]


def outer_part(v, pk, fk, dqk, dv, xk, loc, got, sel, conv_w, heads):
    rows, width = v.shape[0], conv_w.shape[1]
    n = rows // CH
    return pl.pallas_call(
        functools.partial(outer_kernel, heads, len(got)),
        grid=(n,),
        in_specs=[KEPT] * 8 + [whole((3, width))] + [whole((heads, ES, DV))] * len(got),
        out_specs=[KEPT, KEPT, whole((8, width)), KEPT],
        out_shape=[
            kept((rows // 2, width), BF),
            kept((rows, width), BF),
            jax.ShapeDtypeStruct((8, width), F32),
            kept((16, width), F32),
        ],
        scratch_shapes=[pltpu.VMEM((CH + 8, width), F32), pltpu.VMEM((heads, DV, EP), F32)],
        compiler_params=params(5),
        cost_estimate=cost(16 << 30),
        name="outer_part",
    )(*map(keep, (v, pk, fk, dqk, dv, xk, loc, sel)), conv_w, *got)


def run_copies(copies, sems):
    copies = [pltpu.make_async_copy(*one, sems.at[i]) for i, one in enumerate(copies)]
    for copy in copies:
        copy.start()
    for copy in copies:
        copy.wait()


def column_copies(which, place_ref, w_ref, outs):
    wide = outs[0].shape[1]
    for m, out in zip(which, outs):
        start = pl.multiple_of(lax.bitwise_xor(place_ref[0], m) * wide, wide)
        yield w_ref.at[:, pl.ds(start, wide)], out


def near_kernel(which, place_ref, w_ref, x_ref, tail_ref, *refs):
    rows = tail_ref.shape[0]
    copies = list(column_copies(which, place_ref, w_ref, refs[:-1]))
    copies.append((x_ref.at[pl.ds(x_ref.shape[0] - rows, rows), :], tail_ref))
    run_copies(copies, refs[-1])


def rest_kernel(which, place_ref, w_ref, wi_ref, x_ref, blocks_ref, first_ref, *refs):
    copies = list(column_copies(which, place_ref, w_ref, refs[:-1]))
    count, sw = blocks_ref.shape[:2]
    for r in range(count):
        block = 2 * lax.bitwise_xor(place_ref[0], r) + 1 - place_ref[1]
        copies.append((wi_ref.at[pl.ds(pl.multiple_of(block * sw, sw), sw), :], blocks_ref.at[r]))
    copies.append((x_ref.at[pl.ds(0, CH), :], first_ref))
    run_copies(copies, refs[-1])


def copied(kernel, which, place, arrays, extra, specs, copies, name):
    rows, d = arrays[0].shape
    anywhere = pl.BlockSpec(memory_space=pltpu.HBM)
    pairs = lax.axis_size("tp") // 2
    return pl.pallas_call(
        functools.partial(kernel, which),
        grid_spec=pltpu.PrefetchScalarGridSpec(
            num_scalar_prefetch=1,
            grid=(1,),
            in_specs=[anywhere] * len(arrays),
            out_specs=specs + [anywhere] * len(which),
            scratch_shapes=[pltpu.SemaphoreType.DMA((copies,))],
        ),
        out_shape=extra + [jax.ShapeDtypeStruct((rows, d // pairs), arrays[0].dtype)] * len(which),
        compiler_params=pltpu.CompilerParams(vmem_limit_bytes=4 * MIB),
        cost_estimate=LIGHT,
        name=name,
    )(place, *map(stay, arrays))


def near_sends(place, w_out, x):
    tail = jax.ShapeDtypeStruct((16, x.shape[1]), x.dtype)
    spec = pl.BlockSpec(memory_space=pltpu.HBM)
    return copied(near_kernel, (1, 2), place, (w_out, x), [tail], [spec], 3, "near_sends")


def rest_sends(place, w_out, w_in, x):
    pairs = lax.axis_size("tp") // 2
    which = tuple(range(3, pairs))
    blocks = jax.ShapeDtypeStruct((pairs, w_in.shape[0] // (2 * pairs), w_in.shape[1]), w_in.dtype)
    specs = [pl.BlockSpec(memory_space=pltpu.HBM), KEPT]
    extra = [blocks, kept((CH, x.shape[1]), x.dtype)]
    return copied(
        rest_kernel, which, place, (w_out, w_in, x), extra, specs, len(which) + pairs + 1, "rest_sends"
    )


def shifted(array, by):
    count = lax.axis_size("seq")
    pairs = [(i, i + by) for i in range(count) if 0 <= i + by < count]
    return lax.ppermute(array, "seq", pairs)


def from_others(part, sign):
    return [shifted(part, sign * step) for step in range(1, lax.axis_size("seq"))]


def out_kernel(count, sw, place_ref, *refs):
    tops, lows, ws = refs[:count], refs[count : 2 * count], refs[2 * count : 3 * count]
    send_ref, keep_ref = refs[3 * count :]
    c = pl.program_id(0)
    half_chunks = pl.num_programs(0) // 2
    odd = place_ref[1] == 1

    def product(parts):
        total = None
        for part, w in zip(parts, ws):
            one = mm(part[...], w[...])
            total = one if total is None else total + one
        first, second = total[:, :sw], total[:, sw:]
        send_ref[rows_at(c), :] = jnp.where(odd, first, second).astype(BF)
        keep_ref[rows_at(c), :] = jnp.where(odd, second, first)

    @pl.when(c < half_chunks)
    def _():
        product(tops)

    @pl.when(c >= half_chunks)
    def _():
        product(lows)


def out_part(place, tops, lows, ws):
    count = len(ws)
    rows = 2 * CH * (lows[0][1] // CH)
    wide = tops[0][0].shape[1]
    sw = ws[1].shape[1] // 2
    part = rows // (2 * CH)
    operands, specs = [], []
    for array, start in tops:
        operands.append(array)
        specs.append(
            pl.BlockSpec((CH, wide), lambda c, place, s=start // CH: (s + jnp.minimum(c, part - 1), 0))
        )
    for array, start in lows:
        operands.append(array)
        specs.append(
            pl.BlockSpec((CH, wide), lambda c, place, s=start // CH: (s + jnp.maximum(c - part, 0), 0))
        )
    return pl.pallas_call(
        functools.partial(out_kernel, count, sw),
        grid_spec=pltpu.PrefetchScalarGridSpec(
            num_scalar_prefetch=1,
            grid=(rows // CH,),
            in_specs=specs
            + [pl.BlockSpec((wide, 2 * sw), lambda c, place: (0, place[0]))]
            + [pl.BlockSpec((wide, 2 * sw), lambda c, place: (0, 0))] * (count - 1),
            out_specs=[KEPT, KEPT],
        ),
        out_shape=[kept((rows, sw), BF), kept((rows, sw), F32)],
        compiler_params=params(16),
        cost_estimate=cost(16 << 30),
        name="out_part",
    )(place, *operands, *map(stay, ws))


def complete_kernel(dp_ref, last_ref, after_ref, cw_ref, low_ref):
    half = low_ref.shape[0]
    low_ref[...] = dp_ref[half:, :]
    row = lax.broadcasted_iota(jnp.int32, last_ref.shape, 0)
    a0, a1 = after_ref[0:1], after_ref[1:2]
    one = cw_ref[2:3] * a0
    two = cw_ref[1:2] * a0 + cw_ref[2:3] * a1
    tail = last_ref[...] + jnp.where(row == 14, one, 0.0) + jnp.where(row == 15, two, 0.0)
    low_ref[half - 16 :, :] = tail.astype(BF)


def complete(dp, last, after, conv_w):
    rows, width = dp.shape
    return pl.pallas_call(
        complete_kernel,
        in_specs=[KEPT] * 4,
        out_specs=KEPT,
        out_shape=kept((rows // 2, width), BF),
        compiler_params=pltpu.CompilerParams(vmem_limit_bytes=4 * MIB),
        cost_estimate=LIGHT,
        name="complete",
    )(keep(dp), keep(last), after, conv_w)


def grad_kernel(count, low_first, place_ref, dp_ref, other_ref, w_ref, w_other_ref, send_ref, keep_ref, both):
    r = pl.program_id(0)
    half, sw = send_ref.shape[1:]
    width = w_ref.shape[1]

    @pl.when(r == 0)
    def _():
        both[:, :width] = dp_ref[...]
        both[:, width:] = other_ref[...]

    block = 2 * lax.bitwise_xor(place_ref[0], r) + place_ref[1]
    w = w_ref[pl.ds(pl.multiple_of(block * sw, sw), sw), :]
    total = mm_nt(both[...], jnp.concatenate([w, w_other_ref[r]], 1)).astype(BF)
    part = count // 2
    leaves = (r % 2 == 1) if low_first else (r >= part)

    @pl.when(leaves)
    def _():
        send_ref[r // 2 if low_first else r - part] = total

    @pl.when(jnp.logical_not(leaves))
    def _():
        keep_ref[r // 2 if low_first else r] = total


def grad_part(place, dp, other, w_in, w_other, low_first):
    half, width = dp.shape
    count, sw = w_other.shape[:2]
    return pl.pallas_call(
        functools.partial(grad_kernel, count, low_first),
        grid_spec=pltpu.PrefetchScalarGridSpec(
            num_scalar_prefetch=1,
            grid=(count,),
            in_specs=[KEPT] * 4,
            out_specs=[KEPT] * 2,
            scratch_shapes=[pltpu.VMEM((half, 2 * width), BF)],
        ),
        out_shape=[kept((count // 2, half, sw), BF)] * 2,
        compiler_params=params(5),
        cost_estimate=LIGHT,
        name="grad_part",
    )(place, *map(keep, (dp, other, w_in, w_other)))


def halves_kernel(x_ref, y_ref, x_top_ref, y_low_ref):
    half = x_top_ref.shape[0]
    x_top_ref[...] = x_ref[:half, :]
    y_low_ref[...] = y_ref[half:, :]


def halves(x_got, y_got):
    rows, wide = x_got.shape
    return pl.pallas_call(
        halves_kernel,
        in_specs=[KEPT] * 2,
        out_specs=[KEPT] * 2,
        out_shape=[kept((rows // 2, wide), BF)] * 2,
        compiler_params=pltpu.CompilerParams(vmem_limit_bytes=4 * MIB),
        cost_estimate=LIGHT,
        name="halves",
    )(keep(x_got), keep(y_got))


def swapped(array, distance):
    count = lax.axis_size("tp")
    return lax.ppermute(array, "tp", [(i, i ^ distance) for i in range(count)])


def summed(a, b):
    return a.astype(F32) + b.astype(F32)


def passing_kernel(places, *refs):
    ins, out_ref = refs[:-1], refs[-1]
    for i in range(out_ref.shape[0]):
        total = None
        for ref, place in zip(ins, places):
            one = ref[place[i]].astype(F32)
            total = one if total is None else total + one
        out_ref[i] = total.astype(BF)


def passing(terms, blocks):
    places = [[place[i] for i in blocks] for _, place in terms]
    return pl.pallas_call(
        functools.partial(passing_kernel, places),
        in_specs=[KEPT] * len(terms),
        out_specs=KEPT,
        out_shape=kept((len(blocks),) + terms[0][0].shape[1:], BF),
        compiler_params=pltpu.CompilerParams(vmem_limit_bytes=4 * MIB),
        cost_estimate=LIGHT,
        name="passing",
    )(*[keep(array) for array, _ in terms])


def reduce_both(a_send, a_keep, b_send, b_keep, meanwhile):
    pairs = lax.axis_size("tp") // 2
    a_step, b_step = 1, pairs // 2
    left = pairs // 2
    a_terms, b_terms = [(a_keep, list(range(left)))], [(b_keep, list(range(left)))]
    while True:
        a_got, b_got = swapped(a_send, 2 * a_step), swapped(b_send, 2 * b_step)
        a_got, b_got = meanwhile(a_got, b_got)
        a_terms.append((a_got, list(range(left))))
        b_terms.append((b_got, list(range(left))))
        if left == 1:
            return a_terms, b_terms
        half = left // 2
        a_send = passing(a_terms, list(range(1, left, 2)))
        b_send = passing(b_terms, list(range(half, left)))
        a_terms = [(array, place[0::2]) for array, place in a_terms]
        b_terms = [(array, place[:half]) for array, place in b_terms]
        left = half
        a_step, b_step = a_step * 2, b_step // 2


def own_kernel(place_ref, x_ref, ct_ref, x_own_ref, ct_own_ref, sems):
    sw = x_own_ref.shape[1]
    at = pl.ds(pl.multiple_of(place_ref[2] * sw, sw), sw)
    copies = [
        pltpu.make_async_copy(x_ref.at[:, at], x_own_ref, sems.at[0]),
        pltpu.make_async_copy(ct_ref.at[:, at], ct_own_ref, sems.at[1]),
    ]
    for copy in copies:
        copy.start()
    for copy in copies:
        copy.wait()


def own_columns(place, x, ct, sw):
    rows = x.shape[0]
    anywhere = pl.BlockSpec(memory_space=pltpu.HBM)
    return pl.pallas_call(
        own_kernel,
        grid_spec=pltpu.PrefetchScalarGridSpec(
            num_scalar_prefetch=1,
            grid=(1,),
            in_specs=[anywhere] * 2,
            out_specs=[KEPT] * 2,
            scratch_shapes=[pltpu.SemaphoreType.DMA((2,))],
        ),
        out_shape=[kept((rows, sw), x.dtype)] * 2,
        compiler_params=pltpu.CompilerParams(vmem_limit_bytes=4 * MIB),
        cost_estimate=LIGHT,
        name="own_columns",
    )(place, stay(x), stay(ct))


def finish_kernel(places, own_ref, *refs):
    tops, lows, out_ref = refs[: len(places)], refs[len(places) : -1], refs[-1]
    half = out_ref.shape[0] // 2
    for first, ins in ((0, tops), (half, lows)):
        total = own_ref[first : first + half, :].astype(F32)
        for ref, place in zip(ins, places):
            total = total + ref[place].astype(F32)
        out_ref[first : first + half, :] = total.astype(BF)


def finish(own, a_terms, b_terms):
    places = [index[0] for _, index in a_terms]
    assert places == [index[0] for _, index in b_terms]
    terms = [array for array, _ in a_terms + b_terms]
    return pl.pallas_call(
        functools.partial(finish_kernel, places),
        in_specs=[KEPT] * (1 + len(terms)),
        out_shape=jax.ShapeDtypeStruct(own.shape, BF),
        compiler_params=pltpu.CompilerParams(vmem_limit_bytes=6 * MIB),
        cost_estimate=LIGHT,
        name="finish",
    )(*map(keep, [own] + terms))


def finish_out_kernel(own_ref, keep_ref, got_ref, out_ref):
    out_ref[...] = (own_ref[...].astype(F32) + keep_ref[...] + got_ref[...].astype(F32)).astype(BF)


def finish_out(own, kept_part, got):
    return pl.pallas_call(
        finish_out_kernel,
        in_specs=[KEPT] * 3,
        out_shape=jax.ShapeDtypeStruct(own.shape, BF),
        compiler_params=pltpu.CompilerParams(vmem_limit_bytes=6 * MIB),
        cost_estimate=LIGHT,
        name="finish_out",
    )(*map(keep, (own, kept_part, got)))


def per_device(inputs, cotangent, w_in, conv_w, norm_gain, w_out, keep_flags):
    heads = keep_flags.shape[0]
    sel, bias = selectors(heads)
    tp = lax.axis_size("tp")
    pairs = tp // 2
    me = lax.axis_index("tp")
    pair = me // 2
    place = jnp.stack([pair, me % 2, me]).astype(jnp.int32)
    gain = (norm_gain.reshape(heads, DV) * keep_flags.astype(F32)[:, None]).reshape(1, heads * DV)

    half = inputs.shape[0] // 2
    tail, *near = near_sends(place, w_out, inputs)
    halo = shifted(tail, 1)
    near = [swapped(one, 2 * m) for m, one in enumerate(near, 1)]
    w_other, x_first, *far = rest_sends(place, w_out, w_in, inputs)
    w_other = swapped(w_other, 1)
    halo, place, gain, far = lax.optimization_barrier((halo, place, gain, far))
    v, pq, pk, fq, fk, loc, ct_first, state = project(
        inputs, x_first, cotangent, halo, w_in, conv_w, sel, bias, heads)
    state, w_other = lax.optimization_barrier((state, w_other))
    before = from_others(state, 1)
    v, near, far = lax.optimization_barrier((v, near, far))
    far = [swapped(one, 2 * m) for m, one in enumerate(far, 3)]
    g, num, wt, slope = local_part(cotangent, ct_first, w_out, gain, v, pq, pk, loc, fq, fk, sel, heads)
    ho, dn, gloc, pre, gstate = norm_part(
        g, num, gain, pq, before, (v, pk, fq, fk, wt, slope, loc, sel), heads
    )
    step = pairs // 2
    got = {r: swapped(ho, 2 * r) for r in range(1, pairs) if r != 1 + step}
    later = from_others(gstate, -1)
    pre, far = lax.optimization_barrier((pre, far))
    dqk, dv, xk = inner_part(v, pq, pk, fq, wt, slope, dn, loc, pre, sel, fk, gloc, heads)
    dp_top, dp, first, last = outer_part(v, pk, fk, dqk, dv, xk, gloc, later, sel, conv_w, heads)
    other_top = swapped(dp_top, 1)
    after = shifted(first, -1)
    a_send, a_keep = grad_part(place, dp_top, other_top, w_in, w_other, True)
    dp_low = complete(dp, last, after, conv_w)
    other_low = swapped(dp_low, 1)
    x_top, y_low = halves(got[1], got[step])
    x_top, y_low = swapped(x_top, 2 * step), swapped(y_low, 2)
    b_send, b_keep = grad_part(place, dp_low, other_low, w_in, w_other, False)
    tops = [(ho, 0)] + [(got.get(r, x_top), 0) for r in range(1, pairs)]
    lows = [(ho, half)] + [(got[r], half) if r in got else (y_low, 0) for r in range(1, pairs)]
    w_cols = [w_out] + near + far
    place_, b_keep = lax.optimization_barrier((place, b_keep))
    stage = []

    def meanwhile(a_got, b_got):
        if not stage:
            out_send, out_keep = out_part(place, tops, lows, w_cols)
            own = own_columns(place_, inputs, cotangent, inputs.shape[1] // tp)
            out_got = swapped(out_send, 1)
            a_got, b_got, out_keep = lax.optimization_barrier((a_got, b_got, out_keep))
            stage.extend([*own, out_keep, out_got])
        elif len(stage) == 4:
            stage.append(finish_out(stage[0], *stage[2:]))
            a_got, b_got, stage[4] = lax.optimization_barrier((a_got, b_got, stage[4]))
        return a_got, b_got

    a_terms, b_terms = reduce_both(a_send, a_keep, b_send, b_keep, meanwhile)
    return stage[4], finish(stage[1], a_terms, b_terms)


def solution(mesh):
    placed = (
        P("seq", None),
        P("seq", None),
        P(None, "tp"),
        P(None, "tp"),
        P("tp"),
        P("tp", None),
        P("tp"),
    )
    return jax.shard_map(
        per_device,
        mesh=mesh,
        in_specs=placed,
        out_specs=(P("seq", "tp"), P("seq", "tp")),
        check_vma=False,
    )
```

```python
import functools

import jax
import jax.numpy as jnp
import numpy as np
from jax import lax
from jax.experimental import pallas as pl
from jax.experimental.pallas import tpu as pltpu
from jax.sharding import PartitionSpec as P

FEAT = 16
DV = 128
HW = 2 * FEAT + DV
EP = 256
ES = 160
CH = 256
EPS = 1e-06
BF = jnp.bfloat16
F32 = jnp.float32
MIB = 1024 * 1024


def mm(a, b):
    return lax.dot_general(a, b, (((1,), (0,)), ((), ())), preferred_element_type=F32)


def mm_nt(a, b):
    return lax.dot_general(a, b, (((1,), (1,)), ((), ())), preferred_element_type=F32)


def mm_tn(a, b):
    return lax.dot_general(a, b, (((0,), (0,)), ((), ())), preferred_element_type=F32)


def selectors(heads):
    sel = np.zeros((heads, 128, 4 * EP), np.float32)
    bias = np.zeros((8, EP), np.float32)
    bias[1, :FEAT] = 1.0
    bias[0, FEAT] = bias[1, FEAT] = 1.0
    for h in range(heads):
        q0 = (HW * h) % 128
        k0 = q0 + FEAT
        for i in range(FEAT):
            sel[h, q0 + i, i] = 0.5
            sel[h, k0 + i, 2 * EP + i] = 0.5
        col = FEAT + 1
        for i in range(FEAT):
            for j in range(i, FEAT):
                sel[h, q0 + i, col] = 0.25 if i == j else 0.5
                sel[h, q0 + j, EP + col] = 0.5
                sel[h, k0 + i, 2 * EP + col] = 0.5
                sel[h, k0 + j, 3 * EP + col] = 0.5
                col += 1
    return jnp.asarray(sel, BF), jnp.asarray(bias, F32)


def window(h):
    t = (HW * h) // 128
    return slice(128 * t, 128 * t + 128)


def value_place(h):
    start = HW * h + 2 * FEAT
    return start // 128, start % 128


def lane_iota():
    return lax.broadcasted_iota(jnp.int32, (CH, 128), 1)


def take_values(conv, h):
    tile, off = value_place(h)
    first = conv[:, 128 * tile : 128 * tile + 128]
    if off == 0:
        return first
    second = conv[:, 128 * tile + 128 : min(128 * tile + 256, conv.shape[1])]
    if second.shape[1] < 128:
        second = jnp.concatenate([second, jnp.zeros((CH, 128 - second.shape[1]), second.dtype)], 1)
    a = pltpu.roll(first, 128 - off, 1)
    b = pltpu.roll(second, 128 - off, 1)
    return jnp.where(lane_iota() < 128 - off, a, b)


def causal():
    r = lax.broadcasted_iota(jnp.int32, (CH, CH), 0)
    c = lax.broadcasted_iota(jnp.int32, (CH, CH), 1)
    return r >= c


def params(mib):
    return pltpu.CompilerParams(dimension_semantics=("arbitrary",), vmem_limit_bytes=mib * MIB)


def whole(shape):
    return pl.BlockSpec(shape, lambda c, *_: (0,) * len(shape))


KEPT = pl.BlockSpec(memory_space=pltpu.VMEM)


def kept(shape, dtype):
    return pltpu.VMEM(shape, dtype)


def keep(array):
    return pltpu.with_memory_space_constraint(array, pltpu.VMEM)


def stay(array):
    return pltpu.with_memory_space_constraint(array, pltpu.HBM)


def cost(flops):
    return pl.CostEstimate(flops=int(flops), bytes_accessed=1 << 20, transcendentals=0)


LIGHT = cost(1000)


def rows_at(c):
    return pl.ds(pl.multiple_of(c * CH, CH), CH)


def biased(u, bias):
    return jnp.concatenate([u[:, :128] + bias[:, :128], u[:, 128:]], 1)


def with_rows(hbm_ref, first_ref, buf, sems, use):
    c = pl.program_id(0)

    def fetch(k):
        slot = lax.rem(k, 2)
        return pltpu.make_async_copy(hbm_ref.at[rows_at(k), :], buf.at[slot], sems.at[slot])

    @pl.when(c == 0)
    def _():
        fetch(1).start()
        use(first_ref[...])

    @pl.when(c >= 1)
    def _():
        fetch(c).wait()

        @pl.when(c + 1 < pl.num_programs(0))
        def _():
            fetch(c + 1).start()

        use(buf[lax.rem(c, 2)])


def project_kernel(heads, x_ref, x_first_ref, ct_ref, halo_ref, w_ref, cw_ref, sel_ref, bias_ref,
                   v_ref, pq_ref, pk_ref, fq_ref, fk_ref, loc_ref, ct_first_ref, state_ref, ext, run, buf, sems):
    c = pl.program_id(0)
    at = rows_at(c)
    last = pl.num_programs(0) - 1
    ct_copy = pltpu.make_async_copy(ct_ref.at[pl.ds(0, CH), :], ct_first_ref, sems.at[2])

    @pl.when(c == 0)
    def _():
        before = mm(halo_ref[...], w_ref[...]).astype(BF).astype(F32)
        ext[0:8, :] = before[8:16]
        run[...] = jnp.zeros_like(run)

    @pl.when(c == last)
    def _():
        ct_copy.start()

    def product(rows):
        ext[8:, :] = mm(rows, w_ref[...]).astype(BF).astype(F32)

    with_rows(x_ref, x_first_ref, buf, sems, product)
    conv = (cw_ref[0:1] * ext[8 : 8 + CH, :] + cw_ref[1:2] * ext[7 : 7 + CH, :]
            + cw_ref[2:3] * ext[6 : 6 + CH, :])
    ext[0:8, :] = ext[CH : CH + 8, :]
    conv_b = conv.astype(BF)
    conv = conv_b.astype(F32)
    b0 = bias_ref[0:1]
    b1 = bias_ref[1:2]
    for h in range(heads):
        u = mm(conv_b[:, window(h)], sel_ref[h])
        first, second = biased(u[:, :EP], b0), biased(u[:, EP : 2 * EP], b1)
        pq_ref[h, at, :] = (first * second).astype(BF)
        fq_ref[h, at, :EP] = first.astype(BF)
        fq_ref[h, at, EP:] = second.astype(BF)
        first, second = biased(u[:, 2 * EP : 3 * EP], b0), biased(u[:, 3 * EP :], b1)
        pk = (first * second).astype(BF)
        pk_ref[h, at, :] = pk
        fk_ref[h, at, :EP] = first.astype(BF)
        fk_ref[h, at, EP:] = second.astype(BF)
        v = take_values(conv, h).astype(BF)
        v_ref[at, DV * h : DV * h + DV] = v
        loc_ref[c, h] = run[h].astype(BF)
        run[h] = run[h] + mm_tn(v, pk)

    @pl.when(c == last)
    def _():
        for h in range(heads):
            state_ref[h] = run[h].T[:ES].astype(BF)
        ct_copy.wait()


def project(x, x_first, ct, halo, w_in, conv_w, sel, bias, heads):
    rows, d = x.shape
    width = w_in.shape[1]
    n = rows // CH
    return pl.pallas_call(
        functools.partial(project_kernel, heads),
        grid=(n,),
        in_specs=[
            pl.BlockSpec(memory_space=pltpu.HBM),
            KEPT,
            pl.BlockSpec(memory_space=pltpu.HBM),
            whole((16, d)),
            KEPT,
            whole((3, width)),
            KEPT,
            whole(bias.shape),
        ],
        out_specs=[KEPT] * 7 + [whole((heads, ES, DV))],
        out_shape=[
            kept((rows, heads * DV), BF),
            kept((heads, rows, EP), BF),
            kept((heads, rows, EP), BF),
            kept((heads, rows, 2 * EP), BF),
            kept((heads, rows, 2 * EP), BF),
            kept((n, heads, DV, EP), BF),
            kept((CH, d), BF),
            jax.ShapeDtypeStruct((heads, ES, DV), BF),
        ],
        scratch_shapes=[
            pltpu.VMEM((CH + 8, width), F32),
            pltpu.VMEM((heads, DV, EP), F32),
            pltpu.VMEM((2, CH, d), BF),
            pltpu.SemaphoreType.DMA((3,)),
        ],
        compiler_params=params(9),
        cost_estimate=cost(100 << 30),
        name="project",
    )(stay(x), keep(x_first), stay(ct), halo, keep(w_in), conv_w, keep(sel), bias)


def local_kernel(heads, ct_ref, ct_first_ref, wo_ref, gain_ref, v_ref, pq_ref, pk_ref, loc_ref, fq_ref, fk_ref, sel_ref,
                 g_ref, num_ref, wt_ref, slope_ref, buf, sems):
    c = pl.program_id(0)
    at = rows_at(c)

    def product(rows):
        g_ref[at, :] = mm_nt(rows, wo_ref[...]) * gain_ref[...]

    with_rows(ct_ref, ct_first_ref, buf, sems, product)
    mask = causal()
    for h in range(heads):
        pq = pq_ref[h, at, :]
        logits = mm_nt(pq[:, :FEAT], pk_ref[h, at, :FEAT])
        slope = 1.0 + logits
        weights = jnp.where(mask, 0.5 + 0.5 * slope * slope, 0.0).astype(BF)
        wt_ref[h, at, :] = weights
        slope_ref[h, at, :] = jnp.where(mask, slope, 0.0).astype(BF)
        lanes = slice(DV * h, DV * h + DV)
        num_ref[at, lanes] = mm(weights, v_ref[at, lanes]) + mm_nt(pq, loc_ref[c, h])


def local_part(ct, ct_first, w_out, gain, v, pq, pk, loc, fq, fk, sel, heads):
    rows, d = ct.shape
    n = rows // CH
    wide = heads * DV
    return pl.pallas_call(
        functools.partial(local_kernel, heads),
        grid=(n,),
        in_specs=[pl.BlockSpec(memory_space=pltpu.HBM), KEPT, KEPT, whole((1, wide))] + [KEPT] * 7,
        out_specs=[KEPT] * 4,
        out_shape=[kept((rows, wide), F32)] * 2 + [kept((heads, rows, CH), BF)] * 2,
        scratch_shapes=[pltpu.VMEM((2, CH, d), BF), pltpu.SemaphoreType.DMA((2,))],
        compiler_params=params(8),
        cost_estimate=LIGHT,
        name="local_part",
    )(stay(ct), keep(ct_first), keep(w_out), gain, *map(keep, (v, pq, pk, loc, fq, fk, sel)))


def norm_kernel(heads, parts, passed, g_ref, num_ref, gain_ref, pq_ref, ones_ref, *refs):
    got = refs[:parts]
    ho_ref, dn_ref, loc_ref, pre_ref, state_ref, run = refs[parts + passed :]
    step = pl.program_id(0)
    c = pl.num_programs(0) - 1 - step
    at = rows_at(c)

    @pl.when(step == 0)
    def _():
        run[...] = jnp.zeros_like(run)
        total = got[0][...].astype(F32)
        for one in got[1:]:
            total = total + one[...].astype(F32)
        pre_ref[...] = total.astype(BF)

    for h in range(0, heads, 2):
        lanes = slice(DV * h, DV * h + 2 * DV)
        pqs = [pq_ref[h, at, :], pq_ref[h + 1, at, :]]
        num = num_ref[at, lanes] + jnp.concatenate(
            [mm(pqs[0][:, :ES], pre_ref[h]), mm(pqs[1][:, :ES], pre_ref[h + 1])], 1
        )
        inv = lax.rsqrt(mm((num * num).astype(BF), ones_ref[...]) + EPS)
        normed = num * inv
        ho_ref[at, lanes] = (normed * gain_ref[:, lanes]).astype(BF)
        g = g_ref[at, lanes]
        dn = ((g - normed * mm((g * normed).astype(BF), ones_ref[...])) * inv).astype(BF)
        dn_ref[at, lanes] = dn
        for i in range(2):
            loc_ref[c, h + i] = run[h + i].astype(BF)
            run[h + i] = run[h + i] + mm_tn(dn[:, DV * i : DV * i + DV], pqs[i])

    @pl.when(step == pl.num_programs(0) - 1)
    def _():
        for h in range(heads):
            state_ref[h] = run[h].T[:ES].astype(BF)


def norm_part(g, num, gain, pq, got, later, heads):
    ones = jnp.asarray(np.kron(np.eye(2), np.full((DV, DV), 1.0 / DV)), BF)
    rows, wide = g.shape
    n = rows // CH
    return pl.pallas_call(
        functools.partial(norm_kernel, heads, len(got), len(later)),
        grid=(n,),
        in_specs=[KEPT, KEPT, whole((1, wide)), KEPT, whole((2 * DV, 2 * DV))]
        + [whole((heads, ES, DV))] * len(got)
        + [KEPT] * len(later),
        out_specs=[KEPT] * 4 + [whole((heads, ES, DV))],
        out_shape=[
            kept((rows, wide), BF),
            kept((rows, wide), BF),
            kept((n, heads, DV, EP), BF),
            kept((heads, ES, DV), BF),
            jax.ShapeDtypeStruct((heads, ES, DV), BF),
        ],
        scratch_shapes=[pltpu.VMEM((heads, DV, EP), F32)],
        compiler_params=params(5),
        cost_estimate=cost(16 << 30),
        name="norm_part",
    )(keep(g), keep(num), gain, keep(pq), ones, *got, *map(keep, later))


def inner_kernel(heads, v_ref, pq_ref, pk_ref, fq_ref, wt_ref, slope_ref, dn_ref, loc_ref, pre_ref, sel_ref,
                 fk_ref, gloc_ref, dqk_ref, dv_ref, xk_ref, pre_t):
    c = pl.program_id(0)
    at = rows_at(c)

    @pl.when(c == 0)
    def _():
        pre_t[...] = jnp.zeros_like(pre_t)
        for h in range(heads):
            pre_t[h, :, :ES] = pre_ref[h].astype(F32).T

    linear = lane_iota() < FEAT
    dqk = None
    for h in range(heads):
        lanes = slice(DV * h, DV * h + DV)
        dn = dn_ref[at, lanes]
        dv_ref[at, lanes] = mm_tn(wt_ref[h, at, :], dn)
        dl = (mm_nt(dn, v_ref[at, lanes]) * slope_ref[h, at, :].astype(F32)).astype(BF)
        xk_ref[h, at, :] = mm_tn(dl, pq_ref[h, at, :128])
        state = (loc_ref[c, h].astype(F32) + pre_t[h]).astype(BF)
        dphi = mm(dn, state)
        dphi = jnp.concatenate(
            [dphi[:, :128] + jnp.where(linear, mm(dl, pk_ref[h, at, :128]), 0.0), dphi[:, 128:]], 1
        )
        da = (dphi * fq_ref[h, at, EP:].astype(F32)).astype(BF)
        db = (dphi * fq_ref[h, at, :EP].astype(F32)).astype(BF)
        part = mm_nt(da, sel_ref[h, :, :EP]) + mm_nt(db, sel_ref[h, :, EP : 2 * EP])
        dqk = part if dqk is None else dqk + part
    dqk_ref[at, :] = dqk


def inner_part(v, pq, pk, fq, wt, slope, dn, loc, pre, sel, fk, gloc, heads):
    rows = v.shape[0]
    n = rows // CH
    return pl.pallas_call(
        functools.partial(inner_kernel, heads),
        grid=(n,),
        in_specs=[KEPT] * 12,
        out_specs=[KEPT] * 3,
        out_shape=[
            kept((rows, 128), F32),
            kept((rows, heads * DV), F32),
            kept((heads, rows, 128), F32),
        ],
        scratch_shapes=[pltpu.VMEM((heads, DV, EP), F32)],
        compiler_params=params(5),
        cost_estimate=LIGHT,
        name="inner_part",
    )(*map(keep, (v, pq, pk, fq, wt, slope, dn, loc, pre, sel, fk, gloc)))


def outer_kernel(heads, parts, v_ref, pk_ref, fk_ref, dqk_ref, dv_ref, xk_ref, loc_ref, sel_ref, cw_ref, *refs):
    got = refs[:parts]
    top_ref, dp_ref, first_ref, last_ref, ext, suf_t = refs[parts:]
    half_chunks = pl.num_programs(0) // 2
    step = pl.program_id(0)
    c = pl.num_programs(0) - 1 - step
    at = rows_at(c)
    width = cw_ref.shape[1]

    @pl.when(step == 0)
    def _():
        suf_t[...] = jnp.zeros_like(suf_t)
        for h in range(heads):
            total = got[0][h].astype(F32)
            for one in got[1:]:
                total = total + one[h].astype(F32)
            suf_t[h, :, :ES] = total.T
        ext[CH:, :] = jnp.zeros((8, width), F32)

    lane = lane_iota()
    tiles = [None] * (-(-width // 128))

    def put(t, piece):
        tiles[t] = piece if tiles[t] is None else tiles[t] + piece

    dqk = dqk_ref[at, :]
    for h in range(heads):
        lanes = slice(DV * h, DV * h + DV)
        state = (loc_ref[c, h].astype(F32) + suf_t[h]).astype(BF)
        dphi = mm(v_ref[at, lanes], state)
        dphi = jnp.concatenate(
            [dphi[:, :128] + jnp.where(lane < FEAT, xk_ref[h, at, :], 0.0), dphi[:, 128:]], 1
        )
        da = (dphi * fk_ref[h, at, EP:].astype(F32)).astype(BF)
        db = (dphi * fk_ref[h, at, :EP].astype(F32)).astype(BF)
        own = (
            dqk
            + mm_nt(da, sel_ref[h, :, 2 * EP : 3 * EP])
            + mm_nt(db, sel_ref[h, :, 3 * EP : 4 * EP])
        )
        q0 = (HW * h) % 128
        put((HW * h) // 128, jnp.where((lane >= q0) & (lane < q0 + 2 * FEAT), own, 0.0))
        dv = dv_ref[at, lanes] + mm_nt(pk_ref[h, at, :], state)
        tile, off = value_place(h)
        if off == 0:
            put(tile, dv)
        else:
            moved = pltpu.roll(dv, off, 1)
            put(tile, jnp.where(lane >= off, moved, 0.0))
            put(tile + 1, jnp.where(lane < off, moved, 0.0))
    for t, tile in enumerate(tiles):
        end = min(128 * t + 128, width)
        ext[:CH, 128 * t : end] = tile[:, : end - 128 * t]
    dp = (cw_ref[0:1] * ext[:CH, :] + cw_ref[1:2] * ext[1 : CH + 1, :]
          + cw_ref[2:3] * ext[2 : CH + 2, :])
    dp_ref[at, :] = dp.astype(BF)

    @pl.when(c < half_chunks)
    def _():
        top_ref[at, :] = dp.astype(BF)

    @pl.when(step == 0)
    def _():
        last_ref[...] = dp[CH - 16 :]

    ext[CH:, :] = ext[0:8, :]
    first_ref[...] = ext[0:8, :]


def outer_part(v, pk, fk, dqk, dv, xk, loc, got, sel, conv_w, heads):
    rows, width = v.shape[0], conv_w.shape[1]
    n = rows // CH
    return pl.pallas_call(
        functools.partial(outer_kernel, heads, len(got)),
        grid=(n,),
        in_specs=[KEPT] * 8 + [whole((3, width))] + [whole((heads, ES, DV))] * len(got),
        out_specs=[KEPT, KEPT, whole((8, width)), KEPT],
        out_shape=[
            kept((rows // 2, width), BF),
            kept((rows, width), BF),
            jax.ShapeDtypeStruct((8, width), F32),
            kept((16, width), F32),
        ],
        scratch_shapes=[pltpu.VMEM((CH + 8, width), F32), pltpu.VMEM((heads, DV, EP), F32)],
        compiler_params=params(5),
        cost_estimate=cost(16 << 30),
        name="outer_part",
    )(*map(keep, (v, pk, fk, dqk, dv, xk, loc, sel)), conv_w, *got)


def run_copies(copies, sems):
    copies = [pltpu.make_async_copy(*one, sems.at[i]) for i, one in enumerate(copies)]
    for copy in copies:
        copy.start()
    for copy in copies:
        copy.wait()


def column_copies(which, place_ref, w_ref, outs):
    wide = outs[0].shape[1]
    for m, out in zip(which, outs):
        start = pl.multiple_of(lax.bitwise_xor(place_ref[0], m) * wide, wide)
        yield w_ref.at[:, pl.ds(start, wide)], out


def near_kernel(which, place_ref, w_ref, x_ref, tail_ref, *refs):
    rows = tail_ref.shape[0]
    copies = list(column_copies(which, place_ref, w_ref, refs[:-1]))
    copies.append((x_ref.at[pl.ds(x_ref.shape[0] - rows, rows), :], tail_ref))
    run_copies(copies, refs[-1])


def rest_kernel(which, place_ref, w_ref, wi_ref, x_ref, blocks_ref, first_ref, *refs):
    copies = list(column_copies(which, place_ref, w_ref, refs[:-1]))
    count, sw = blocks_ref.shape[:2]
    for r in range(count):
        block = 2 * lax.bitwise_xor(place_ref[0], r) + 1 - place_ref[1]
        copies.append((wi_ref.at[pl.ds(pl.multiple_of(block * sw, sw), sw), :], blocks_ref.at[r]))
    copies.append((x_ref.at[pl.ds(0, CH), :], first_ref))
    run_copies(copies, refs[-1])


def copied(kernel, which, place, arrays, extra, specs, copies, name):
    rows, d = arrays[0].shape
    anywhere = pl.BlockSpec(memory_space=pltpu.HBM)
    pairs = lax.axis_size("tp") // 2
    return pl.pallas_call(
        functools.partial(kernel, which),
        grid_spec=pltpu.PrefetchScalarGridSpec(
            num_scalar_prefetch=1,
            grid=(1,),
            in_specs=[anywhere] * len(arrays),
            out_specs=specs + [anywhere] * len(which),
            scratch_shapes=[pltpu.SemaphoreType.DMA((copies,))],
        ),
        out_shape=extra + [jax.ShapeDtypeStruct((rows, d // pairs), arrays[0].dtype)] * len(which),
        compiler_params=pltpu.CompilerParams(vmem_limit_bytes=4 * MIB),
        cost_estimate=LIGHT,
        name=name,
    )(place, *map(stay, arrays))


def near_sends(place, w_out, x):
    tail = jax.ShapeDtypeStruct((16, x.shape[1]), x.dtype)
    spec = pl.BlockSpec(memory_space=pltpu.HBM)
    return copied(near_kernel, (1, 2), place, (w_out, x), [tail], [spec], 3, "near_sends")


def rest_sends(place, w_out, w_in, x):
    pairs = lax.axis_size("tp") // 2
    which = tuple(range(3, pairs))
    blocks = jax.ShapeDtypeStruct((pairs, w_in.shape[0] // (2 * pairs), w_in.shape[1]), w_in.dtype)
    specs = [pl.BlockSpec(memory_space=pltpu.HBM), KEPT]
    extra = [blocks, kept((CH, x.shape[1]), x.dtype)]
    return copied(
        rest_kernel, which, place, (w_out, w_in, x), extra, specs, len(which) + pairs + 1, "rest_sends"
    )


def shifted(array, by):
    count = lax.axis_size("seq")
    pairs = [(i, i + by) for i in range(count) if 0 <= i + by < count]
    return lax.ppermute(array, "seq", pairs)


def from_others(part, sign):
    return [shifted(part, sign * step) for step in range(1, lax.axis_size("seq"))]


def out_kernel(count, sw, place_ref, *refs):
    tops, lows, ws = refs[:count], refs[count : 2 * count], refs[2 * count : 3 * count]
    send_ref, keep_ref = refs[3 * count :]
    c = pl.program_id(0)
    half_chunks = pl.num_programs(0) // 2
    odd = place_ref[1] == 1

    def product(parts):
        total = None
        for part, w in zip(parts, ws):
            one = mm(part[...], w[...])
            total = one if total is None else total + one
        first, second = total[:, :sw], total[:, sw:]
        send_ref[rows_at(c), :] = jnp.where(odd, first, second).astype(BF)
        keep_ref[rows_at(c), :] = jnp.where(odd, second, first)

    @pl.when(c < half_chunks)
    def _():
        product(tops)

    @pl.when(c >= half_chunks)
    def _():
        product(lows)


def out_part(place, tops, lows, ws):
    count = len(ws)
    rows = 2 * CH * (lows[0][1] // CH)
    wide = tops[0][0].shape[1]
    sw = ws[1].shape[1] // 2
    part = rows // (2 * CH)
    operands, specs = [], []
    for array, start in tops:
        operands.append(array)
        specs.append(
            pl.BlockSpec((CH, wide), lambda c, place, s=start // CH: (s + jnp.minimum(c, part - 1), 0))
        )
    for array, start in lows:
        operands.append(array)
        specs.append(
            pl.BlockSpec((CH, wide), lambda c, place, s=start // CH: (s + jnp.maximum(c - part, 0), 0))
        )
    return pl.pallas_call(
        functools.partial(out_kernel, count, sw),
        grid_spec=pltpu.PrefetchScalarGridSpec(
            num_scalar_prefetch=1,
            grid=(rows // CH,),
            in_specs=specs
            + [pl.BlockSpec((wide, 2 * sw), lambda c, place: (0, place[0]))]
            + [pl.BlockSpec((wide, 2 * sw), lambda c, place: (0, 0))] * (count - 1),
            out_specs=[KEPT, KEPT],
        ),
        out_shape=[kept((rows, sw), BF), kept((rows, sw), F32)],
        compiler_params=params(16),
        cost_estimate=cost(16 << 30),
        name="out_part",
    )(place, *operands, *map(stay, ws))


def complete_kernel(dp_ref, last_ref, after_ref, cw_ref, low_ref):
    half = low_ref.shape[0]
    low_ref[...] = dp_ref[half:, :]
    row = lax.broadcasted_iota(jnp.int32, last_ref.shape, 0)
    a0, a1 = after_ref[0:1], after_ref[1:2]
    one = cw_ref[2:3] * a0
    two = cw_ref[1:2] * a0 + cw_ref[2:3] * a1
    tail = last_ref[...] + jnp.where(row == 14, one, 0.0) + jnp.where(row == 15, two, 0.0)
    low_ref[half - 16 :, :] = tail.astype(BF)


def complete(dp, last, after, conv_w):
    rows, width = dp.shape
    return pl.pallas_call(
        complete_kernel,
        in_specs=[KEPT] * 4,
        out_specs=KEPT,
        out_shape=kept((rows // 2, width), BF),
        compiler_params=pltpu.CompilerParams(vmem_limit_bytes=4 * MIB),
        cost_estimate=LIGHT,
        name="complete",
    )(keep(dp), keep(last), after, conv_w)


def grad_kernel(count, low_first, place_ref, dp_ref, other_ref, w_ref, w_other_ref, send_ref, keep_ref, both):
    r = pl.program_id(0)
    half, sw = send_ref.shape[1:]
    width = w_ref.shape[1]

    @pl.when(r == 0)
    def _():
        both[:, :width] = dp_ref[...]
        both[:, width:] = other_ref[...]

    block = 2 * lax.bitwise_xor(place_ref[0], r) + place_ref[1]
    w = w_ref[pl.ds(pl.multiple_of(block * sw, sw), sw), :]
    total = mm_nt(both[...], jnp.concatenate([w, w_other_ref[r]], 1)).astype(BF)
    part = count // 2
    leaves = (r % 2 == 1) if low_first else (r >= part)

    @pl.when(leaves)
    def _():
        send_ref[r // 2 if low_first else r - part] = total

    @pl.when(jnp.logical_not(leaves))
    def _():
        keep_ref[r // 2 if low_first else r] = total


def grad_part(place, dp, other, w_in, w_other, low_first):
    half, width = dp.shape
    count, sw = w_other.shape[:2]
    return pl.pallas_call(
        functools.partial(grad_kernel, count, low_first),
        grid_spec=pltpu.PrefetchScalarGridSpec(
            num_scalar_prefetch=1,
            grid=(count,),
            in_specs=[KEPT] * 4,
            out_specs=[KEPT] * 2,
            scratch_shapes=[pltpu.VMEM((half, 2 * width), BF)],
        ),
        out_shape=[kept((count // 2, half, sw), BF)] * 2,
        compiler_params=params(5),
        cost_estimate=LIGHT,
        name="grad_part",
    )(place, *map(keep, (dp, other, w_in, w_other)))


def halves_kernel(x_ref, y_ref, x_top_ref, y_low_ref):
    half = x_top_ref.shape[0]
    x_top_ref[...] = x_ref[:half, :]
    y_low_ref[...] = y_ref[half:, :]


def halves(x_got, y_got):
    rows, wide = x_got.shape
    return pl.pallas_call(
        halves_kernel,
        in_specs=[KEPT] * 2,
        out_specs=[KEPT] * 2,
        out_shape=[kept((rows // 2, wide), BF)] * 2,
        compiler_params=pltpu.CompilerParams(vmem_limit_bytes=4 * MIB),
        cost_estimate=LIGHT,
        name="halves",
    )(keep(x_got), keep(y_got))


def swapped(array, distance):
    count = lax.axis_size("tp")
    return lax.ppermute(array, "tp", [(i, i ^ distance) for i in range(count)])


def summed(a, b):
    return a.astype(F32) + b.astype(F32)


def passing_kernel(places, *refs):
    ins, out_ref = refs[:-1], refs[-1]
    for i in range(out_ref.shape[0]):
        total = None
        for ref, place in zip(ins, places):
            one = ref[place[i]].astype(F32)
            total = one if total is None else total + one
        out_ref[i] = total.astype(BF)


def passing(terms, blocks):
    places = [[place[i] for i in blocks] for _, place in terms]
    return pl.pallas_call(
        functools.partial(passing_kernel, places),
        in_specs=[KEPT] * len(terms),
        out_specs=KEPT,
        out_shape=kept((len(blocks),) + terms[0][0].shape[1:], BF),
        compiler_params=pltpu.CompilerParams(vmem_limit_bytes=4 * MIB),
        cost_estimate=LIGHT,
        name="passing",
    )(*[keep(array) for array, _ in terms])


def reduce_both(a_send, a_keep, b_send, b_keep, meanwhile):
    pairs = lax.axis_size("tp") // 2
    a_step, b_step = 1, pairs // 2
    left = pairs // 2
    a_terms, b_terms = [(a_keep, list(range(left)))], [(b_keep, list(range(left)))]
    while True:
        a_got, b_got = swapped(a_send, 2 * a_step), swapped(b_send, 2 * b_step)
        a_got, b_got = meanwhile(a_got, b_got)
        a_terms.append((a_got, list(range(left))))
        b_terms.append((b_got, list(range(left))))
        if left == 1:
            return a_terms, b_terms
        half = left // 2
        a_send = passing(a_terms, list(range(1, left, 2)))
        b_send = passing(b_terms, list(range(half, left)))
        a_terms = [(array, place[0::2]) for array, place in a_terms]
        b_terms = [(array, place[:half]) for array, place in b_terms]
        left = half
        a_step, b_step = a_step * 2, b_step // 2


def own_kernel(place_ref, x_ref, ct_ref, x_own_ref, ct_own_ref, sems):
    sw = x_own_ref.shape[1]
    at = pl.ds(pl.multiple_of(place_ref[2] * sw, sw), sw)
    copies = [
        pltpu.make_async_copy(x_ref.at[:, at], x_own_ref, sems.at[0]),
        pltpu.make_async_copy(ct_ref.at[:, at], ct_own_ref, sems.at[1]),
    ]
    for copy in copies:
        copy.start()
    for copy in copies:
        copy.wait()


def own_columns(place, x, ct, sw):
    rows = x.shape[0]
    anywhere = pl.BlockSpec(memory_space=pltpu.HBM)
    return pl.pallas_call(
        own_kernel,
        grid_spec=pltpu.PrefetchScalarGridSpec(
            num_scalar_prefetch=1,
            grid=(1,),
            in_specs=[anywhere] * 2,
            out_specs=[KEPT] * 2,
            scratch_shapes=[pltpu.SemaphoreType.DMA((2,))],
        ),
        out_shape=[kept((rows, sw), x.dtype)] * 2,
        compiler_params=pltpu.CompilerParams(vmem_limit_bytes=4 * MIB),
        cost_estimate=LIGHT,
        name="own_columns",
    )(place, stay(x), stay(ct))


def finish_kernel(places, own_ref, *refs):
    tops, lows, out_ref = refs[: len(places)], refs[len(places) : -1], refs[-1]
    half = out_ref.shape[0] // 2
    for first, ins in ((0, tops), (half, lows)):
        total = own_ref[first : first + half, :].astype(F32)
        for ref, place in zip(ins, places):
            total = total + ref[place].astype(F32)
        out_ref[first : first + half, :] = total.astype(BF)


def partial_kernel(places, own_ref, *refs):
    tops, lows, out_ref = refs[: len(places)], refs[len(places) : -1], refs[-1]
    half = out_ref.shape[0] // 2
    for first, ins in ((0, tops), (half, lows)):
        total = own_ref[first : first + half, :].astype(F32)
        for ref, place in zip(ins, places):
            total = total + ref[place].astype(F32)
        out_ref[first : first + half, :] = total


def partial_sum(own, a_terms, b_terms):
    places = [index[0] for _, index in a_terms]
    terms = [array for array, _ in a_terms + b_terms]
    return pl.pallas_call(
        functools.partial(partial_kernel, places),
        in_specs=[KEPT] * (1 + len(terms)),
        out_specs=KEPT,
        out_shape=kept(own.shape, F32),
        compiler_params=pltpu.CompilerParams(vmem_limit_bytes=6 * MIB),
        cost_estimate=LIGHT,
        name="partial_sum",
    )(*map(keep, [own] + terms))


def finish(own, a_terms, b_terms):
    places = [index[0] for _, index in a_terms]
    assert places == [index[0] for _, index in b_terms]
    terms = [array for array, _ in a_terms + b_terms]
    return pl.pallas_call(
        functools.partial(finish_kernel, places),
        in_specs=[KEPT] * (1 + len(terms)),
        out_shape=jax.ShapeDtypeStruct(own.shape, BF),
        compiler_params=pltpu.CompilerParams(vmem_limit_bytes=6 * MIB),
        cost_estimate=LIGHT,
        name="finish",
    )(*map(keep, [own] + terms))


def finish_out_kernel(own_ref, keep_ref, got_ref, out_ref):
    out_ref[...] = (own_ref[...].astype(F32) + keep_ref[...] + got_ref[...].astype(F32)).astype(BF)


def finish_out(own, kept_part, got):
    return pl.pallas_call(
        finish_out_kernel,
        in_specs=[KEPT] * 3,
        out_shape=jax.ShapeDtypeStruct(own.shape, BF),
        compiler_params=pltpu.CompilerParams(vmem_limit_bytes=6 * MIB),
        cost_estimate=LIGHT,
        name="finish_out",
    )(*map(keep, (own, kept_part, got)))


def per_device(inputs, cotangent, w_in, conv_w, norm_gain, w_out, keep_flags):
    heads = keep_flags.shape[0]
    sel, bias = selectors(heads)
    tp = lax.axis_size("tp")
    pairs = tp // 2
    me = lax.axis_index("tp")
    pair = me // 2
    place = jnp.stack([pair, me % 2, me]).astype(jnp.int32)
    gain = (norm_gain.reshape(heads, DV) * keep_flags.astype(F32)[:, None]).reshape(1, heads * DV)

    half = inputs.shape[0] // 2
    tail, *near = near_sends(place, w_out, inputs)
    halo = shifted(tail, 1)
    near = [swapped(one, 2 * m) for m, one in enumerate(near, 1)]
    w_other, x_first, *far = rest_sends(place, w_out, w_in, inputs)
    w_other = swapped(w_other, 1)
    halo, place, gain, far = lax.optimization_barrier((halo, place, gain, far))
    v, pq, pk, fq, fk, loc, ct_first, state = project(
        inputs, x_first, cotangent, halo, w_in, conv_w, sel, bias, heads)
    state, w_other = lax.optimization_barrier((state, w_other))
    before = from_others(state, 1)
    v, near, far = lax.optimization_barrier((v, near, far))
    far = [swapped(one, 2 * m) for m, one in enumerate(far, 3)]
    g, num, wt, slope = local_part(cotangent, ct_first, w_out, gain, v, pq, pk, loc, fq, fk, sel, heads)
    ho, dn, gloc, pre, gstate = norm_part(
        g, num, gain, pq, before, (v, pk, fq, fk, wt, slope, loc, sel), heads
    )
    step = pairs // 2
    got = {r: swapped(ho, 2 * r) for r in range(1, pairs) if r != 1 + step}
    later = from_others(gstate, -1)
    pre, far = lax.optimization_barrier((pre, far))
    dqk, dv, xk = inner_part(v, pq, pk, fq, wt, slope, dn, loc, pre, sel, fk, gloc, heads)
    dp_top, dp, first, last = outer_part(v, pk, fk, dqk, dv, xk, gloc, later, sel, conv_w, heads)
    other_top = swapped(dp_top, 1)
    after = shifted(first, -1)
    a_send, a_keep = grad_part(place, dp_top, other_top, w_in, w_other, True)
    dp_low = complete(dp, last, after, conv_w)
    other_low = swapped(dp_low, 1)
    x_top, y_low = halves(got[1], got[step])
    x_top, y_low = swapped(x_top, 2 * step), swapped(y_low, 2)
    b_send, b_keep = grad_part(place, dp_low, other_low, w_in, w_other, False)
    tops = [(ho, 0)] + [(got.get(r, x_top), 0) for r in range(1, pairs)]
    lows = [(ho, half)] + [(got[r], half) if r in got else (y_low, 0) for r in range(1, pairs)]
    w_cols = [w_out] + near + far
    place_, b_keep = lax.optimization_barrier((place, b_keep))
    stage = []

    def meanwhile(a_got, b_got):
        if not stage:
            out_send, out_keep = out_part(place, tops, lows, w_cols)
            own = own_columns(place_, inputs, cotangent, inputs.shape[1] // tp)
            out_got = swapped(out_send, 1)
            a_got, b_got, out_keep = lax.optimization_barrier((a_got, b_got, out_keep))
            stage.extend([*own, out_keep, out_got])
        elif len(stage) == 4:
            stage.append(finish_out(stage[0], *stage[2:]))
            a_got, b_got, stage[4] = lax.optimization_barrier((a_got, b_got, stage[4]))
        return a_got, b_got

    a_terms, b_terms = reduce_both(a_send, a_keep, b_send, b_keep, meanwhile)
    rest = partial_sum(stage[1], a_terms[:-1], b_terms[:-1])
    rest, a_got, b_got = lax.optimization_barrier((rest, a_terms[-1][0], b_terms[-1][0]))
    return stage[4], finish(rest, [(a_got, a_terms[-1][1])], [(b_got, b_terms[-1][1])])


def solution(mesh):
    placed = (
        P("seq", None),
        P("seq", None),
        P(None, "tp"),
        P(None, "tp"),
        P("tp"),
        P("tp", None),
        P("tp"),
    )
    return jax.shard_map(
        per_device,
        mesh=mesh,
        in_specs=placed,
        out_specs=(P("seq", "tp"), P("seq", "tp")),
        check_vma=False,
    )
```

```python
import functools

import jax
import jax.numpy as jnp
import numpy as np
from jax import lax
from jax.experimental import pallas as pl
from jax.experimental.pallas import tpu as pltpu
from jax.sharding import PartitionSpec as P

FEAT = 16
DV = 128
HW = 2 * FEAT + DV
EP = 256
ES = 160
CH = 256
EPS = 1e-06
BF = jnp.bfloat16
F32 = jnp.float32
MIB = 1024 * 1024


def mm(a, b):
    return lax.dot_general(a, b, (((1,), (0,)), ((), ())), preferred_element_type=F32)


def mm_nt(a, b):
    return lax.dot_general(a, b, (((1,), (1,)), ((), ())), preferred_element_type=F32)


def mm_tn(a, b):
    return lax.dot_general(a, b, (((0,), (0,)), ((), ())), preferred_element_type=F32)


def selectors(heads):
    sel = np.zeros((heads, 128, 4 * EP), np.float32)
    bias = np.zeros((8, EP), np.float32)
    bias[1, :FEAT] = 1.0
    bias[0, FEAT] = bias[1, FEAT] = 1.0
    for h in range(heads):
        q0 = (HW * h) % 128
        k0 = q0 + FEAT
        for i in range(FEAT):
            sel[h, q0 + i, i] = 0.5
            sel[h, k0 + i, 2 * EP + i] = 0.5
        col = FEAT + 1
        for i in range(FEAT):
            for j in range(i, FEAT):
                sel[h, q0 + i, col] = 0.25 if i == j else 0.5
                sel[h, q0 + j, EP + col] = 0.5
                sel[h, k0 + i, 2 * EP + col] = 0.5
                sel[h, k0 + j, 3 * EP + col] = 0.5
                col += 1
    return jnp.asarray(sel, BF), jnp.asarray(bias, F32)


def window(h):
    t = (HW * h) // 128
    return slice(128 * t, 128 * t + 128)


def value_place(h):
    start = HW * h + 2 * FEAT
    return start // 128, start % 128


def lane_iota():
    return lax.broadcasted_iota(jnp.int32, (CH, 128), 1)


def take_values(conv, h):
    tile, off = value_place(h)
    first = conv[:, 128 * tile : 128 * tile + 128]
    if off == 0:
        return first
    second = conv[:, 128 * tile + 128 : min(128 * tile + 256, conv.shape[1])]
    if second.shape[1] < 128:
        second = jnp.concatenate([second, jnp.zeros((CH, 128 - second.shape[1]), second.dtype)], 1)
    a = pltpu.roll(first, 128 - off, 1)
    b = pltpu.roll(second, 128 - off, 1)
    return jnp.where(lane_iota() < 128 - off, a, b)


def causal():
    r = lax.broadcasted_iota(jnp.int32, (CH, CH), 0)
    c = lax.broadcasted_iota(jnp.int32, (CH, CH), 1)
    return r >= c


def params(mib):
    return pltpu.CompilerParams(dimension_semantics=("arbitrary",), vmem_limit_bytes=mib * MIB)


def whole(shape):
    return pl.BlockSpec(shape, lambda c, *_: (0,) * len(shape))


KEPT = pl.BlockSpec(memory_space=pltpu.VMEM)


def kept(shape, dtype):
    return pltpu.VMEM(shape, dtype)


def keep(array):
    return pltpu.with_memory_space_constraint(array, pltpu.VMEM)


def stay(array):
    return pltpu.with_memory_space_constraint(array, pltpu.HBM)


def cost(flops):
    return pl.CostEstimate(flops=int(flops), bytes_accessed=1 << 20, transcendentals=0)


LIGHT = cost(1000)


def rows_at(c):
    return pl.ds(pl.multiple_of(c * CH, CH), CH)


def biased(u, bias):
    return jnp.concatenate([u[:, :128] + bias[:, :128], u[:, 128:]], 1)


def with_rows(hbm_ref, first_ref, buf, sems, use):
    c = pl.program_id(0)

    def fetch(k):
        slot = lax.rem(k, 2)
        return pltpu.make_async_copy(hbm_ref.at[rows_at(k), :], buf.at[slot], sems.at[slot])

    @pl.when(c == 0)
    def _():
        fetch(1).start()
        use(first_ref[...])

    @pl.when(c >= 1)
    def _():
        fetch(c).wait()

        @pl.when(c + 1 < pl.num_programs(0))
        def _():
            fetch(c + 1).start()

        use(buf[lax.rem(c, 2)])


def project_kernel(heads, x_ref, x_first_ref, ct_ref, halo_ref, w_ref, cw_ref, sel_ref, bias_ref,
                   v_ref, pq_ref, pk_ref, fq_ref, fk_ref, loc_ref, ct_first_ref, state_ref, ext, run, buf, sems):
    c = pl.program_id(0)
    at = rows_at(c)
    last = pl.num_programs(0) - 1
    ct_copy = pltpu.make_async_copy(ct_ref.at[pl.ds(0, CH), :], ct_first_ref, sems.at[2])

    @pl.when(c == 0)
    def _():
        before = mm(halo_ref[...], w_ref[...]).astype(BF).astype(F32)
        ext[0:8, :] = before[8:16]
        run[...] = jnp.zeros_like(run)

    @pl.when(c == last)
    def _():
        ct_copy.start()

    def product(rows):
        ext[8:, :] = mm(rows, w_ref[...]).astype(BF).astype(F32)

    with_rows(x_ref, x_first_ref, buf, sems, product)
    conv = (cw_ref[0:1] * ext[8 : 8 + CH, :] + cw_ref[1:2] * ext[7 : 7 + CH, :]
            + cw_ref[2:3] * ext[6 : 6 + CH, :])
    ext[0:8, :] = ext[CH : CH + 8, :]
    conv_b = conv.astype(BF)
    conv = conv_b.astype(F32)
    b0 = bias_ref[0:1]
    b1 = bias_ref[1:2]
    for h in range(heads):
        u = mm(conv_b[:, window(h)], sel_ref[h])
        first, second = biased(u[:, :EP], b0), biased(u[:, EP : 2 * EP], b1)
        pq_ref[h, at, :] = (first * second).astype(BF)
        fq_ref[h, at, :EP] = first.astype(BF)
        fq_ref[h, at, EP:] = second.astype(BF)
        first, second = biased(u[:, 2 * EP : 3 * EP], b0), biased(u[:, 3 * EP :], b1)
        pk = (first * second).astype(BF)
        pk_ref[h, at, :] = pk
        fk_ref[h, at, :EP] = first.astype(BF)
        fk_ref[h, at, EP:] = second.astype(BF)
        v = take_values(conv, h).astype(BF)
        v_ref[at, DV * h : DV * h + DV] = v
        loc_ref[c, h] = run[h].astype(BF)
        run[h] = run[h] + mm_tn(v, pk)

    @pl.when(c == last)
    def _():
        for h in range(heads):
            state_ref[h] = run[h].T[:ES].astype(BF)
        ct_copy.wait()


def project(x, x_first, ct, halo, w_in, conv_w, sel, bias, heads):
    rows, d = x.shape
    width = w_in.shape[1]
    n = rows // CH
    return pl.pallas_call(
        functools.partial(project_kernel, heads),
        grid=(n,),
        in_specs=[
            pl.BlockSpec(memory_space=pltpu.HBM),
            KEPT,
            pl.BlockSpec(memory_space=pltpu.HBM),
            whole((16, d)),
            KEPT,
            whole((3, width)),
            KEPT,
            whole(bias.shape),
        ],
        out_specs=[KEPT] * 7 + [whole((heads, ES, DV))],
        out_shape=[
            kept((rows, heads * DV), BF),
            kept((heads, rows, EP), BF),
            kept((heads, rows, EP), BF),
            kept((heads, rows, 2 * EP), BF),
            kept((heads, rows, 2 * EP), BF),
            kept((n, heads, DV, EP), BF),
            kept((CH, d), BF),
            jax.ShapeDtypeStruct((heads, ES, DV), BF),
        ],
        scratch_shapes=[
            pltpu.VMEM((CH + 8, width), F32),
            pltpu.VMEM((heads, DV, EP), F32),
            pltpu.VMEM((2, CH, d), BF),
            pltpu.SemaphoreType.DMA((3,)),
        ],
        compiler_params=params(9),
        cost_estimate=cost(100 << 30),
        name="project",
    )(stay(x), keep(x_first), stay(ct), halo, keep(w_in), conv_w, keep(sel), bias)


def local_kernel(heads, ct_ref, ct_first_ref, wo_ref, gain_ref, v_ref, pq_ref, pk_ref, loc_ref, fq_ref, fk_ref, sel_ref,
                 g_ref, num_ref, wt_ref, slope_ref, buf, sems):
    c = pl.program_id(0)
    at = rows_at(c)

    def product(rows):
        g_ref[at, :] = mm_nt(rows, wo_ref[...]) * gain_ref[...]

    with_rows(ct_ref, ct_first_ref, buf, sems, product)
    mask = causal()
    for h in range(heads):
        pq = pq_ref[h, at, :]
        logits = mm_nt(pq[:, :FEAT], pk_ref[h, at, :FEAT])
        slope = 1.0 + logits
        weights = jnp.where(mask, 0.5 + 0.5 * slope * slope, 0.0).astype(BF)
        wt_ref[h, at, :] = weights
        slope_ref[h, at, :] = jnp.where(mask, slope, 0.0).astype(BF)
        lanes = slice(DV * h, DV * h + DV)
        num_ref[at, lanes] = mm(weights, v_ref[at, lanes]) + mm_nt(pq, loc_ref[c, h])


def local_part(ct, ct_first, w_out, gain, v, pq, pk, loc, fq, fk, sel, heads):
    rows, d = ct.shape
    n = rows // CH
    wide = heads * DV
    return pl.pallas_call(
        functools.partial(local_kernel, heads),
        grid=(n,),
        in_specs=[pl.BlockSpec(memory_space=pltpu.HBM), KEPT, KEPT, whole((1, wide))] + [KEPT] * 7,
        out_specs=[KEPT] * 4,
        out_shape=[kept((rows, wide), F32)] * 2 + [kept((heads, rows, CH), BF)] * 2,
        scratch_shapes=[pltpu.VMEM((2, CH, d), BF), pltpu.SemaphoreType.DMA((2,))],
        compiler_params=params(8),
        cost_estimate=LIGHT,
        name="local_part",
    )(stay(ct), keep(ct_first), keep(w_out), gain, *map(keep, (v, pq, pk, loc, fq, fk, sel)))


def norm_kernel(heads, parts, passed, g_ref, num_ref, gain_ref, pq_ref, ones_ref, *refs):
    got = refs[:parts]
    ho_ref, dn_ref, loc_ref, pre_ref, state_ref, run = refs[parts + passed :]
    step = pl.program_id(0)
    c = pl.num_programs(0) - 1 - step
    at = rows_at(c)

    @pl.when(step == 0)
    def _():
        run[...] = jnp.zeros_like(run)
        total = got[0][...].astype(F32)
        for one in got[1:]:
            total = total + one[...].astype(F32)
        pre_ref[...] = total.astype(BF)

    for h in range(0, heads, 2):
        lanes = slice(DV * h, DV * h + 2 * DV)
        pqs = [pq_ref[h, at, :], pq_ref[h + 1, at, :]]
        num = num_ref[at, lanes] + jnp.concatenate(
            [mm(pqs[0][:, :ES], pre_ref[h]), mm(pqs[1][:, :ES], pre_ref[h + 1])], 1
        )
        inv = lax.rsqrt(mm((num * num).astype(BF), ones_ref[...]) + EPS)
        normed = num * inv
        ho_ref[at, lanes] = (normed * gain_ref[:, lanes]).astype(BF)
        g = g_ref[at, lanes]
        dn = ((g - normed * mm((g * normed).astype(BF), ones_ref[...])) * inv).astype(BF)
        dn_ref[at, lanes] = dn
        for i in range(2):
            loc_ref[c, h + i] = run[h + i].astype(BF)
            run[h + i] = run[h + i] + mm_tn(dn[:, DV * i : DV * i + DV], pqs[i])

    @pl.when(step == pl.num_programs(0) - 1)
    def _():
        for h in range(heads):
            state_ref[h] = run[h].T[:ES].astype(BF)


def norm_part(g, num, gain, pq, got, later, heads):
    ones = jnp.asarray(np.kron(np.eye(2), np.full((DV, DV), 1.0 / DV)), BF)
    rows, wide = g.shape
    n = rows // CH
    return pl.pallas_call(
        functools.partial(norm_kernel, heads, len(got), len(later)),
        grid=(n,),
        in_specs=[KEPT, KEPT, whole((1, wide)), KEPT, whole((2 * DV, 2 * DV))]
        + [whole((heads, ES, DV))] * len(got)
        + [KEPT] * len(later),
        out_specs=[KEPT] * 4 + [whole((heads, ES, DV))],
        out_shape=[
            kept((rows, wide), BF),
            kept((rows, wide), BF),
            kept((n, heads, DV, EP), BF),
            kept((heads, ES, DV), BF),
            jax.ShapeDtypeStruct((heads, ES, DV), BF),
        ],
        scratch_shapes=[pltpu.VMEM((heads, DV, EP), F32)],
        compiler_params=params(5),
        cost_estimate=cost(16 << 30),
        name="norm_part",
    )(keep(g), keep(num), gain, keep(pq), ones, *got, *map(keep, later))


def inner_kernel(heads, v_ref, pq_ref, pk_ref, fq_ref, wt_ref, slope_ref, dn_ref, loc_ref, pre_ref, sel_ref,
                 fk_ref, gloc_ref, dqk_ref, dv_ref, xk_ref, pre_t):
    c = pl.program_id(0)
    at = rows_at(c)

    @pl.when(c == 0)
    def _():
        pre_t[...] = jnp.zeros_like(pre_t)
        for h in range(heads):
            pre_t[h, :, :ES] = pre_ref[h].astype(F32).T

    linear = lane_iota() < FEAT
    dqk = None
    for h in range(heads):
        lanes = slice(DV * h, DV * h + DV)
        dn = dn_ref[at, lanes]
        dv_ref[at, lanes] = mm_tn(wt_ref[h, at, :], dn)
        dl = (mm_nt(dn, v_ref[at, lanes]) * slope_ref[h, at, :].astype(F32)).astype(BF)
        xk_ref[h, at, :] = mm_tn(dl, pq_ref[h, at, :128])
        state = (loc_ref[c, h].astype(F32) + pre_t[h]).astype(BF)
        dphi = mm(dn, state)
        dphi = jnp.concatenate(
            [dphi[:, :128] + jnp.where(linear, mm(dl, pk_ref[h, at, :128]), 0.0), dphi[:, 128:]], 1
        )
        da = (dphi * fq_ref[h, at, EP:].astype(F32)).astype(BF)
        db = (dphi * fq_ref[h, at, :EP].astype(F32)).astype(BF)
        part = mm_nt(da, sel_ref[h, :, :EP]) + mm_nt(db, sel_ref[h, :, EP : 2 * EP])
        dqk = part if dqk is None else dqk + part
    dqk_ref[at, :] = dqk


def inner_part(v, pq, pk, fq, wt, slope, dn, loc, pre, sel, fk, gloc, heads):
    rows = v.shape[0]
    n = rows // CH
    return pl.pallas_call(
        functools.partial(inner_kernel, heads),
        grid=(n,),
        in_specs=[KEPT] * 12,
        out_specs=[KEPT] * 3,
        out_shape=[
            kept((rows, 128), F32),
            kept((rows, heads * DV), F32),
            kept((heads, rows, 128), F32),
        ],
        scratch_shapes=[pltpu.VMEM((heads, DV, EP), F32)],
        compiler_params=params(5),
        cost_estimate=LIGHT,
        name="inner_part",
    )(*map(keep, (v, pq, pk, fq, wt, slope, dn, loc, pre, sel, fk, gloc)))


def outer_kernel(heads, parts, v_ref, pk_ref, fk_ref, dqk_ref, dv_ref, xk_ref, loc_ref, sel_ref, cw_ref, *refs):
    got = refs[:parts]
    top_ref, dp_ref, first_ref, last_ref, ext, suf_t = refs[parts:]
    half_chunks = pl.num_programs(0) // 2
    step = pl.program_id(0)
    c = pl.num_programs(0) - 1 - step
    at = rows_at(c)
    width = cw_ref.shape[1]

    @pl.when(step == 0)
    def _():
        suf_t[...] = jnp.zeros_like(suf_t)
        for h in range(heads):
            total = got[0][h].astype(F32)
            for one in got[1:]:
                total = total + one[h].astype(F32)
            suf_t[h, :, :ES] = total.T
        ext[CH:, :] = jnp.zeros((8, width), F32)

    lane = lane_iota()
    tiles = [None] * (-(-width // 128))

    def put(t, piece):
        tiles[t] = piece if tiles[t] is None else tiles[t] + piece

    dqk = dqk_ref[at, :]
    for h in range(heads):
        lanes = slice(DV * h, DV * h + DV)
        state = (loc_ref[c, h].astype(F32) + suf_t[h]).astype(BF)
        dphi = mm(v_ref[at, lanes], state)
        dphi = jnp.concatenate(
            [dphi[:, :128] + jnp.where(lane < FEAT, xk_ref[h, at, :], 0.0), dphi[:, 128:]], 1
        )
        da = (dphi * fk_ref[h, at, EP:].astype(F32)).astype(BF)
        db = (dphi * fk_ref[h, at, :EP].astype(F32)).astype(BF)
        own = (
            dqk
            + mm_nt(da, sel_ref[h, :, 2 * EP : 3 * EP])
            + mm_nt(db, sel_ref[h, :, 3 * EP : 4 * EP])
        )
        q0 = (HW * h) % 128
        put((HW * h) // 128, jnp.where((lane >= q0) & (lane < q0 + 2 * FEAT), own, 0.0))
        dv = dv_ref[at, lanes] + mm_nt(pk_ref[h, at, :], state)
        tile, off = value_place(h)
        if off == 0:
            put(tile, dv)
        else:
            moved = pltpu.roll(dv, off, 1)
            put(tile, jnp.where(lane >= off, moved, 0.0))
            put(tile + 1, jnp.where(lane < off, moved, 0.0))
    for t, tile in enumerate(tiles):
        end = min(128 * t + 128, width)
        ext[:CH, 128 * t : end] = tile[:, : end - 128 * t]
    dp = (cw_ref[0:1] * ext[:CH, :] + cw_ref[1:2] * ext[1 : CH + 1, :]
          + cw_ref[2:3] * ext[2 : CH + 2, :])
    dp_ref[at, :] = dp.astype(BF)

    @pl.when(c < half_chunks)
    def _():
        top_ref[at, :] = dp.astype(BF)

    @pl.when(step == 0)
    def _():
        last_ref[...] = dp[CH - 16 :]

    ext[CH:, :] = ext[0:8, :]
    first_ref[...] = ext[0:8, :]


def outer_part(v, pk, fk, dqk, dv, xk, loc, got, sel, conv_w, heads):
    rows, width = v.shape[0], conv_w.shape[1]
    n = rows // CH
    return pl.pallas_call(
        functools.partial(outer_kernel, heads, len(got)),
        grid=(n,),
        in_specs=[KEPT] * 8 + [whole((3, width))] + [whole((heads, ES, DV))] * len(got),
        out_specs=[KEPT, KEPT, whole((8, width)), KEPT],
        out_shape=[
            kept((rows // 2, width), BF),
            kept((rows, width), BF),
            jax.ShapeDtypeStruct((8, width), F32),
            kept((16, width), F32),
        ],
        scratch_shapes=[pltpu.VMEM((CH + 8, width), F32), pltpu.VMEM((heads, DV, EP), F32)],
        compiler_params=params(5),
        cost_estimate=cost(16 << 30),
        name="outer_part",
    )(*map(keep, (v, pk, fk, dqk, dv, xk, loc, sel)), conv_w, *got)


def run_copies(copies, sems):
    copies = [pltpu.make_async_copy(*one, sems.at[i]) for i, one in enumerate(copies)]
    for copy in copies:
        copy.start()
    for copy in copies:
        copy.wait()


def column_copies(which, place_ref, w_ref, outs):
    wide = outs[0].shape[1]
    for m, out in zip(which, outs):
        start = pl.multiple_of(lax.bitwise_xor(place_ref[0], m) * wide, wide)
        yield w_ref.at[:, pl.ds(start, wide)], out


def near_kernel(which, place_ref, w_ref, x_ref, tail_ref, *refs):
    rows = tail_ref.shape[0]
    copies = list(column_copies(which, place_ref, w_ref, refs[:-1]))
    copies.append((x_ref.at[pl.ds(x_ref.shape[0] - rows, rows), :], tail_ref))
    run_copies(copies, refs[-1])


def rest_kernel(which, place_ref, w_ref, wi_ref, x_ref, blocks_ref, first_ref, *refs):
    copies = list(column_copies(which, place_ref, w_ref, refs[:-1]))
    count, sw = blocks_ref.shape[:2]
    for r in range(count):
        block = 2 * lax.bitwise_xor(place_ref[0], r) + 1 - place_ref[1]
        copies.append((wi_ref.at[pl.ds(pl.multiple_of(block * sw, sw), sw), :], blocks_ref.at[r]))
    copies.append((x_ref.at[pl.ds(0, CH), :], first_ref))
    run_copies(copies, refs[-1])


def copied(kernel, which, place, arrays, extra, specs, copies, name):
    rows, d = arrays[0].shape
    anywhere = pl.BlockSpec(memory_space=pltpu.HBM)
    pairs = lax.axis_size("tp") // 2
    return pl.pallas_call(
        functools.partial(kernel, which),
        grid_spec=pltpu.PrefetchScalarGridSpec(
            num_scalar_prefetch=1,
            grid=(1,),
            in_specs=[anywhere] * len(arrays),
            out_specs=specs + [anywhere] * len(which),
            scratch_shapes=[pltpu.SemaphoreType.DMA((copies,))],
        ),
        out_shape=extra + [jax.ShapeDtypeStruct((rows, d // pairs), arrays[0].dtype)] * len(which),
        compiler_params=pltpu.CompilerParams(vmem_limit_bytes=4 * MIB),
        cost_estimate=LIGHT,
        name=name,
    )(place, *map(stay, arrays))


def near_sends(place, w_out, x):
    tail = jax.ShapeDtypeStruct((16, x.shape[1]), x.dtype)
    spec = pl.BlockSpec(memory_space=pltpu.HBM)
    return copied(near_kernel, (1, 2), place, (w_out, x), [tail], [spec], 3, "near_sends")


def rest_sends(place, w_out, w_in, x):
    pairs = lax.axis_size("tp") // 2
    which = tuple(range(3, pairs))
    blocks = jax.ShapeDtypeStruct((pairs, w_in.shape[0] // (2 * pairs), w_in.shape[1]), w_in.dtype)
    specs = [pl.BlockSpec(memory_space=pltpu.HBM), KEPT]
    extra = [blocks, kept((CH, x.shape[1]), x.dtype)]
    return copied(
        rest_kernel, which, place, (w_out, w_in, x), extra, specs, len(which) + pairs + 1, "rest_sends"
    )


def shifted(array, by):
    count = lax.axis_size("seq")
    pairs = [(i, i + by) for i in range(count) if 0 <= i + by < count]
    return lax.ppermute(array, "seq", pairs)


def from_others(part, sign):
    steps = range(1, lax.axis_size("seq"))
    return [shifted(part, sign * step) for step in (steps if sign > 0 else reversed(steps))]


def out_kernel(count, sw, place_ref, *refs):
    tops, lows, ws = refs[:count], refs[count : 2 * count], refs[2 * count : 3 * count]
    send_ref, keep_ref = refs[3 * count :]
    c = pl.program_id(0)
    half_chunks = pl.num_programs(0) // 2
    odd = place_ref[1] == 1

    def product(parts):
        total = None
        for part, w in zip(parts, ws):
            one = mm(part[...], w[...])
            total = one if total is None else total + one
        first, second = total[:, :sw], total[:, sw:]
        send_ref[rows_at(c), :] = jnp.where(odd, first, second).astype(BF)
        keep_ref[rows_at(c), :] = jnp.where(odd, second, first)

    @pl.when(c < half_chunks)
    def _():
        product(tops)

    @pl.when(c >= half_chunks)
    def _():
        product(lows)


def out_part(place, tops, lows, ws):
    count = len(ws)
    rows = 2 * CH * (lows[0][1] // CH)
    wide = tops[0][0].shape[1]
    sw = ws[1].shape[1] // 2
    part = rows // (2 * CH)
    operands, specs = [], []
    for array, start in tops:
        operands.append(array)
        specs.append(
            pl.BlockSpec((CH, wide), lambda c, place, s=start // CH: (s + jnp.minimum(c, part - 1), 0))
        )
    for array, start in lows:
        operands.append(array)
        specs.append(
            pl.BlockSpec((CH, wide), lambda c, place, s=start // CH: (s + jnp.maximum(c - part, 0), 0))
        )
    return pl.pallas_call(
        functools.partial(out_kernel, count, sw),
        grid_spec=pltpu.PrefetchScalarGridSpec(
            num_scalar_prefetch=1,
            grid=(rows // CH,),
            in_specs=specs
            + [pl.BlockSpec((wide, 2 * sw), lambda c, place: (0, place[0]))]
            + [pl.BlockSpec((wide, 2 * sw), lambda c, place: (0, 0))] * (count - 1),
            out_specs=[KEPT, KEPT],
        ),
        out_shape=[kept((rows, sw), BF), kept((rows, sw), F32)],
        compiler_params=params(16),
        cost_estimate=cost(16 << 30),
        name="out_part",
    )(place, *operands, *map(stay, ws))


def complete_kernel(dp_ref, last_ref, after_ref, cw_ref, low_ref):
    half = low_ref.shape[0]
    low_ref[...] = dp_ref[half:, :]
    row = lax.broadcasted_iota(jnp.int32, last_ref.shape, 0)
    a0, a1 = after_ref[0:1], after_ref[1:2]
    one = cw_ref[2:3] * a0
    two = cw_ref[1:2] * a0 + cw_ref[2:3] * a1
    tail = last_ref[...] + jnp.where(row == 14, one, 0.0) + jnp.where(row == 15, two, 0.0)
    low_ref[half - 16 :, :] = tail.astype(BF)


def complete(dp, last, after, conv_w):
    rows, width = dp.shape
    return pl.pallas_call(
        complete_kernel,
        in_specs=[KEPT] * 4,
        out_specs=KEPT,
        out_shape=kept((rows // 2, width), BF),
        compiler_params=pltpu.CompilerParams(vmem_limit_bytes=4 * MIB),
        cost_estimate=LIGHT,
        name="complete",
    )(keep(dp), keep(last), after, conv_w)


def grad_kernel(count, low_first, place_ref, dp_ref, other_ref, w_ref, w_other_ref, send_ref, keep_ref, both):
    r = pl.program_id(0)
    half, sw = send_ref.shape[1:]
    width = w_ref.shape[1]

    @pl.when(r == 0)
    def _():
        both[:, :width] = dp_ref[...]
        both[:, width:] = other_ref[...]

    block = 2 * lax.bitwise_xor(place_ref[0], r) + place_ref[1]
    w = w_ref[pl.ds(pl.multiple_of(block * sw, sw), sw), :]
    total = mm_nt(both[...], jnp.concatenate([w, w_other_ref[r]], 1)).astype(BF)
    part = count // 2
    leaves = (r % 2 == 1) if low_first else (r >= part)

    @pl.when(leaves)
    def _():
        send_ref[r // 2 if low_first else r - part] = total

    @pl.when(jnp.logical_not(leaves))
    def _():
        keep_ref[r // 2 if low_first else r] = total


def grad_part(place, dp, other, w_in, w_other, low_first):
    half, width = dp.shape
    count, sw = w_other.shape[:2]
    return pl.pallas_call(
        functools.partial(grad_kernel, count, low_first),
        grid_spec=pltpu.PrefetchScalarGridSpec(
            num_scalar_prefetch=1,
            grid=(count,),
            in_specs=[KEPT] * 4,
            out_specs=[KEPT] * 2,
            scratch_shapes=[pltpu.VMEM((half, 2 * width), BF)],
        ),
        out_shape=[kept((count // 2, half, sw), BF)] * 2,
        compiler_params=params(5),
        cost_estimate=LIGHT,
        name="grad_part",
    )(place, *map(keep, (dp, other, w_in, w_other)))


def halves_kernel(x_ref, y_ref, x_top_ref, y_low_ref):
    half = x_top_ref.shape[0]
    x_top_ref[...] = x_ref[:half, :]
    y_low_ref[...] = y_ref[half:, :]


def halves(x_got, y_got):
    rows, wide = x_got.shape
    return pl.pallas_call(
        halves_kernel,
        in_specs=[KEPT] * 2,
        out_specs=[KEPT] * 2,
        out_shape=[kept((rows // 2, wide), BF)] * 2,
        compiler_params=pltpu.CompilerParams(vmem_limit_bytes=4 * MIB),
        cost_estimate=LIGHT,
        name="halves",
    )(keep(x_got), keep(y_got))


def swapped(array, distance):
    count = lax.axis_size("tp")
    return lax.ppermute(array, "tp", [(i, i ^ distance) for i in range(count)])


def summed(a, b):
    return a.astype(F32) + b.astype(F32)


def passing_kernel(places, *refs):
    ins, out_ref = refs[:-1], refs[-1]
    for i in range(out_ref.shape[0]):
        total = None
        for ref, place in zip(ins, places):
            one = ref[place[i]].astype(F32)
            total = one if total is None else total + one
        out_ref[i] = total.astype(BF)


def passing(terms, blocks):
    places = [[place[i] for i in blocks] for _, place in terms]
    return pl.pallas_call(
        functools.partial(passing_kernel, places),
        in_specs=[KEPT] * len(terms),
        out_specs=KEPT,
        out_shape=kept((len(blocks),) + terms[0][0].shape[1:], BF),
        compiler_params=pltpu.CompilerParams(vmem_limit_bytes=4 * MIB),
        cost_estimate=LIGHT,
        name="passing",
    )(*[keep(array) for array, _ in terms])


def reduce_both(a_send, a_keep, b_send, b_keep, meanwhile):
    pairs = lax.axis_size("tp") // 2
    a_step, b_step = 1, pairs // 2
    left = pairs // 2
    a_terms, b_terms = [(a_keep, list(range(left)))], [(b_keep, list(range(left)))]
    while True:
        a_got, b_got = swapped(a_send, 2 * a_step), swapped(b_send, 2 * b_step)
        a_got, b_got = meanwhile(a_got, b_got)
        a_terms.append((a_got, list(range(left))))
        b_terms.append((b_got, list(range(left))))
        if left == 1:
            return a_terms, b_terms
        half = left // 2
        a_send = passing(a_terms, list(range(1, left, 2)))
        b_send = passing(b_terms, list(range(half, left)))
        a_terms = [(array, place[0::2]) for array, place in a_terms]
        b_terms = [(array, place[:half]) for array, place in b_terms]
        left = half
        a_step, b_step = a_step * 2, b_step // 2


def own_kernel(place_ref, x_ref, ct_ref, x_own_ref, ct_own_ref, sems):
    sw = x_own_ref.shape[1]
    at = pl.ds(pl.multiple_of(place_ref[2] * sw, sw), sw)
    copies = [
        pltpu.make_async_copy(x_ref.at[:, at], x_own_ref, sems.at[0]),
        pltpu.make_async_copy(ct_ref.at[:, at], ct_own_ref, sems.at[1]),
    ]
    for copy in copies:
        copy.start()
    for copy in copies:
        copy.wait()


def own_columns(place, x, ct, sw):
    rows = x.shape[0]
    anywhere = pl.BlockSpec(memory_space=pltpu.HBM)
    return pl.pallas_call(
        own_kernel,
        grid_spec=pltpu.PrefetchScalarGridSpec(
            num_scalar_prefetch=1,
            grid=(1,),
            in_specs=[anywhere] * 2,
            out_specs=[KEPT] * 2,
            scratch_shapes=[pltpu.SemaphoreType.DMA((2,))],
        ),
        out_shape=[kept((rows, sw), x.dtype)] * 2,
        compiler_params=pltpu.CompilerParams(vmem_limit_bytes=4 * MIB),
        cost_estimate=LIGHT,
        name="own_columns",
    )(place, stay(x), stay(ct))


def finish_kernel(places, own_ref, *refs):
    tops, lows, out_ref = refs[: len(places)], refs[len(places) : -1], refs[-1]
    half = out_ref.shape[0] // 2
    for first, ins in ((0, tops), (half, lows)):
        total = own_ref[first : first + half, :].astype(F32)
        for ref, place in zip(ins, places):
            total = total + ref[place].astype(F32)
        out_ref[first : first + half, :] = total.astype(BF)


def partial_kernel(places, own_ref, *refs):
    tops, lows, out_ref = refs[: len(places)], refs[len(places) : -1], refs[-1]
    half = out_ref.shape[0] // 2
    for first, ins in ((0, tops), (half, lows)):
        total = own_ref[first : first + half, :].astype(F32)
        for ref, place in zip(ins, places):
            total = total + ref[place].astype(F32)
        out_ref[first : first + half, :] = total


def partial_sum(own, a_terms, b_terms):
    places = [index[0] for _, index in a_terms]
    terms = [array for array, _ in a_terms + b_terms]
    return pl.pallas_call(
        functools.partial(partial_kernel, places),
        in_specs=[KEPT] * (1 + len(terms)),
        out_specs=KEPT,
        out_shape=kept(own.shape, F32),
        compiler_params=pltpu.CompilerParams(vmem_limit_bytes=6 * MIB),
        cost_estimate=LIGHT,
        name="partial_sum",
    )(*map(keep, [own] + terms))


def finish(own, a_terms, b_terms):
    places = [index[0] for _, index in a_terms]
    assert places == [index[0] for _, index in b_terms]
    terms = [array for array, _ in a_terms + b_terms]
    return pl.pallas_call(
        functools.partial(finish_kernel, places),
        in_specs=[KEPT] * (1 + len(terms)),
        out_shape=jax.ShapeDtypeStruct(own.shape, BF),
        compiler_params=pltpu.CompilerParams(vmem_limit_bytes=6 * MIB),
        cost_estimate=LIGHT,
        name="finish",
    )(*map(keep, [own] + terms))


def finish_out_kernel(own_ref, keep_ref, got_ref, out_ref):
    out_ref[...] = (own_ref[...].astype(F32) + keep_ref[...] + got_ref[...].astype(F32)).astype(BF)


def finish_out(own, kept_part, got):
    return pl.pallas_call(
        finish_out_kernel,
        in_specs=[KEPT] * 3,
        out_shape=jax.ShapeDtypeStruct(own.shape, BF),
        compiler_params=pltpu.CompilerParams(vmem_limit_bytes=6 * MIB),
        cost_estimate=LIGHT,
        name="finish_out",
    )(*map(keep, (own, kept_part, got)))


def per_device(inputs, cotangent, w_in, conv_w, norm_gain, w_out, keep_flags):
    heads = keep_flags.shape[0]
    sel, bias = selectors(heads)
    tp = lax.axis_size("tp")
    pairs = tp // 2
    me = lax.axis_index("tp")
    pair = me // 2
    place = jnp.stack([pair, me % 2, me]).astype(jnp.int32)
    gain = (norm_gain.reshape(heads, DV) * keep_flags.astype(F32)[:, None]).reshape(1, heads * DV)

    half = inputs.shape[0] // 2
    tail, *near = near_sends(place, w_out, inputs)
    halo = shifted(tail, 1)
    near = [swapped(one, 2 * m) for m, one in enumerate(near, 1)]
    w_other, x_first, *far = rest_sends(place, w_out, w_in, inputs)
    w_other = swapped(w_other, 1)
    halo, place, gain, far = lax.optimization_barrier((halo, place, gain, far))
    v, pq, pk, fq, fk, loc, ct_first, state = project(
        inputs, x_first, cotangent, halo, w_in, conv_w, sel, bias, heads)
    state, w_other = lax.optimization_barrier((state, w_other))
    before = from_others(state, 1)
    v, near, far = lax.optimization_barrier((v, near, far))
    far = [swapped(one, 2 * m) for m, one in enumerate(far, 3)]
    g, num, wt, slope = local_part(cotangent, ct_first, w_out, gain, v, pq, pk, loc, fq, fk, sel, heads)
    ho, dn, gloc, pre, gstate = norm_part(
        g, num, gain, pq, before, (v, pk, fq, fk, wt, slope, loc, sel), heads
    )
    step = pairs // 2
    got = {r: swapped(ho, 2 * r) for r in range(1, pairs) if r != 1 + step}
    later = from_others(gstate, -1)
    pre, far = lax.optimization_barrier((pre, far))
    dqk, dv, xk = inner_part(v, pq, pk, fq, wt, slope, dn, loc, pre, sel, fk, gloc, heads)
    dp_top, dp, first, last = outer_part(v, pk, fk, dqk, dv, xk, gloc, later, sel, conv_w, heads)
    other_top = swapped(dp_top, 1)
    after = shifted(first, -1)
    a_send, a_keep = grad_part(place, dp_top, other_top, w_in, w_other, True)
    dp_low = complete(dp, last, after, conv_w)
    other_low = swapped(dp_low, 1)
    x_top, y_low = halves(got[1], got[step])
    x_top, y_low = swapped(x_top, 2 * step), swapped(y_low, 2)
    b_send, b_keep = grad_part(place, dp_low, other_low, w_in, w_other, False)
    tops = [(ho, 0)] + [(got.get(r, x_top), 0) for r in range(1, pairs)]
    lows = [(ho, half)] + [(got[r], half) if r in got else (y_low, 0) for r in range(1, pairs)]
    w_cols = [w_out] + near + far
    place_, b_keep = lax.optimization_barrier((place, b_keep))
    stage = []

    def meanwhile(a_got, b_got):
        if not stage:
            out_send, out_keep = out_part(place, tops, lows, w_cols)
            own = own_columns(place_, inputs, cotangent, inputs.shape[1] // tp)
            out_got = swapped(out_send, 1)
            a_got, b_got, out_keep = lax.optimization_barrier((a_got, b_got, out_keep))
            stage.extend([*own, out_keep, out_got])
        elif len(stage) == 4:
            stage.append(finish_out(stage[0], *stage[2:]))
            a_got, b_got, stage[4] = lax.optimization_barrier((a_got, b_got, stage[4]))
        return a_got, b_got

    a_terms, b_terms = reduce_both(a_send, a_keep, b_send, b_keep, meanwhile)
    rest = partial_sum(stage[1], a_terms[:-1], b_terms[:-1])
    rest, a_got, b_got = lax.optimization_barrier((rest, a_terms[-1][0], b_terms[-1][0]))
    return stage[4], finish(rest, [(a_got, a_terms[-1][1])], [(b_got, b_terms[-1][1])])


def solution(mesh):
    placed = (
        P("seq", None),
        P("seq", None),
        P(None, "tp"),
        P(None, "tp"),
        P("tp"),
        P("tp", None),
        P("tp"),
    )
    return jax.shard_map(
        per_device,
        mesh=mesh,
        in_specs=placed,
        out_specs=(P("seq", "tp"), P("seq", "tp")),
        check_vma=False,
    )
```

```python
import functools

import jax
import jax.numpy as jnp
import numpy as np
from jax import lax
from jax.experimental import pallas as pl
from jax.experimental.pallas import tpu as pltpu
from jax.sharding import PartitionSpec as P

FEAT = 16
DV = 128
HW = 2 * FEAT + DV
EP = 256
ES = 160
CH = 256
EPS = 1e-06
BF = jnp.bfloat16
F32 = jnp.float32
MIB = 1024 * 1024


def mm(a, b):
    return lax.dot_general(a, b, (((1,), (0,)), ((), ())), preferred_element_type=F32)


def mm_nt(a, b):
    return lax.dot_general(a, b, (((1,), (1,)), ((), ())), preferred_element_type=F32)


def mm_tn(a, b):
    return lax.dot_general(a, b, (((0,), (0,)), ((), ())), preferred_element_type=F32)


def selectors(heads):
    sel = np.zeros((heads, 128, 4 * EP), np.float32)
    bias = np.zeros((8, EP), np.float32)
    bias[1, :FEAT] = 1.0
    bias[0, FEAT] = bias[1, FEAT] = 1.0
    for h in range(heads):
        q0 = (HW * h) % 128
        k0 = q0 + FEAT
        for i in range(FEAT):
            sel[h, q0 + i, i] = 0.5
            sel[h, k0 + i, 2 * EP + i] = 0.5
        col = FEAT + 1
        for i in range(FEAT):
            for j in range(i, FEAT):
                sel[h, q0 + i, col] = 0.25 if i == j else 0.5
                sel[h, q0 + j, EP + col] = 0.5
                sel[h, k0 + i, 2 * EP + col] = 0.5
                sel[h, k0 + j, 3 * EP + col] = 0.5
                col += 1
    return jnp.asarray(sel, BF), jnp.asarray(bias, F32)


def window(h):
    t = (HW * h) // 128
    return slice(128 * t, 128 * t + 128)


def value_place(h):
    start = HW * h + 2 * FEAT
    return start // 128, start % 128


def lane_iota():
    return lax.broadcasted_iota(jnp.int32, (CH, 128), 1)


def take_values(conv, h):
    tile, off = value_place(h)
    first = conv[:, 128 * tile : 128 * tile + 128]
    if off == 0:
        return first
    second = conv[:, 128 * tile + 128 : min(128 * tile + 256, conv.shape[1])]
    if second.shape[1] < 128:
        second = jnp.concatenate([second, jnp.zeros((CH, 128 - second.shape[1]), second.dtype)], 1)
    a = pltpu.roll(first, 128 - off, 1)
    b = pltpu.roll(second, 128 - off, 1)
    return jnp.where(lane_iota() < 128 - off, a, b)


def causal():
    r = lax.broadcasted_iota(jnp.int32, (CH, CH), 0)
    c = lax.broadcasted_iota(jnp.int32, (CH, CH), 1)
    return r >= c


def params(mib):
    return pltpu.CompilerParams(dimension_semantics=("arbitrary",), vmem_limit_bytes=mib * MIB)


def whole(shape):
    return pl.BlockSpec(shape, lambda c, *_: (0,) * len(shape))


KEPT = pl.BlockSpec(memory_space=pltpu.VMEM)


def kept(shape, dtype):
    return pltpu.VMEM(shape, dtype)


def keep(array):
    return pltpu.with_memory_space_constraint(array, pltpu.VMEM)


def stay(array):
    return pltpu.with_memory_space_constraint(array, pltpu.HBM)


def cost(flops):
    return pl.CostEstimate(flops=int(flops), bytes_accessed=1 << 20, transcendentals=0)


LIGHT = cost(1000)


def rows_at(c):
    return pl.ds(pl.multiple_of(c * CH, CH), CH)


def biased(u, bias):
    return jnp.concatenate([u[:, :128] + bias[:, :128], u[:, 128:]], 1)


def with_rows(hbm_ref, first_ref, buf, sems, use):
    c = pl.program_id(0)

    def fetch(k):
        slot = lax.rem(k, 2)
        return pltpu.make_async_copy(hbm_ref.at[rows_at(k), :], buf.at[slot], sems.at[slot])

    @pl.when(c == 0)
    def _():
        fetch(1).start()
        use(first_ref[...])

    @pl.when(c >= 1)
    def _():
        fetch(c).wait()

        @pl.when(c + 1 < pl.num_programs(0))
        def _():
            fetch(c + 1).start()

        use(buf[lax.rem(c, 2)])


def project_kernel(heads, x_ref, x_first_ref, ct_ref, halo_ref, w_ref, cw_ref, sel_ref, bias_ref,
                   v_ref, pq_ref, pk_ref, fq_ref, fk_ref, loc_ref, ct_first_ref, state_ref, ext, run, buf, sems):
    c = pl.program_id(0)
    at = rows_at(c)
    last = pl.num_programs(0) - 1
    ct_copy = pltpu.make_async_copy(ct_ref.at[pl.ds(0, CH), :], ct_first_ref, sems.at[2])

    @pl.when(c == 0)
    def _():
        before = mm(halo_ref[...], w_ref[...]).astype(BF).astype(F32)
        ext[0:8, :] = before[8:16]
        run[...] = jnp.zeros_like(run)

    @pl.when(c == last)
    def _():
        ct_copy.start()

    def product(rows):
        ext[8:, :] = mm(rows, w_ref[...]).astype(BF).astype(F32)

    with_rows(x_ref, x_first_ref, buf, sems, product)
    conv = (cw_ref[0:1] * ext[8 : 8 + CH, :] + cw_ref[1:2] * ext[7 : 7 + CH, :]
            + cw_ref[2:3] * ext[6 : 6 + CH, :])
    ext[0:8, :] = ext[CH : CH + 8, :]
    conv_b = conv.astype(BF)
    conv = conv_b.astype(F32)
    b0 = bias_ref[0:1]
    b1 = bias_ref[1:2]
    for h in range(heads):
        u = mm(conv_b[:, window(h)], sel_ref[h])
        first, second = biased(u[:, :EP], b0), biased(u[:, EP : 2 * EP], b1)
        pq_ref[h, at, :] = (first * second).astype(BF)
        fq_ref[h, at, :EP] = first.astype(BF)
        fq_ref[h, at, EP:] = second.astype(BF)
        first, second = biased(u[:, 2 * EP : 3 * EP], b0), biased(u[:, 3 * EP :], b1)
        pk = (first * second).astype(BF)
        pk_ref[h, at, :] = pk
        fk_ref[h, at, :EP] = first.astype(BF)
        fk_ref[h, at, EP:] = second.astype(BF)
        v = take_values(conv, h).astype(BF)
        v_ref[at, DV * h : DV * h + DV] = v
        loc_ref[c, h] = run[h].astype(BF)
        run[h] = run[h] + mm_tn(v, pk)

    @pl.when(c == last)
    def _():
        for h in range(heads):
            state_ref[h] = run[h].T[:ES].astype(BF)
        ct_copy.wait()


def project(x, x_first, ct, halo, w_in, conv_w, sel, bias, heads):
    rows, d = x.shape
    width = w_in.shape[1]
    n = rows // CH
    return pl.pallas_call(
        functools.partial(project_kernel, heads),
        grid=(n,),
        in_specs=[
            pl.BlockSpec(memory_space=pltpu.HBM),
            KEPT,
            pl.BlockSpec(memory_space=pltpu.HBM),
            whole((16, d)),
            KEPT,
            whole((3, width)),
            KEPT,
            whole(bias.shape),
        ],
        out_specs=[KEPT] * 7 + [whole((heads, ES, DV))],
        out_shape=[
            kept((rows, heads * DV), BF),
            kept((heads, rows, EP), BF),
            kept((heads, rows, EP), BF),
            kept((heads, rows, 2 * EP), BF),
            kept((heads, rows, 2 * EP), BF),
            kept((n, heads, DV, EP), BF),
            kept((CH, d), BF),
            jax.ShapeDtypeStruct((heads, ES, DV), BF),
        ],
        scratch_shapes=[
            pltpu.VMEM((CH + 8, width), F32),
            pltpu.VMEM((heads, DV, EP), F32),
            pltpu.VMEM((2, CH, d), BF),
            pltpu.SemaphoreType.DMA((3,)),
        ],
        compiler_params=params(9),
        cost_estimate=cost(100 << 30),
        name="project",
    )(stay(x), keep(x_first), stay(ct), halo, keep(w_in), conv_w, keep(sel), bias)


def local_kernel(heads, ct_ref, ct_first_ref, wo_ref, gain_ref, v_ref, pq_ref, pk_ref, loc_ref, fq_ref, fk_ref, sel_ref,
                 g_ref, num_ref, wt_ref, slope_ref, buf, sems):
    c = pl.program_id(0)
    at = rows_at(c)

    def product(rows):
        g_ref[at, :] = mm_nt(rows, wo_ref[...]) * gain_ref[...]

    with_rows(ct_ref, ct_first_ref, buf, sems, product)
    mask = causal()
    for h in range(heads):
        pq = pq_ref[h, at, :]
        logits = mm_nt(pq[:, :FEAT], pk_ref[h, at, :FEAT])
        slope = 1.0 + logits
        weights = jnp.where(mask, 0.5 + 0.5 * slope * slope, 0.0).astype(BF)
        wt_ref[h, at, :] = weights
        slope_ref[h, at, :] = jnp.where(mask, slope, 0.0).astype(BF)
        lanes = slice(DV * h, DV * h + DV)
        num_ref[at, lanes] = mm(weights, v_ref[at, lanes]) + mm_nt(pq, loc_ref[c, h])


def local_part(ct, ct_first, w_out, gain, v, pq, pk, loc, fq, fk, sel, heads):
    rows, d = ct.shape
    n = rows // CH
    wide = heads * DV
    return pl.pallas_call(
        functools.partial(local_kernel, heads),
        grid=(n,),
        in_specs=[pl.BlockSpec(memory_space=pltpu.HBM), KEPT, KEPT, whole((1, wide))] + [KEPT] * 7,
        out_specs=[KEPT] * 4,
        out_shape=[kept((rows, wide), F32)] * 2 + [kept((heads, rows, CH), BF)] * 2,
        scratch_shapes=[pltpu.VMEM((2, CH, d), BF), pltpu.SemaphoreType.DMA((2,))],
        compiler_params=params(8),
        cost_estimate=LIGHT,
        name="local_part",
    )(stay(ct), keep(ct_first), keep(w_out), gain, *map(keep, (v, pq, pk, loc, fq, fk, sel)))


def norm_kernel(heads, parts, passed, g_ref, num_ref, gain_ref, pq_ref, ones_ref, *refs):
    got = refs[:parts]
    ho_ref, dn_ref, loc_ref, pre_ref, state_ref, run = refs[parts + passed :]
    step = pl.program_id(0)
    c = pl.num_programs(0) - 1 - step
    at = rows_at(c)

    @pl.when(step == 0)
    def _():
        run[...] = jnp.zeros_like(run)
        total = got[0][...].astype(F32)
        for one in got[1:]:
            total = total + one[...].astype(F32)
        pre_ref[...] = total.astype(BF)

    for h in range(0, heads, 2):
        lanes = slice(DV * h, DV * h + 2 * DV)
        pqs = [pq_ref[h, at, :], pq_ref[h + 1, at, :]]
        num = num_ref[at, lanes] + jnp.concatenate(
            [mm(pqs[0][:, :ES], pre_ref[h]), mm(pqs[1][:, :ES], pre_ref[h + 1])], 1
        )
        inv = lax.rsqrt(mm((num * num).astype(BF), ones_ref[...]) + EPS)
        normed = num * inv
        ho_ref[at, lanes] = (normed * gain_ref[:, lanes]).astype(BF)
        g = g_ref[at, lanes]
        dn = ((g - normed * mm((g * normed).astype(BF), ones_ref[...])) * inv).astype(BF)
        dn_ref[at, lanes] = dn
        for i in range(2):
            loc_ref[c, h + i] = run[h + i].astype(BF)
            run[h + i] = run[h + i] + mm_tn(dn[:, DV * i : DV * i + DV], pqs[i])

    @pl.when(step == pl.num_programs(0) - 1)
    def _():
        for h in range(heads):
            state_ref[h] = run[h].T[:ES].astype(BF)


def norm_part(g, num, gain, pq, got, later, heads):
    ones = jnp.asarray(np.kron(np.eye(2), np.full((DV, DV), 1.0 / DV)), BF)
    rows, wide = g.shape
    n = rows // CH
    return pl.pallas_call(
        functools.partial(norm_kernel, heads, len(got), len(later)),
        grid=(n,),
        in_specs=[KEPT, KEPT, whole((1, wide)), KEPT, whole((2 * DV, 2 * DV))]
        + [whole((heads, ES, DV))] * len(got)
        + [KEPT] * len(later),
        out_specs=[KEPT] * 4 + [whole((heads, ES, DV))],
        out_shape=[
            kept((rows, wide), BF),
            kept((rows, wide), BF),
            kept((n, heads, DV, EP), BF),
            kept((heads, ES, DV), BF),
            jax.ShapeDtypeStruct((heads, ES, DV), BF),
        ],
        scratch_shapes=[pltpu.VMEM((heads, DV, EP), F32)],
        compiler_params=params(5),
        cost_estimate=cost(16 << 30),
        name="norm_part",
    )(keep(g), keep(num), gain, keep(pq), ones, *got, *map(keep, later))


def inner_kernel(heads, v_ref, pq_ref, pk_ref, fq_ref, wt_ref, slope_ref, dn_ref, loc_ref, pre_ref, sel_ref,
                 fk_ref, gloc_ref, dqk_ref, dv_ref, xk_ref, pre_t):
    c = pl.program_id(0)
    at = rows_at(c)

    @pl.when(c == 0)
    def _():
        pre_t[...] = jnp.zeros_like(pre_t)
        for h in range(heads):
            pre_t[h, :, :ES] = pre_ref[h].astype(F32).T

    linear = lane_iota() < FEAT
    dqk = None
    for h in range(heads):
        lanes = slice(DV * h, DV * h + DV)
        dn = dn_ref[at, lanes]
        dv_ref[at, lanes] = mm_tn(wt_ref[h, at, :], dn)
        dl = (mm_nt(dn, v_ref[at, lanes]) * slope_ref[h, at, :].astype(F32)).astype(BF)
        xk_ref[h, at, :] = mm_tn(dl, pq_ref[h, at, :128])
        state = (loc_ref[c, h].astype(F32) + pre_t[h]).astype(BF)
        dphi = mm(dn, state)
        dphi = jnp.concatenate(
            [dphi[:, :128] + jnp.where(linear, mm(dl, pk_ref[h, at, :128]), 0.0), dphi[:, 128:]], 1
        )
        da = (dphi * fq_ref[h, at, EP:].astype(F32)).astype(BF)
        db = (dphi * fq_ref[h, at, :EP].astype(F32)).astype(BF)
        part = mm_nt(da, sel_ref[h, :, :EP]) + mm_nt(db, sel_ref[h, :, EP : 2 * EP])
        dqk = part if dqk is None else dqk + part
    dqk_ref[at, :] = dqk


def inner_part(v, pq, pk, fq, wt, slope, dn, loc, pre, sel, fk, gloc, heads):
    rows = v.shape[0]
    n = rows // CH
    return pl.pallas_call(
        functools.partial(inner_kernel, heads),
        grid=(n,),
        in_specs=[KEPT] * 12,
        out_specs=[KEPT] * 3,
        out_shape=[
            kept((rows, 128), F32),
            kept((rows, heads * DV), F32),
            kept((heads, rows, 128), F32),
        ],
        scratch_shapes=[pltpu.VMEM((heads, DV, EP), F32)],
        compiler_params=params(5),
        cost_estimate=LIGHT,
        name="inner_part",
    )(*map(keep, (v, pq, pk, fq, wt, slope, dn, loc, pre, sel, fk, gloc)))


def outer_kernel(heads, parts, v_ref, pk_ref, fk_ref, dqk_ref, dv_ref, xk_ref, loc_ref, sel_ref, cw_ref, *refs):
    got = refs[:parts]
    top_ref, dp_ref, first_ref, last_ref, ext, suf_t = refs[parts:]
    half_chunks = pl.num_programs(0) // 2
    step = pl.program_id(0)
    c = pl.num_programs(0) - 1 - step
    at = rows_at(c)
    width = cw_ref.shape[1]

    @pl.when(step == 0)
    def _():
        suf_t[...] = jnp.zeros_like(suf_t)
        for h in range(heads):
            total = got[0][h].astype(F32)
            for one in got[1:]:
                total = total + one[h].astype(F32)
            suf_t[h, :, :ES] = total.T
        ext[CH:, :] = jnp.zeros((8, width), F32)

    lane = lane_iota()
    tiles = [None] * (-(-width // 128))

    def put(t, piece):
        tiles[t] = piece if tiles[t] is None else tiles[t] + piece

    dqk = dqk_ref[at, :]
    for h in range(heads):
        lanes = slice(DV * h, DV * h + DV)
        state = (loc_ref[c, h].astype(F32) + suf_t[h]).astype(BF)
        dphi = mm(v_ref[at, lanes], state)
        dphi = jnp.concatenate(
            [dphi[:, :128] + jnp.where(lane < FEAT, xk_ref[h, at, :], 0.0), dphi[:, 128:]], 1
        )
        da = (dphi * fk_ref[h, at, EP:].astype(F32)).astype(BF)
        db = (dphi * fk_ref[h, at, :EP].astype(F32)).astype(BF)
        own = (
            dqk
            + mm_nt(da, sel_ref[h, :, 2 * EP : 3 * EP])
            + mm_nt(db, sel_ref[h, :, 3 * EP : 4 * EP])
        )
        q0 = (HW * h) % 128
        put((HW * h) // 128, jnp.where((lane >= q0) & (lane < q0 + 2 * FEAT), own, 0.0))
        dv = dv_ref[at, lanes] + mm_nt(pk_ref[h, at, :], state)
        tile, off = value_place(h)
        if off == 0:
            put(tile, dv)
        else:
            moved = pltpu.roll(dv, off, 1)
            put(tile, jnp.where(lane >= off, moved, 0.0))
            put(tile + 1, jnp.where(lane < off, moved, 0.0))
    for t, tile in enumerate(tiles):
        end = min(128 * t + 128, width)
        ext[:CH, 128 * t : end] = tile[:, : end - 128 * t]
    dp = (cw_ref[0:1] * ext[:CH, :] + cw_ref[1:2] * ext[1 : CH + 1, :]
          + cw_ref[2:3] * ext[2 : CH + 2, :])
    dp_ref[at, :] = dp.astype(BF)

    @pl.when(c < half_chunks)
    def _():
        top_ref[at, :] = dp.astype(BF)

    @pl.when(step == 0)
    def _():
        last_ref[...] = dp[CH - 16 :]

    ext[CH:, :] = ext[0:8, :]
    first_ref[...] = ext[0:8, :]


def outer_part(v, pk, fk, dqk, dv, xk, loc, got, sel, conv_w, heads):
    rows, width = v.shape[0], conv_w.shape[1]
    n = rows // CH
    return pl.pallas_call(
        functools.partial(outer_kernel, heads, len(got)),
        grid=(n,),
        in_specs=[KEPT] * 8 + [whole((3, width))] + [whole((heads, ES, DV))] * len(got),
        out_specs=[KEPT, KEPT, whole((8, width)), KEPT],
        out_shape=[
            kept((rows // 2, width), BF),
            kept((rows, width), BF),
            jax.ShapeDtypeStruct((8, width), F32),
            kept((16, width), F32),
        ],
        scratch_shapes=[pltpu.VMEM((CH + 8, width), F32), pltpu.VMEM((heads, DV, EP), F32)],
        compiler_params=params(5),
        cost_estimate=cost(16 << 30),
        name="outer_part",
    )(*map(keep, (v, pk, fk, dqk, dv, xk, loc, sel)), conv_w, *got)


def run_copies(copies, sems):
    copies = [pltpu.make_async_copy(*one, sems.at[i]) for i, one in enumerate(copies)]
    for copy in copies:
        copy.start()
    for copy in copies:
        copy.wait()


def column_copies(which, place_ref, w_ref, outs):
    wide = outs[0].shape[1]
    for m, out in zip(which, outs):
        start = pl.multiple_of(lax.bitwise_xor(place_ref[0], m) * wide, wide)
        yield w_ref.at[:, pl.ds(start, wide)], out


def near_kernel(which, place_ref, w_ref, x_ref, tail_ref, *refs):
    rows = tail_ref.shape[0]
    copies = list(column_copies(which, place_ref, w_ref, refs[:-1]))
    copies.append((x_ref.at[pl.ds(x_ref.shape[0] - rows, rows), :], tail_ref))
    run_copies(copies, refs[-1])


def rest_kernel(which, place_ref, w_ref, wi_ref, x_ref, blocks_ref, first_ref, *refs):
    copies = list(column_copies(which, place_ref, w_ref, refs[:-1]))
    count, sw = blocks_ref.shape[:2]
    for r in range(count):
        block = 2 * lax.bitwise_xor(place_ref[0], r) + 1 - place_ref[1]
        copies.append((wi_ref.at[pl.ds(pl.multiple_of(block * sw, sw), sw), :], blocks_ref.at[r]))
    copies.append((x_ref.at[pl.ds(0, CH), :], first_ref))
    run_copies(copies, refs[-1])


def copied(kernel, which, place, arrays, extra, specs, copies, name):
    rows, d = arrays[0].shape
    anywhere = pl.BlockSpec(memory_space=pltpu.HBM)
    pairs = lax.axis_size("tp") // 2
    return pl.pallas_call(
        functools.partial(kernel, which),
        grid_spec=pltpu.PrefetchScalarGridSpec(
            num_scalar_prefetch=1,
            grid=(1,),
            in_specs=[anywhere] * len(arrays),
            out_specs=specs + [anywhere] * len(which),
            scratch_shapes=[pltpu.SemaphoreType.DMA((copies,))],
        ),
        out_shape=extra + [jax.ShapeDtypeStruct((rows, d // pairs), arrays[0].dtype)] * len(which),
        compiler_params=pltpu.CompilerParams(vmem_limit_bytes=4 * MIB),
        cost_estimate=LIGHT,
        name=name,
    )(place, *map(stay, arrays))


def near_sends(place, w_out, x):
    tail = jax.ShapeDtypeStruct((16, x.shape[1]), x.dtype)
    spec = pl.BlockSpec(memory_space=pltpu.HBM)
    return copied(near_kernel, (1, 2), place, (w_out, x), [tail], [spec], 3, "near_sends")


def rest_sends(place, w_out, w_in, x):
    pairs = lax.axis_size("tp") // 2
    which = tuple(range(3, pairs))
    blocks = jax.ShapeDtypeStruct((pairs, w_in.shape[0] // (2 * pairs), w_in.shape[1]), w_in.dtype)
    specs = [pl.BlockSpec(memory_space=pltpu.HBM), KEPT]
    extra = [blocks, kept((CH, x.shape[1]), x.dtype)]
    return copied(
        rest_kernel, which, place, (w_out, w_in, x), extra, specs, len(which) + pairs + 1, "rest_sends"
    )


def shifted(array, by):
    count = lax.axis_size("seq")
    pairs = [(i, i + by) for i in range(count) if 0 <= i + by < count]
    return lax.ppermute(array, "seq", pairs)


def from_others(part, sign):
    return [shifted(part, sign * step) for step in reversed(range(1, lax.axis_size("seq")))]


def out_kernel(count, sw, place_ref, *refs):
    tops, lows, ws = refs[:count], refs[count : 2 * count], refs[2 * count : 3 * count]
    send_ref, keep_ref = refs[3 * count :]
    c = pl.program_id(0)
    half_chunks = pl.num_programs(0) // 2
    odd = place_ref[1] == 1

    def product(parts):
        total = None
        for part, w in zip(parts, ws):
            one = mm(part[...], w[...])
            total = one if total is None else total + one
        first, second = total[:, :sw], total[:, sw:]
        send_ref[rows_at(c), :] = jnp.where(odd, first, second).astype(BF)
        keep_ref[rows_at(c), :] = jnp.where(odd, second, first)

    @pl.when(c < half_chunks)
    def _():
        product(tops)

    @pl.when(c >= half_chunks)
    def _():
        product(lows)


def out_part(place, tops, lows, ws):
    count = len(ws)
    rows = 2 * CH * (lows[0][1] // CH)
    wide = tops[0][0].shape[1]
    sw = ws[1].shape[1] // 2
    part = rows // (2 * CH)
    operands, specs = [], []
    for array, start in tops:
        operands.append(array)
        specs.append(
            pl.BlockSpec((CH, wide), lambda c, place, s=start // CH: (s + jnp.minimum(c, part - 1), 0))
        )
    for array, start in lows:
        operands.append(array)
        specs.append(
            pl.BlockSpec((CH, wide), lambda c, place, s=start // CH: (s + jnp.maximum(c - part, 0), 0))
        )
    return pl.pallas_call(
        functools.partial(out_kernel, count, sw),
        grid_spec=pltpu.PrefetchScalarGridSpec(
            num_scalar_prefetch=1,
            grid=(rows // CH,),
            in_specs=specs
            + [pl.BlockSpec((wide, 2 * sw), lambda c, place: (0, place[0]))]
            + [pl.BlockSpec((wide, 2 * sw), lambda c, place: (0, 0))] * (count - 1),
            out_specs=[KEPT, KEPT],
        ),
        out_shape=[kept((rows, sw), BF), kept((rows, sw), F32)],
        compiler_params=params(16),
        cost_estimate=cost(16 << 30),
        name="out_part",
    )(place, *operands, *map(stay, ws))


def complete_kernel(dp_ref, last_ref, after_ref, cw_ref, low_ref):
    half = low_ref.shape[0]
    low_ref[...] = dp_ref[half:, :]
    row = lax.broadcasted_iota(jnp.int32, last_ref.shape, 0)
    a0, a1 = after_ref[0:1], after_ref[1:2]
    one = cw_ref[2:3] * a0
    two = cw_ref[1:2] * a0 + cw_ref[2:3] * a1
    tail = last_ref[...] + jnp.where(row == 14, one, 0.0) + jnp.where(row == 15, two, 0.0)
    low_ref[half - 16 :, :] = tail.astype(BF)


def complete(dp, last, after, conv_w):
    rows, width = dp.shape
    return pl.pallas_call(
        complete_kernel,
        in_specs=[KEPT] * 4,
        out_specs=KEPT,
        out_shape=kept((rows // 2, width), BF),
        compiler_params=pltpu.CompilerParams(vmem_limit_bytes=4 * MIB),
        cost_estimate=LIGHT,
        name="complete",
    )(keep(dp), keep(last), after, conv_w)


def grad_kernel(count, low_first, place_ref, dp_ref, other_ref, w_ref, w_other_ref, send_ref, keep_ref, both):
    r = pl.program_id(0)
    half, sw = send_ref.shape[1:]
    width = w_ref.shape[1]

    @pl.when(r == 0)
    def _():
        both[:, :width] = dp_ref[...]
        both[:, width:] = other_ref[...]

    block = 2 * lax.bitwise_xor(place_ref[0], r) + place_ref[1]
    w = w_ref[pl.ds(pl.multiple_of(block * sw, sw), sw), :]
    total = mm_nt(both[...], jnp.concatenate([w, w_other_ref[r]], 1)).astype(BF)
    part = count // 2
    leaves = (r % 2 == 1) if low_first else (r >= part)

    @pl.when(leaves)
    def _():
        send_ref[r // 2 if low_first else r - part] = total

    @pl.when(jnp.logical_not(leaves))
    def _():
        keep_ref[r // 2 if low_first else r] = total


def grad_part(place, dp, other, w_in, w_other, low_first):
    half, width = dp.shape
    count, sw = w_other.shape[:2]
    return pl.pallas_call(
        functools.partial(grad_kernel, count, low_first),
        grid_spec=pltpu.PrefetchScalarGridSpec(
            num_scalar_prefetch=1,
            grid=(count,),
            in_specs=[KEPT] * 4,
            out_specs=[KEPT] * 2,
            scratch_shapes=[pltpu.VMEM((half, 2 * width), BF)],
        ),
        out_shape=[kept((count // 2, half, sw), BF)] * 2,
        compiler_params=params(5),
        cost_estimate=LIGHT,
        name="grad_part",
    )(place, *map(keep, (dp, other, w_in, w_other)))


def halves_kernel(x_ref, y_ref, x_top_ref, y_low_ref):
    half = x_top_ref.shape[0]
    x_top_ref[...] = x_ref[:half, :]
    y_low_ref[...] = y_ref[half:, :]


def halves(x_got, y_got):
    rows, wide = x_got.shape
    return pl.pallas_call(
        halves_kernel,
        in_specs=[KEPT] * 2,
        out_specs=[KEPT] * 2,
        out_shape=[kept((rows // 2, wide), BF)] * 2,
        compiler_params=pltpu.CompilerParams(vmem_limit_bytes=4 * MIB),
        cost_estimate=LIGHT,
        name="halves",
    )(keep(x_got), keep(y_got))


def swapped(array, distance):
    count = lax.axis_size("tp")
    return lax.ppermute(array, "tp", [(i, i ^ distance) for i in range(count)])


def summed(a, b):
    return a.astype(F32) + b.astype(F32)


def passing_kernel(places, *refs):
    ins, out_ref = refs[:-1], refs[-1]
    for i in range(out_ref.shape[0]):
        total = None
        for ref, place in zip(ins, places):
            one = ref[place[i]].astype(F32)
            total = one if total is None else total + one
        out_ref[i] = total.astype(BF)


def passing(terms, blocks):
    places = [[place[i] for i in blocks] for _, place in terms]
    return pl.pallas_call(
        functools.partial(passing_kernel, places),
        in_specs=[KEPT] * len(terms),
        out_specs=KEPT,
        out_shape=kept((len(blocks),) + terms[0][0].shape[1:], BF),
        compiler_params=pltpu.CompilerParams(vmem_limit_bytes=4 * MIB),
        cost_estimate=LIGHT,
        name="passing",
    )(*[keep(array) for array, _ in terms])


def reduce_both(a_send, a_keep, b_send, b_keep, meanwhile):
    pairs = lax.axis_size("tp") // 2
    a_step, b_step = 1, pairs // 2
    left = pairs // 2
    a_terms, b_terms = [(a_keep, list(range(left)))], [(b_keep, list(range(left)))]
    while True:
        a_got, b_got = swapped(a_send, 2 * a_step), swapped(b_send, 2 * b_step)
        a_got, b_got = meanwhile(a_got, b_got)
        a_terms.append((a_got, list(range(left))))
        b_terms.append((b_got, list(range(left))))
        if left == 1:
            return a_terms, b_terms
        half = left // 2
        a_send = passing(a_terms, list(range(1, left, 2)))
        b_send = passing(b_terms, list(range(half, left)))
        a_terms = [(array, place[0::2]) for array, place in a_terms]
        b_terms = [(array, place[:half]) for array, place in b_terms]
        left = half
        a_step, b_step = a_step * 2, b_step // 2


def own_kernel(place_ref, x_ref, ct_ref, x_own_ref, ct_own_ref, sems):
    sw = x_own_ref.shape[1]
    at = pl.ds(pl.multiple_of(place_ref[2] * sw, sw), sw)
    copies = [
        pltpu.make_async_copy(x_ref.at[:, at], x_own_ref, sems.at[0]),
        pltpu.make_async_copy(ct_ref.at[:, at], ct_own_ref, sems.at[1]),
    ]
    for copy in copies:
        copy.start()
    for copy in copies:
        copy.wait()


def own_columns(place, x, ct, sw):
    rows = x.shape[0]
    anywhere = pl.BlockSpec(memory_space=pltpu.HBM)
    return pl.pallas_call(
        own_kernel,
        grid_spec=pltpu.PrefetchScalarGridSpec(
            num_scalar_prefetch=1,
            grid=(1,),
            in_specs=[anywhere] * 2,
            out_specs=[KEPT] * 2,
            scratch_shapes=[pltpu.SemaphoreType.DMA((2,))],
        ),
        out_shape=[kept((rows, sw), x.dtype)] * 2,
        compiler_params=pltpu.CompilerParams(vmem_limit_bytes=4 * MIB),
        cost_estimate=LIGHT,
        name="own_columns",
    )(place, stay(x), stay(ct))


def finish_kernel(places, own_ref, *refs):
    tops, lows, out_ref = refs[: len(places)], refs[len(places) : -1], refs[-1]
    half = out_ref.shape[0] // 2
    for first, ins in ((0, tops), (half, lows)):
        total = own_ref[first : first + half, :].astype(F32)
        for ref, place in zip(ins, places):
            total = total + ref[place].astype(F32)
        out_ref[first : first + half, :] = total.astype(BF)


def partial_kernel(places, own_ref, *refs):
    tops, lows, out_ref = refs[: len(places)], refs[len(places) : -1], refs[-1]
    half = out_ref.shape[0] // 2
    for first, ins in ((0, tops), (half, lows)):
        total = own_ref[first : first + half, :].astype(F32)
        for ref, place in zip(ins, places):
            total = total + ref[place].astype(F32)
        out_ref[first : first + half, :] = total


def partial_sum(own, a_terms, b_terms):
    places = [index[0] for _, index in a_terms]
    terms = [array for array, _ in a_terms + b_terms]
    return pl.pallas_call(
        functools.partial(partial_kernel, places),
        in_specs=[KEPT] * (1 + len(terms)),
        out_specs=KEPT,
        out_shape=kept(own.shape, F32),
        compiler_params=pltpu.CompilerParams(vmem_limit_bytes=6 * MIB),
        cost_estimate=LIGHT,
        name="partial_sum",
    )(*map(keep, [own] + terms))


def finish(own, a_terms, b_terms):
    places = [index[0] for _, index in a_terms]
    assert places == [index[0] for _, index in b_terms]
    terms = [array for array, _ in a_terms + b_terms]
    return pl.pallas_call(
        functools.partial(finish_kernel, places),
        in_specs=[KEPT] * (1 + len(terms)),
        out_shape=jax.ShapeDtypeStruct(own.shape, BF),
        compiler_params=pltpu.CompilerParams(vmem_limit_bytes=6 * MIB),
        cost_estimate=LIGHT,
        name="finish",
    )(*map(keep, [own] + terms))


def finish_out_kernel(own_ref, keep_ref, got_ref, out_ref):
    out_ref[...] = (own_ref[...].astype(F32) + keep_ref[...] + got_ref[...].astype(F32)).astype(BF)


def finish_out(own, kept_part, got):
    return pl.pallas_call(
        finish_out_kernel,
        in_specs=[KEPT] * 3,
        out_shape=jax.ShapeDtypeStruct(own.shape, BF),
        compiler_params=pltpu.CompilerParams(vmem_limit_bytes=6 * MIB),
        cost_estimate=LIGHT,
        name="finish_out",
    )(*map(keep, (own, kept_part, got)))


def per_device(inputs, cotangent, w_in, conv_w, norm_gain, w_out, keep_flags):
    heads = keep_flags.shape[0]
    sel, bias = selectors(heads)
    tp = lax.axis_size("tp")
    pairs = tp // 2
    me = lax.axis_index("tp")
    pair = me // 2
    place = jnp.stack([pair, me % 2, me]).astype(jnp.int32)
    gain = (norm_gain.reshape(heads, DV) * keep_flags.astype(F32)[:, None]).reshape(1, heads * DV)

    half = inputs.shape[0] // 2
    tail, *near = near_sends(place, w_out, inputs)
    halo = shifted(tail, 1)
    near = [swapped(one, 2 * m) for m, one in enumerate(near, 1)]
    w_other, x_first, *far = rest_sends(place, w_out, w_in, inputs)
    w_other = swapped(w_other, 1)
    halo, place, gain, far = lax.optimization_barrier((halo, place, gain, far))
    v, pq, pk, fq, fk, loc, ct_first, state = project(
        inputs, x_first, cotangent, halo, w_in, conv_w, sel, bias, heads)
    state, w_other = lax.optimization_barrier((state, w_other))
    before = from_others(state, 1)
    v, near, far = lax.optimization_barrier((v, near, far))
    far = [swapped(one, 2 * m) for m, one in enumerate(far, 3)]
    g, num, wt, slope = local_part(cotangent, ct_first, w_out, gain, v, pq, pk, loc, fq, fk, sel, heads)
    ho, dn, gloc, pre, gstate = norm_part(
        g, num, gain, pq, before, (v, pk, fq, fk, wt, slope, loc, sel), heads
    )
    step = pairs // 2
    got = {r: swapped(ho, 2 * r) for r in range(1, pairs) if r != 1 + step}
    later = from_others(gstate, -1)
    pre, far = lax.optimization_barrier((pre, far))
    dqk, dv, xk = inner_part(v, pq, pk, fq, wt, slope, dn, loc, pre, sel, fk, gloc, heads)
    dp_top, dp, first, last = outer_part(v, pk, fk, dqk, dv, xk, gloc, later, sel, conv_w, heads)
    other_top = swapped(dp_top, 1)
    after = shifted(first, -1)
    a_send, a_keep = grad_part(place, dp_top, other_top, w_in, w_other, True)
    dp_low = complete(dp, last, after, conv_w)
    other_low = swapped(dp_low, 1)
    x_top, y_low = halves(got[1], got[step])
    x_top, y_low = swapped(x_top, 2 * step), swapped(y_low, 2)
    b_send, b_keep = grad_part(place, dp_low, other_low, w_in, w_other, False)
    tops = [(ho, 0)] + [(got.get(r, x_top), 0) for r in range(1, pairs)]
    lows = [(ho, half)] + [(got[r], half) if r in got else (y_low, 0) for r in range(1, pairs)]
    w_cols = [w_out] + near + far
    place_, b_keep = lax.optimization_barrier((place, b_keep))
    stage = []

    def meanwhile(a_got, b_got):
        if not stage:
            out_send, out_keep = out_part(place, tops, lows, w_cols)
            own = own_columns(place_, inputs, cotangent, inputs.shape[1] // tp)
            out_got = swapped(out_send, 1)
            a_got, b_got, out_keep = lax.optimization_barrier((a_got, b_got, out_keep))
            stage.extend([*own, out_keep, out_got])
        elif len(stage) == 4:
            stage.append(finish_out(stage[0], *stage[2:]))
            a_got, b_got, stage[4] = lax.optimization_barrier((a_got, b_got, stage[4]))
        return a_got, b_got

    a_terms, b_terms = reduce_both(a_send, a_keep, b_send, b_keep, meanwhile)
    rest = partial_sum(stage[1], a_terms[:-1], b_terms[:-1])
    rest, a_got, b_got = lax.optimization_barrier((rest, a_terms[-1][0], b_terms[-1][0]))
    return stage[4], finish(rest, [(a_got, a_terms[-1][1])], [(b_got, b_terms[-1][1])])


def solution(mesh):
    placed = (
        P("seq", None),
        P("seq", None),
        P(None, "tp"),
        P(None, "tp"),
        P("tp"),
        P("tp", None),
        P("tp"),
    )
    return jax.shard_map(
        per_device,
        mesh=mesh,
        in_specs=placed,
        out_specs=(P("seq", "tp"), P("seq", "tp")),
        check_vma=False,
    )
```
